32 devices in a mesh: narrow: 2 (over y), wide: 16 (over z, x, core).
Axes of the slice: x: 2, y: 2, z: 4, core: 2. Of those that a mesh axis runs over, the one named last changes fastest.
Arguments:
- hidden: bfloat16 [2, 48, 208, 1152], P('narrow', 'wide'), may hold values from -6 to 6
- cotangent: bfloat16 [2, 48, 208, 1152], P('narrow', 'wide'), may hold values from -6 to 6
- text: bfloat16 [2, 128, 4096], P('narrow'), may hold values from -6 to 6
- timesteps: int32 [2], P('narrow'), may hold values from 0 to 999
- seg_ids: int32 [2, 48], P('narrow'), may hold values from 0 to 5, never falling along the last dimension, each value on 1 to 16 neighbouring positions
- text_len: int32 [2], P('narrow'), may hold values from 32 to 128, as said below
- ada_weight: bfloat16 [1152, 10368], P('wide'), may hold values from -0.1875 to 0.1875
- text_weight: bfloat16 [4096, 1152], P('wide'), may hold values from -0.09375 to 0.09375
- kv_weight: bfloat16 [1152, 2304], P('wide'), may hold values from -0.1875 to 0.1875
- qkv_weight: bfloat16 [1152, 3456], P('wide'), may hold values from -0.1875 to 0.1875
- out_weight: bfloat16 [1152, 1152], P('wide'), may hold values from -1.5 to 1.5
- cross_q_weight: bfloat16 [1152, 1152], P('wide'), may hold values from -0.1875 to 0.1875
- cross_out_weight: bfloat16 [1152, 1152], P('wide'), may hold values from -1 to 1
- temp_qkv_weight: bfloat16 [1152, 3456], P('wide'), may hold values from -0.1875 to 0.1875
- temp_out_weight: bfloat16 [1152, 1152], P('wide'), may hold values from -0.25 to 0.25
- up_weight: bfloat16 [1152, 4608], P('wide'), may hold values from -0.1875 to 0.1875
- down_weight: bfloat16 [4608, 1152], P('wide'), may hold values from -0.09375 to 0.09375
- cross_gain: float32 [1152], replicated, may hold values from 0.25 to 1.75
Outputs:
- block_out: bfloat16 [2, 48, 208, 1152], P('narrow', 'wide')
- grad_hidden: bfloat16 [2, 48, 208, 1152], P('narrow', 'wide')
- grad_ada: float32 [1152, 10368], P('wide')
- grad_text: float32 [4096, 1152], P('wide')
- grad_kv: float32 [1152, 2304], P('wide')
- grad_qkv: float32 [1152, 3456], P('wide')
- grad_out: float32 [1152, 1152], P('wide')
- grad_cross_q: float32 [1152, 1152], P('wide')
- grad_cross_out: float32 [1152, 1152], P('wide')
- grad_temp_qkv: float32 [1152, 3456], P('wide')
- grad_temp_out: float32 [1152, 1152], P('wide')
- grad_up: float32 [1152, 4608], P('wide')
- grad_down: float32 [4608, 1152], P('wide')
- grad_gain: float32 [1152], replicated
The draws below stay inside these ranges and needn't reach their ends.
Inputs may be any that keep to these rules, and one draw needn't show every extreme that they name: `seg_ids`: clip numbers never fall along the frames of a bucket; a clip spans 1 to 16 frames, and some clip spans exactly 16. `text_len`: in every draw some bucket uses all 128 text tokens.
All inputs are finite; a program needn't handle non-finite values.
Results may differ from the reference program's by a relative error of at most 0.024.
Values may be sent and summed in bfloat16 or wider, within the bound.
A program may use at most 384 MiB of HBM per device.

```python
import math
import jax
import jax.numpy as jnp
import numpy as np
from jax import lax

D = 1152
HEADS = 16
HEAD_DIM = 72
FF = 4608
TD = 4096
P_SIZE = 208
TEXT_LEN = 128
CLIP_MOST = 16
BUCKETS = 2
FRAMES = 48
CLIPS = 6


def draw_text_len(key, part):
    key = jax.random.fold_in(key, 11)
    lengths = jax.random.randint(key, (BUCKETS,), TEXT_LEN // 4, TEXT_LEN)
    chosen = jax.random.randint(jax.random.fold_in(key, 7), (), 0, BUCKETS)
    return jnp.where(jnp.arange(BUCKETS) == chosen, TEXT_LEN, lengths).astype(jnp.int32)


def level_of(key, shape, pieces, smallest, top_value):
    loudness, own = 1.0, jax.random.fold_in(key, 6)
    for position, blocks in pieces:
        heights = jnp.exp(jax.random.uniform(jax.random.fold_in(own, position), (blocks,), jnp.float32, smallest / len(pieces), top_value / len(pieces)))
        loudness = loudness * jnp.repeat(heights, shape[position] // blocks).reshape([-1 if axis == position else 1 for axis in range(len(shape))])
    return loudness


def profile(count, total, most, lean):
    portions = [(1 << 20) // math.isqrt(standing ** lean) + 1 for standing in range(2, count + 1)]
    spare, given = total - most - (count - 1), [1] * (count - 1)
    while spare > 0:
        candidates = [i for i in range(count - 1) if given[i] < most]
        mass, remaining = sum([portions[i] for i in candidates]), spare
        for i in candidates:
            addition = min(most - given[i], max(1, remaining * portions[i] // mass), spare)
            given[i] = given[i] + addition
            spare = spare - addition
    return np.array([most] + given)


def uneven(key, count, total, bound, slope):
    if count == 2:
        one = jax.random.randint(key, (), max(1, total - bound), min(bound, total - 1) + 1)
        return jnp.stack([one, total - one])
    sizes = jnp.asarray(profile(count, total, bound, slope), jnp.int32)
    twos = (count - 1) // 2
    source_of, sink = sizes[1:1 + 2 * twos:2], sizes[2:2 + 2 * twos:2]
    slack = jnp.minimum(source_of - 1, bound - sink)
    moved = jax.random.randint(jax.random.fold_in(key, 1), (twos,), 0, 1 << 20) % (slack + 1)
    sizes = sizes.at[1:1 + 2 * twos:2].set(source_of - moved).at[2:2 + 2 * twos:2].set(sink + moved)
    return sizes[jax.random.permutation(jax.random.fold_in(key, 2), count)]


def normal_values(own_key, dims, scale, limit, split=(), kind=jnp.bfloat16):
    array = jax.random.normal(own_key, dims, jnp.float32) * scale
    if len(split) > 0:
        array = level_of(own_key, dims, split, -0.22, 0.18) * array
    return jnp.clip(array, min=-limit, max=limit).astype(kind)


def setup_inputs(seed: int = 0) -> dict:
    seeds = jax.random.split(jax.random.key(seed), 19)
    return {
        "hidden": normal_values(seeds[0], (BUCKETS, FRAMES, P_SIZE, D), 1.0, 6.0, ((0, 2), (1, 16))),
        "cotangent": normal_values(seeds[1], (BUCKETS, FRAMES, P_SIZE, D), 1.0, 6.0, ((0, 2), (1, 16))),
        "text": normal_values(seeds[2], (BUCKETS, TEXT_LEN, TD), 1.0, 6.0, ((0, 2),)),
        "timesteps": jax.random.randint(seeds[3], (BUCKETS,), 0, 1000).astype(jnp.int32),
        "seg_ids": jax.vmap(lambda own: jnp.searchsorted(jnp.cumsum(uneven(own, CLIPS, FRAMES, CLIP_MOST, 1)), jnp.arange(FRAMES), side="right"))(jax.random.split(seeds[4], BUCKETS)).reshape((BUCKETS, FRAMES)).astype(jnp.int32),
        "text_len": draw_text_len(jax.random.fold_in(seeds[18], 71), 0),
        "ada_weight": normal_values(seeds[6], (D, 9 * D), D ** -0.5, 0.1875, ((0, 16),)),
        "text_weight": normal_values(seeds[7], (TD, D), TD ** -0.5, 0.09375, ((0, 16),)),
        "kv_weight": normal_values(seeds[8], (D, 2 * D), D ** -0.5, 0.1875, ((0, 16),)),
        "qkv_weight": normal_values(seeds[9], (D, 3 * D), D ** -0.5, 0.1875, ((0, 16),)),
        "out_weight": normal_values(seeds[10], (D, D), (D // 64) ** -0.5, 1.5, ((0, 16),)),
        "cross_q_weight": normal_values(seeds[11], (D, D), D ** -0.5, 0.1875, ((0, 16),)),
        "cross_out_weight": normal_values(seeds[12], (D, D), (D // 32) ** -0.5, 1.0, ((0, 16),)),
        "temp_qkv_weight": normal_values(seeds[13], (D, 3 * D), D ** -0.5, 0.1875, ((0, 16),)),
        "temp_out_weight": normal_values(seeds[14], (D, D), (D // 2) ** -0.5, 0.25, ((0, 16),)),
        "up_weight": normal_values(seeds[15], (D, FF), D ** -0.5, 0.1875, ((0, 16),)),
        "down_weight": normal_values(seeds[16], (FF, D), FF ** -0.5, 0.09375, ((0, 16),)),
        "cross_gain": jnp.clip(1.0 + 0.15 * jax.random.normal(seeds[17], (D,), jnp.float32), 0.25, 1.75),
    }


@jax.custom_vjp
def low(v):
    return lax.optimization_barrier(v.astype(jnp.bfloat16)).astype(jnp.float32)

@jax.custom_vjp
def low_back(v):
    return v

def low_keep(v):
    return (low(v), None)

def low_pass(kept, grad):
    return (grad,)

def back_keep(v):
    return (v, None)

def back_low(kept, grad):
    return (low(grad),)
low.defvjp(low_keep, low_pass)
low_back.defvjp(back_keep, back_low)

def rounded(values):
    return low_back(low(values))

def dense_hi(operand, weights):
    return jnp.dot(operand, weights, precision=lax.Precision.HIGHEST)

def layer_norm(values):
    centred = values - lax.optimization_barrier(jnp.mean(values, -1, keepdims=True))
    variance = lax.optimization_barrier(jnp.mean(centred * centred, -1, keepdims=True))
    return centred * lax.rsqrt(variance + 1e-06)

def modulate(values, shift_vec, scale_vec):
    return layer_norm(values) * (1.0 + scale_vec) + shift_vec

def time_embed(steps, model_width):
    half_width = model_width // 2
    freqs = jnp.exp(-math.log(10000.0) * jnp.arange(half_width, dtype=jnp.float32) / half_width)
    angles = steps.astype(jnp.float32) * freqs
    return jnp.concatenate([jnp.cos(angles), jnp.sin(angles)], -1)

def spatial_frame(triple):
    query, keys, values = triple
    score_scale = HEAD_DIM ** (-0.5)
    scores = low_back(jnp.einsum('phd,qhd->hpq', query, keys, precision=lax.Precision.HIGHEST) * score_scale)
    probs = jax.nn.softmax(scores, -1)
    return jnp.einsum('hpq,qhd->phd', low(probs), values, precision=lax.Precision.HIGHEST)

def cross_frame(query, keys, values, valid):
    score_scale = HEAD_DIM ** (-0.5)
    scores = low_back(jnp.einsum('phd,lhd->hpl', query, keys, precision=lax.Precision.HIGHEST) * score_scale)
    scores = jnp.where(valid, scores, -1e+30)
    probs = jax.nn.softmax(scores, -1)
    return jnp.einsum('hpl,lhd->phd', low(probs), values, precision=lax.Precision.HIGHEST)

def bucket_forward(tokens_in, prompt_in, step, clip_ids, length, ada_w, text_w, kv_w, qkv_w, out_w, cross_q_w, cross_out_w, temp_qkv_w, temp_out_w, up_w, down_w, gain):
    score_scale = HEAD_DIM ** (-0.5)
    row_count = FRAMES * P_SIZE
    signal = low(jax.nn.silu(time_embed(step, D)))
    modulation = dense_hi(signal[None, :], ada_w)[0].reshape(9, D)
    prompt = rounded(dense_hi(prompt_in, text_w))
    text_kv = rounded(dense_hi(prompt, kv_w))
    keys_c = text_kv[:, :D].reshape(TEXT_LEN, HEADS, HEAD_DIM)
    values_c = text_kv[:, D:].reshape(TEXT_LEN, HEADS, HEAD_DIM)
    valid = jnp.arange(TEXT_LEN) < length
    start = tokens_in.reshape(row_count, D)
    normed_a = low(modulate(start, modulation[0], modulation[1]))
    qkv_a = rounded(dense_hi(normed_a, qkv_w)).reshape(FRAMES, P_SIZE, 3, HEADS, HEAD_DIM)
    attn_a = lax.map(jax.checkpoint(spatial_frame), (qkv_a[:, :, 0], qkv_a[:, :, 1], qkv_a[:, :, 2]))
    attn_a = rounded(attn_a.reshape(row_count, D))
    first = start + modulation[2] * low_back(dense_hi(attn_a, out_w))
    normed_c = low(layer_norm(first) * gain)
    query_c = rounded(dense_hi(normed_c, cross_q_w)).reshape(FRAMES, P_SIZE, HEADS, HEAD_DIM)
    attn_c = lax.map(jax.checkpoint(lambda query: cross_frame(query, keys_c, values_c, valid)), query_c)
    attn_c = rounded(attn_c.reshape(row_count, D))
    second = first + low_back(dense_hi(attn_c, cross_out_w))
    normed_t = low(modulate(second, modulation[3], modulation[4]))
    qkv_t = rounded(dense_hi(normed_t, temp_qkv_w)).reshape(FRAMES, P_SIZE, 3, HEADS, HEAD_DIM)
    query_t = qkv_t[:, :, 0]
    pad_spec = ((2, 2), (0, 0), (0, 0), (0, 0))
    keys_pad = jnp.pad(qkv_t[:, :, 1], pad_spec)
    values_pad = jnp.pad(qkv_t[:, :, 2], pad_spec)
    clip_pad = jnp.pad(clip_ids, 2, constant_values=-1)
    score_list = []
    allow_list = []
    for offset in range(5):
        score_list.append(lax.optimization_barrier(jnp.sum(query_t * keys_pad[offset:offset + FRAMES], -1)) * score_scale)
        allow_list.append(clip_pad[offset:offset + FRAMES] == clip_ids)
    scores_t = jnp.stack(score_list, -1)
    allowed = jnp.stack(allow_list, -1)
    scores_t = jnp.where(allowed[:, None, None, :], scores_t, -1e+30)
    probs_t = low(jax.nn.softmax(scores_t, -1))
    attn_t = jnp.zeros((FRAMES, P_SIZE, HEADS, HEAD_DIM), jnp.float32)
    for offset in range(5):
        attn_t = attn_t + probs_t[..., offset, None] * values_pad[offset:offset + FRAMES]
    attn_t = rounded(attn_t.reshape(row_count, D))
    third = second + modulation[5] * low_back(dense_hi(attn_t, temp_out_w))
    normed_m = low(modulate(third, modulation[6], modulation[7]))
    hidden_m = low_back(dense_hi(normed_m, up_w))
    act = low(jax.nn.gelu(hidden_m, approximate=True))
    result = third + modulation[8] * low_back(dense_hi(act, down_w))
    return result.reshape(FRAMES, P_SIZE, D)

def reference(hidden, cotangent, text, timesteps, seg_ids, text_len, ada_weight, text_weight, kv_weight, qkv_weight, out_weight, cross_q_weight, cross_out_weight, temp_qkv_weight, temp_out_weight, up_weight, down_weight, cross_gain):
    text_f = text.astype(jnp.float32)

    def forward(tokens_in, ada_w, text_w, kv_w, qkv_w, out_w, cross_q_w, cross_out_w, temp_qkv_w, temp_out_w, up_w, down_w, gain):
        results = []
        for bucket in range(BUCKETS):
            results.append(bucket_forward(tokens_in[bucket], text_f[bucket], timesteps[bucket], seg_ids[bucket], text_len[bucket], ada_w, text_w, kv_w, qkv_w, out_w, cross_q_w, cross_out_w, temp_qkv_w, temp_out_w, up_w, down_w, gain))
        return jnp.stack(results)
    params = (hidden.astype(jnp.float32), ada_weight.astype(jnp.float32), text_weight.astype(jnp.float32), kv_weight.astype(jnp.float32), qkv_weight.astype(jnp.float32), out_weight.astype(jnp.float32), cross_q_weight.astype(jnp.float32), cross_out_weight.astype(jnp.float32), temp_qkv_weight.astype(jnp.float32), temp_out_weight.astype(jnp.float32), up_weight.astype(jnp.float32), down_weight.astype(jnp.float32), cross_gain.astype(jnp.float32))
    result, pull_back = jax.vjp(forward, *params)
    grads = pull_back(cotangent.astype(jnp.float32))
    return (result.astype(jnp.bfloat16), grads[0].astype(jnp.bfloat16), grads[1], grads[2], grads[3], grads[4], grads[5], grads[6], grads[7], grads[8], grads[9], grads[10], grads[11], grads[12])
```

```python
import functools
import math

import jax
import jax.numpy as jnp
from jax import lax
from jax.experimental import pallas as pl
from jax.experimental.pallas import tpu as pltpu
from jax.sharding import PartitionSpec as P

HEADS = 16
MESH = pl.DeviceIdType.MESH
DMA = pltpu.SemaphoreType.DMA
LIMIT = 60 * 2**20


class Place:
    def __init__(self, wide):
        self.wide = wide
        self.chips = wide // 2
        self.plane = lax.axis_index("narrow")
        self.index = lax.axis_index("wide")
        self.core = lax.rem(self.index, 2)
        chip = lax.div(self.index, 2)
        odd = lax.rem(chip, 2)
        half = lax.div(chip, 2)
        self.pos = (1 - odd) * half + odd * (self.chips - 1 - half)

    def chip(self, step):
        n = self.chips
        q = lax.rem(self.pos + (step % n), n)
        high = lax.div(q, n // 2)
        return (1 - high) * (2 * q) + high * (2 * (n - q) - 1)

    def member(self, step, core=None):
        return 2 * self.chip(step) + (self.core if core is None else core)

    def near(self):
        return ((self.plane, self.member(1)), (self.plane, self.member(-1)),
                (1 - self.plane, self.index), (self.plane, self.index + 1 - 2 * self.core))

def greet(devices):
    barrier = pltpu.get_barrier_semaphore()
    for device in devices:
        pl.semaphore_signal(barrier, inc=1, device_id=device, device_id_type=MESH)
    pl.semaphore_wait(barrier, len(devices))

def remote(src, dst, send, recv, device):
    return pltpu.make_async_remote_copy(src_ref=src, dst_ref=dst, send_sem=send, recv_sem=recv,
                                        device_id=device, device_id_type=MESH)

def lanes(start, size):
    return pl.ds(pl.multiple_of(start, 128), size)

def gather_scratch(wide, count):
    chips = wide // 2; reach = chips // 2
    return [DMA((count, 2, reach, 2)), DMA((count, 2, reach, 2)), DMA((count, chips - 1)), DMA((count, chips - 1)),
            DMA((count, chips)), DMA((count, chips)), DMA((count,))]

def gather_steps(place, own, full, sems):
    ring_s, ring_r, side_s, side_r, twin_s, twin_r, loc = sems
    count = len(own)
    chips = place.chips
    reach = chips // 2
    right, left, across, twin = place.near()
    y = place.plane
    sends = []
    def go(c):
        c.start(); sends.append(c)
    def cols(i, part):
        width = own[i].shape[-1]; a = width // 3
        if part == 0: return lanes(y * (width - a), a)
        if part == 1: return lanes(a, width - 2 * a)
        return lanes((1 - y) * (width - a), a)
    def ring(i, d, s, part, j, src=None):
        sl = cols(i, part)
        source = full[i].at[j, :, sl] if src is None else src.at[:, sl]
        return remote(source, full[i].at[j, :, sl], ring_s.at[i, d, s-1, part], ring_r.at[i, d, s-1, part], (right, left)[d])
    def side(i, slot, j, part):
        sl = cols(i, part)
        return remote(full[i].at[j, :, sl], full[i].at[j, :, sl], side_s.at[i, slot], side_r.at[i, slot], across)
    def core_copy(i, slot, j, src=None):
        return remote(full[i].at[j] if src is None else src, full[i].at[j], twin_s.at[i, slot], twin_r.at[i, slot], twin)
    me = place.index
    for part in (0, 1):
        for i in range(count):
            for d in (0, 1):
                go(ring(i, d, 1, part, me, own[i]))
    local = []
    for i in range(count):
        c = pltpu.make_async_copy(own[i], full[i].at[me], loc.at[i]); c.start(); local.append(c)
        go(core_copy(i, chips - 1, me, own[i]))
    yield
    def shards(s):
        if s == reach: return [(2 * s - 2, place.member(s))]
        return [(2 * s - 2, place.member(-s)), (2 * s - 1, place.member(s))]
    def finish(s, i):
        for slot, j in shards(s):
            side(i, slot, j, 2).wait_recv()
            go(core_copy(i, slot, j))
    for s in range(1, reach + 1):
        for part in (0, 1):
            for i in range(count):
                for d in (0, 1):
                    if s == reach and part != d: continue
                    j = place.member(-s if d == 0 else s)
                    ring(i, d, s, part, j).wait_recv()
                    if s + 1 < reach or (s + 1 == reach and part == d):
                        go(ring(i, d, s + 1, part, j))
                    if part == 0:
                        go(side(i, 2 * s - 2 + (0 if s == reach else d), j, 0))
            yield
        if s > 1:
            for i in range(count): finish(s - 1, i)
    for i in range(count): finish(reach, i)
    yield
    other = 1 - place.core
    for s in range(1, reach + 1):
        for i in range(count):
            for (slot, _), step in zip(shards(s), (-s, s)):
                core_copy(i, slot, place.member(step, other)).wait_recv()
    for i in range(count):
        core_copy(i, chips - 1, place.member(0, other)).wait_recv()
    for c in local: c.wait()
    for c in sends: c.wait_send()

def gather_kernel(wide, count, *refs):
    own, full = refs[:count], refs[count:2*count]
    place = Place(wide)
    greet(place.near())
    for _ in gather_steps(place, own, full, refs[2*count:]): pass

ANY = pl.BlockSpec(memory_space=pl.ANY)
VM = pl.BlockSpec(memory_space=pltpu.VMEM)

def gather(wide, arrays, collective_id):
    count = len(arrays)
    return pl.pallas_call(
        functools.partial(gather_kernel, wide, count),
        out_shape=[jax.ShapeDtypeStruct((wide,) + a.shape, a.dtype) for a in arrays],
        in_specs=[ANY] * count,
        out_specs=[ANY] * count,
        scratch_shapes=gather_scratch(wide, count),
        compiler_params=pltpu.CompilerParams(collective_id=collective_id, has_side_effects=True),
        name="gather_rows",
    )(*arrays)

def scatter_scratch(wide, shapes):
    chips = wide // 2; reach = chips // 2; count = len(shapes)
    bufs = []
    for rows, width in shapes:
        bufs += [pltpu.VMEM((chips, rows, width), jnp.bfloat16),
                 pltpu.VMEM((chips, rows, width), jnp.bfloat16),
                 pltpu.VMEM((chips, rows, 2 * (width // 9)), jnp.bfloat16),
                 pltpu.VMEM((2, reach, rows, width - 2 * (width // 9)), jnp.bfloat16),
                 pltpu.VMEM((rows, width), jnp.bfloat16)]
    sems = [DMA((count, chips)), DMA((count, chips)), DMA((count, chips)), DMA((count, chips)), DMA((count, chips)),
            DMA((count, 2, reach)), DMA((count, 2, reach)), DMA((count,)), DMA((count,))]
    return bufs + sems

def scatter_steps(place, parts, outs, bufs, sems):
    load, twin_s, twin_r, side_s, side_r, ring_s, ring_r, last_s, last_r = sems
    count = len(parts)
    chips = place.chips
    reach = chips // 2
    right, left, across, twin = place.near()
    y = place.plane
    other = 1 - place.core
    sends = []
    def go(c):
        c.start(); sends.append(c)
    own = [bufs[5*i] for i in range(count)]; tw = [bufs[5*i+1] for i in range(count)]
    sd = [bufs[5*i+2] for i in range(count)]; rg = [bufs[5*i+3] for i in range(count)]; lt = [bufs[5*i+4] for i in range(count)]
    steps = [reach] + [x for s in range(reach - 1, 0, -1) for x in (s, -s)] + [0]
    slot_of = {s: k for k, s in enumerate(steps)}
    slot_of[-reach] = slot_of[reach]
    w = [o.shape[-1] // 9 for o in own]
    def ringcols(i, d, s):
        base = y * 2 * w[i]
        if s > 1: return base, 7 * w[i]
        k = 4 if (d + i) % 2 == 0 else 3
        return (base, 4 * w[i]) if k == 4 else (base + 4 * w[i], 3 * w[i])
    def twin_copy(i, k):
        return remote(parts[i].at[place.member(steps[k], other)], tw[i].at[k], twin_s.at[i, k], twin_r.at[i, k], twin)
    def load_copy(i, k):
        return pltpu.make_async_copy(parts[i].at[place.member(steps[k])], own[i].at[k], load.at[i, k])
    def side(i, k):
        return remote(own[i].at[k, :, lanes((1 - y) * 7 * w[i], 2 * w[i])], sd[i].at[k], side_s.at[i, k], side_r.at[i, k], across)
    def ring(i, d, s):
        start, size = ringcols(i, d, s)
        k = slot_of[(reach + 1 - s) if d == 0 else -(reach + 1 - s)]
        return remote(own[i].at[k, :, lanes(start, size)], rg[i].at[d, s-1, :, lanes(start - y * 2 * w[i], size)],
                      ring_s.at[i, d, s-1], ring_r.at[i, d, s-1], (right, left)[d])
    def last(i):
        sl = lanes(y * 2 * w[i], 7 * w[i])
        return remote(own[i].at[slot_of[0], :, sl], lt[i].at[:, sl], last_s.at[i], last_r.at[i], across)
    def add(i, dst_k, start, src, src_start, pieces):
        def one(t, _):
            to = lanes(start + t * w[i], w[i])
            value = own[i][dst_k, :, to].astype(jnp.float32)
            value += src[:, lanes(src_start + t * w[i], w[i])].astype(jnp.float32)
            own[i][dst_k, :, to] = value.astype(jnp.bfloat16)
            return 0
        lax.fori_loop(0, pieces, one, 0)
    for k in range(chips):
        for i in range(count):
            go(twin_copy(i, k)); load_copy(i, k).start()
    yield
    def pair(k):
        for i in range(count):
            load_copy(i, k).wait(); twin_copy(i, k).wait_recv()
            add(i, k, 0, tw[i].at[k], 0, 9)
            go(side(i, k))
    def planes(k):
        for i in range(count):
            side(i, k).wait_recv()
            add(i, k, y * 7 * w[i], sd[i].at[k], 0, 2)
    def ring_in(i, d, s):
        ring(i, d, s).wait_recv()
        start, size = ringcols(i, d, s)
        t = reach - s
        add(i, slot_of[t if d == 0 else -t], start, rg[i].at[d, s-1], start - y * 2 * w[i], size // w[i])
    need = {1: [slot_of[reach]]}
    for s in range(2, reach + 1):
        need[s] = [slot_of[reach + 1 - s], slot_of[-(reach + 1 - s)]]
    pair(0); yield
    pair(1); pair(2); yield
    planes(0)
    for i in range(count):
        for d in (0, 1): go(ring(i, d, 1))
    yield
    done = 3
    for s in range(2, reach + 1):
        while done < min(chips, 2 * s + 1):
            pair(done); done += 1
        if s == reach:
            while done < chips:
                pair(done); done += 1
        for k in need[s]: planes(k)
        yield
        for i in range(count):
            for d in (0, 1):
                ring_in(i, d, s - 1)
                go(ring(i, d, s))
        yield
    planes(slot_of[0])
    for i in range(count):
        for d in (0, 1): ring_in(i, d, reach)
        go(last(i))
    yield
    for i in range(count):
        last(i).wait_recv()
        k = slot_of[0]
        mine, theirs = y * 7 * w[i], (1 - y) * 7 * w[i]
        def copy(t, _, i=i, k=k, mine=mine, theirs=theirs):
            a, b = lanes(mine + t * w[i], w[i]), lanes(theirs + t * w[i], w[i])
            outs[i][:, a] = own[i][k, :, a]
            outs[i][:, b] = lt[i][:, b]
            return 0
        lax.fori_loop(0, 2, copy, 0)
        def both(t, _, i=i, k=k):
            c = lanes((2 + t) * w[i], w[i])
            outs[i][:, c] = (own[i][k, :, c].astype(jnp.float32) + lt[i][:, c].astype(jnp.float32)).astype(jnp.bfloat16)
            return 0
        lax.fori_loop(0, 5, both, 0)
    for c in sends: c.wait_send()

def scatter_kernel(wide, count, *refs):
    parts, outs = refs[:count], refs[count:2*count]
    bufs, sems = refs[2*count:7*count], refs[7*count:]
    place = Place(wide)
    greet(place.near())
    for _ in scatter_steps(place, parts, outs, bufs, sems): pass

def scatter(wide, arrays, collective_id):
    count = len(arrays)
    shapes = [a.shape[1:] for a in arrays]
    return pl.pallas_call(
        functools.partial(scatter_kernel, wide, count),
        out_shape=[jax.ShapeDtypeStruct(s, jnp.bfloat16) for s in shapes],
        in_specs=[ANY] * count,
        out_specs=[VM] * count,
        scratch_shapes=scatter_scratch(wide, shapes),
        compiler_params=pltpu.CompilerParams(collective_id=collective_id, has_side_effects=True, vmem_limit_bytes=LIMIT),
        name="scatter_rows",
    )(*arrays)


def front_scratch(wide, mod_block, text_block, kv_block):
    f32, bf16 = jnp.float32, jnp.bfloat16
    return ([pltpu.VMEM((wide,) + mod_block, f32), pltpu.VMEM((wide,) + text_block, bf16),
             pltpu.VMEM((wide,) + kv_block, bf16), pltpu.VMEM((wide,) + kv_block, bf16)]
            + [DMA((wide,))] * 10)


def peers(place):
    n = place.wide
    return [(t, lax.rem(place.index + t, n)) for t in range(1, n)]


def front_steps(place, mod_parts, text_parts, kv_rows, mod_all, kv_all, prompt, scratch):
    mod_in, text_in, kv_out, kv_in = scratch[:4]
    ms, mr, ts, tr, gs, gr, ks, kr, hs, hr = scratch[4:]
    n, me, y = place.wide, place.index, place.plane
    others = peers(place)
    sends = []

    def go(copy):
        copy.start()
        sends.append(copy)

    def mod_copy(t, j):
        return remote(mod_parts.at[j], mod_in.at[t], ms.at[t], mr.at[t], (y, j))

    def text_copy(t, j):
        return remote(text_parts.at[j], text_in.at[t], ts.at[t], tr.at[t], (y, j))

    def mod_back(t, j, i):
        return remote(mod_all.at[i], mod_all.at[i], gs.at[t], gr.at[t], (y, j))

    def kv_copy(t, j):
        return remote(kv_out.at[j], kv_in.at[t], ks.at[t], kr.at[t], (y, j))

    def kv_back(t, j, i):
        return remote(kv_all.at[i], kv_all.at[i], hs.at[t], hr.at[t], (y, j))

    for t, j in others:
        go(text_copy(t, j))
        go(mod_copy(t, j))
    yield
    total = text_parts[me].astype(jnp.float32)
    for t, j in others:
        text_copy(t, j).wait_recv()
        total += text_in[t].astype(jnp.float32)
    prompt[...] = total.astype(jnp.bfloat16)

    def block(j, _):
        kv_out[j] = jnp.dot(prompt[...], kv_rows[j], preferred_element_type=jnp.float32).astype(jnp.bfloat16)
        return 0

    lax.fori_loop(0, n, block, 0)
    for t, j in others:
        go(kv_copy(t, j))
    total = mod_parts[me]
    for t, j in others:
        mod_copy(t, j).wait_recv()
        total += mod_in[t]
    mod_all[me] = total
    for t, j in others:
        go(mod_back(t, j, me))
    yield
    total = kv_out[me].astype(jnp.float32)
    for t, j in others:
        kv_copy(t, j).wait_recv()
        total += kv_in[t].astype(jnp.float32)
    kv_all[me] = total.astype(jnp.bfloat16)
    for t, j in others:
        go(kv_back(t, j, me))
    yield
    for t, j in others:
        i = lax.rem(me + n - t, n)
        mod_back(t, j, i).wait_recv()
        kv_back(t, j, i).wait_recv()
    for copy in sends:
        copy.wait_send()


def start_kernel(wide, count, *refs):
    mod_parts, text_parts, kv_rows = refs[:3]
    own, refs = refs[3:3 + count], refs[3 + count:]
    mod_all, kv_all, prompt = refs[:3]
    full, refs = refs[3:3 + count], refs[3 + count:]
    place = Place(wide)
    right, left, across, twin = place.near()
    greet([across] + [(place.plane, j) for t, j in peers(place)])
    small = front_steps(place, mod_parts, text_parts, kv_rows, mod_all, kv_all, prompt, refs[:14])
    large = gather_steps(place, own, full, refs[14:])
    next(large)
    next(small)
    next(large)
    next(small)
    next(large)
    next(small)
    for _ in large:
        pass
    for _ in small:
        pass


def start(wide, mod_parts, text_parts, kv_rows, arrays, collective_id):
    count = len(arrays)
    kv_block = (text_parts.shape[1], kv_rows.shape[2])
    out = pl.pallas_call(
        functools.partial(start_kernel, wide, count),
        out_shape=[
            jax.ShapeDtypeStruct(mod_parts.shape, mod_parts.dtype),
            jax.ShapeDtypeStruct((wide,) + kv_block, jnp.bfloat16),
            jax.ShapeDtypeStruct(text_parts.shape[1:], jnp.bfloat16),
        ]
        + [jax.ShapeDtypeStruct((wide,) + a.shape, a.dtype) for a in arrays],
        in_specs=[VM] * 3 + [ANY] * count,
        out_specs=[VM] * 3 + [ANY] * count,
        scratch_shapes=front_scratch(wide, mod_parts.shape[1:], text_parts.shape[1:], kv_block)
        + gather_scratch(wide, count),
        compiler_params=pltpu.CompilerParams(
            collective_id=collective_id, has_side_effects=True, vmem_limit_bytes=LIMIT
        ),
        name="start",
    )(mod_parts, text_parts, kv_rows, *arrays)
    return out[0], out[1], out[2], out[3:]


def everyone(place):
    n, me, y = place.wide, place.index, place.plane
    near = [(t, (y, lax.rem(me + t, n))) for t in range(1, n)]
    return near + [(n + t, (1 - y, lax.rem(me + t, n))) for t in range(n)]


def finish_scratch(wide, vec_block, kv_block):
    f32, bf16 = jnp.float32, jnp.bfloat16
    return ([pltpu.VMEM((wide,) + vec_block, f32), pltpu.VMEM((wide,) + kv_block, bf16)]
            + [DMA((wide,))] * 4 + [DMA((2 * wide,))] * 6)


def finish_steps(place, vec_parts, kv_parts, kv_rows, vec_all, kv_all, prompt_all, scratch):
    vec_in, kv_in = scratch[:2]
    vs, vr, ks, kr, gs, gr, hs, hr, ps, pr = scratch[2:]
    n, me, y = place.wide, place.index, place.plane
    others = peers(place)
    all_others = everyone(place)
    sends = []

    def go(copy):
        copy.start()
        sends.append(copy)

    def vec_copy(t, j):
        return remote(vec_parts.at[j], vec_in.at[t], vs.at[t], vr.at[t], (y, j))

    def kv_copy(t, j):
        return remote(kv_parts.at[j], kv_in.at[t], ks.at[t], kr.at[t], (y, j))

    def source(u):
        return (y if u < n else 1 - y), lax.rem(me + 2 * n - u, n)

    def spread(ref, send, recv, u, device, plane, i):
        return remote(ref.at[plane, i], ref.at[plane, i], send.at[u], recv.at[u], device)

    for t, j in others:
        go(kv_copy(t, j))
        go(vec_copy(t, j))
    total = kv_parts[me].astype(jnp.float32)
    for t, j in others:
        kv_copy(t, j).wait_recv()
        total += kv_in[t].astype(jnp.float32)
    kv_all[y, me] = total.astype(jnp.bfloat16)
    for u, device in all_others:
        go(spread(kv_all, hs, hr, u, device, y, me))
    total = vec_parts[me]
    for t, j in others:
        vec_copy(t, j).wait_recv()
        total += vec_in[t]
    vec_all[y, me] = total
    for u, device in all_others:
        go(spread(vec_all, gs, gr, u, device, y, me))
    yield
    for u, device in all_others:
        plane, i = source(u)
        if u < n:
            spread(kv_all, hs, hr, u, device, plane, i).wait_recv()

    def block(j, total):
        return total + lax.dot_general(
            kv_all[y, j], kv_rows[j], (((1,), (1,)), ((), ())), preferred_element_type=jnp.float32
        )

    rows = lax.fori_loop(0, n, block, jnp.zeros(prompt_all.shape[2:], jnp.float32))
    prompt_all[y, me] = rows.astype(jnp.bfloat16)
    for u, device in all_others:
        go(spread(prompt_all, ps, pr, u, device, y, me))
    yield
    for u, device in all_others:
        plane, i = source(u)
        if u >= n:
            spread(kv_all, hs, hr, u, device, plane, i).wait_recv()
        spread(vec_all, gs, gr, u, device, plane, i).wait_recv()
        spread(prompt_all, ps, pr, u, device, plane, i).wait_recv()
    for copy in sends:
        copy.wait_send()


def finish_kernel(wide, vec_parts, kv_parts, kv_rows, vec_all, kv_all, prompt_all, *scratch):
    place = Place(wide)
    greet([device for u, device in everyone(place)])
    for _ in finish_steps(place, vec_parts, kv_parts, kv_rows, vec_all, kv_all, prompt_all, scratch):
        pass


def finish(wide, vec_parts, kv_parts, kv_rows, collective_id):
    text_count, rows = kv_parts.shape[1], kv_rows.shape[1]
    return pl.pallas_call(
        functools.partial(finish_kernel, wide),
        out_shape=[
            jax.ShapeDtypeStruct((2,) + vec_parts.shape, jnp.float32),
            jax.ShapeDtypeStruct((2,) + kv_parts.shape, jnp.bfloat16),
            jax.ShapeDtypeStruct((2, wide, text_count, rows), jnp.bfloat16),
        ],
        in_specs=[VM] * 3,
        out_specs=[VM] * 3,
        scratch_shapes=finish_scratch(wide, vec_parts.shape[1:], kv_parts.shape[1:]),
        compiler_params=pltpu.CompilerParams(
            collective_id=collective_id, has_side_effects=True, vmem_limit_bytes=LIMIT
        ),
        name="finish",
    )(vec_parts, kv_parts, kv_rows)


def with_halo(block, sides, width):
    for axis, dim in sides:
        count = lax.axis_size(axis)
        forward = [(i, i + 1) for i in range(count - 1)]
        backward = [(target, source) for source, target in forward]
        low = lax.ppermute(
            lax.slice_in_dim(block, block.shape[dim] - width, None, axis=dim), axis, forward
        )
        high = lax.ppermute(lax.slice_in_dim(block, 0, width, axis=dim), axis, backward)
        block = jnp.concatenate([low, block, high], axis=dim)
    return block


def layer_norm(values):
    centred = values - jnp.mean(values, -1, keepdims=True)
    variance = jnp.mean(centred * centred, -1, keepdims=True)
    return centred * lax.rsqrt(variance + 1e-06)


def modulate(values, shift_vec, scale_vec):
    return layer_norm(values) * (1.0 + scale_vec) + shift_vec


def scaled_norm(values, gain_vec):
    return layer_norm(values) * gain_vec


def time_embed(steps, model_width):
    half_width = model_width // 2
    freqs = jnp.exp(-math.log(10000.0) * jnp.arange(half_width, dtype=jnp.float32) / half_width)
    angles = steps.astype(jnp.float32)[:, None] * freqs[None, :]
    return jnp.concatenate([jnp.cos(angles), jnp.sin(angles)], -1)


def project(operand, weights):
    return jnp.dot(operand, weights, preferred_element_type=jnp.float32)


def project_back(gradient, weights):
    return lax.dot_general(
        gradient, weights, (((1,), (1,)), ((), ())), preferred_element_type=jnp.float32
    )


def project_rows(operand, gradient):
    return lax.dot_general(
        operand, gradient, (((0,), (0,)), ((), ())), preferred_element_type=jnp.float32
    )


def whole(value):
    return value.reshape(-1, value.shape[-1])


def part_rows(wide, operand, gradient):
    return project_rows(operand, gradient).astype(jnp.bfloat16).reshape(wide, -1, gradient.shape[-1])


def body(
    hidden,
    cotangent,
    text,
    timesteps,
    seg_ids,
    text_len,
    ada_weight,
    text_weight,
    kv_weight,
    qkv_weight,
    out_weight,
    cross_q_weight,
    cross_out_weight,
    temp_qkv_weight,
    temp_out_weight,
    up_weight,
    down_weight,
    cross_gain,
):
    frames = hidden.shape[1]
    patches = hidden.shape[2]
    model_width = hidden.shape[3]
    head_count = HEADS
    head_size = model_width // head_count
    row_count = frames * patches
    text_count = text.shape[1]
    position = lax.axis_index("wide")
    rows_model = ada_weight.shape[0]
    rows_text = text_weight.shape[0]
    score_scale = head_size ** (-0.5)
    plane = lax.axis_index("narrow")
    wide = lax.axis_size("wide")

    def swap(value):
        return lax.ppermute(value, "narrow", [(0, 1), (1, 0)])

    def by_plane(own, other):
        return jnp.where(plane == 0, jnp.stack([own, other]), jnp.stack([other, own]))

    def blocks(value):
        return value.reshape(value.shape[0], wide, -1).transpose(1, 0, 2)

    signal = jax.nn.silu(time_embed(timesteps, model_width)[0]).astype(jnp.bfloat16)
    signal_rows = lax.dynamic_slice_in_dim(signal, position * rows_model, rows_model)
    mod_part = jnp.dot(signal_rows, ada_weight, preferred_element_type=jnp.float32)
    prompt_rows = lax.dynamic_slice_in_dim(text[0], position * rows_text, rows_text, 1)
    text_part = project(prompt_rows, text_weight)
    kv_rows = blocks(kv_weight)
    modulation, kv_all, prompt_cols, (full_qkv, full_out) = start(
        wide,
        mod_part.reshape(wide, 1, -1),
        blocks(text_part).astype(jnp.bfloat16),
        kv_rows,
        (qkv_weight, out_weight),
        0,
    )
    full_qkv, full_out = whole(full_qkv), whole(full_out)
    modulation = modulation.reshape(9, model_width)
    shift_a, scale_a, gate_a = (modulation[0], modulation[1], modulation[2])
    shift_t, scale_t, gate_t = (modulation[3], modulation[4], modulation[5])
    shift_m, scale_m, gate_m = (modulation[6], modulation[7], modulation[8])
    text_kv = kv_all.transpose(1, 0, 2).reshape(text_count, 2 * model_width)
    keys_c = text_kv[:, :model_width].reshape(text_count, head_count, head_size)
    values_c = text_kv[:, model_width:].reshape(text_count, head_count, head_size)
    valid = jnp.arange(text_count) < text_len[0]
    tokens = hidden[0].reshape(row_count, model_width).astype(jnp.float32)
    normed_a = modulate(tokens, shift_a, scale_a).astype(jnp.bfloat16)
    qkv_a = (
        project(normed_a, full_qkv)
        .astype(jnp.bfloat16)
        .reshape(frames, patches, 3, head_count, head_size)
    )
    query_a, keys_a, values_a = (qkv_a[:, :, 0], qkv_a[:, :, 1], qkv_a[:, :, 2])
    scores_a = (
        jnp.einsum("fphd,fqhd->fhpq", query_a, keys_a, preferred_element_type=jnp.float32)
        * score_scale
    )
    total_a = jax.nn.logsumexp(scores_a, axis=-1, keepdims=True)
    probs_a = jnp.exp(scores_a - total_a).astype(jnp.bfloat16)
    attn_a = jnp.einsum("fhpq,fqhd->fphd", probs_a, values_a, preferred_element_type=jnp.float32)
    attn_a = attn_a.astype(jnp.bfloat16).reshape(row_count, model_width)
    branch_a = project(attn_a, full_out)
    first = tokens + gate_a * branch_a
    full_cross_q, full_cross_out, full_temp_qkv, full_temp_out = map(
        whole, gather(wide, (cross_q_weight, cross_out_weight, temp_qkv_weight, temp_out_weight), 1)
    )
    normed_c = scaled_norm(first, cross_gain).astype(jnp.bfloat16)
    query_c = (
        project(normed_c, full_cross_q)
        .astype(jnp.bfloat16)
        .reshape(row_count, head_count, head_size)
    )
    scores_c = (
        jnp.einsum("nhd,lhd->hnl", query_c, keys_c, preferred_element_type=jnp.float32)
        * score_scale
    )
    scores_c = jnp.where(valid, scores_c, -1e30)
    total_c = jax.nn.logsumexp(scores_c, axis=-1, keepdims=True)
    probs_c = jnp.exp(scores_c - total_c).astype(jnp.bfloat16)
    attn_c = jnp.einsum("hnl,lhd->nhd", probs_c, values_c, preferred_element_type=jnp.float32)
    attn_c = attn_c.astype(jnp.bfloat16).reshape(row_count, model_width)
    branch_c = project(attn_c, full_cross_out)
    second = first + branch_c
    normed_t = modulate(second, shift_t, scale_t).astype(jnp.bfloat16)
    qkv_t = (
        project(normed_t, full_temp_qkv)
        .astype(jnp.bfloat16)
        .reshape(frames, patches, 3 * model_width)
    )
    query_t = qkv_t[:, :, :model_width].reshape(frames, patches, head_count, head_size)
    nearby = with_halo(qkv_t[:, :, model_width:], (("wide", 0),), 2)
    clip_pad = jnp.pad(seg_ids[0], 2, constant_values=-1)
    clip_local = lax.dynamic_slice_in_dim(clip_pad, position * frames, frames + 4)
    own_clip = clip_local[2 : frames + 2]
    allowed = jnp.stack(
        [clip_local[offset : offset + frames] == own_clip for offset in range(5)], -1
    )

    def window_keys(offset):
        return nearby[offset : offset + frames, :, :model_width].reshape(
            frames, patches, head_count, head_size
        )

    def window_values(offset):
        return nearby[offset : offset + frames, :, model_width:].reshape(
            frames, patches, head_count, head_size
        )

    def temporal_probs():
        score_list = [
            jnp.einsum(
                "fphd,fphd->fph", query_t, window_keys(offset), preferred_element_type=jnp.float32
            )
            * score_scale
            for offset in range(5)
        ]
        scores_t = jnp.where(allowed[:, None, None, :], jnp.stack(score_list, -1), -1e30)
        return jax.nn.softmax(scores_t, -1)

    probs_t = temporal_probs()
    probs_low_t = probs_t.astype(jnp.bfloat16)
    attn_t = jnp.zeros((frames, patches, head_count, head_size), jnp.float32)
    for offset in range(5):
        attn_t = attn_t + jnp.einsum(
            "fph,fphd->fphd",
            probs_low_t[..., offset],
            window_values(offset),
            preferred_element_type=jnp.float32,
        )
    attn_t = attn_t.astype(jnp.bfloat16).reshape(row_count, model_width)
    branch_t = project(attn_t, full_temp_out)
    third = second + gate_t * branch_t
    full_up, full_down = map(whole, gather(wide, (up_weight, down_weight), 2))
    normed_m = modulate(third, shift_m, scale_m).astype(jnp.bfloat16)
    hidden_m = project(normed_m, full_up)
    act = jax.nn.gelu(hidden_m, approximate=True).astype(jnp.bfloat16)
    branch_m = project(act, full_down)
    result = third + gate_m * branch_m
    block_out = result.astype(jnp.bfloat16).reshape(1, frames, patches, model_width)
    gradient = cotangent[0].reshape(row_count, model_width).astype(jnp.float32)
    d_gate_m = jnp.sum(gradient * branch_m, 0)
    d_branch_m = (gate_m * gradient).astype(jnp.bfloat16)
    back_down = full_down
    grad_down = part_rows(wide, act, d_branch_m)
    d_act = project_back(d_branch_m, back_down)
    unused_gelu, gelu_back = jax.vjp(lambda values: jax.nn.gelu(values, approximate=True), hidden_m)
    d_hidden_m = gelu_back(d_act)[0].astype(jnp.bfloat16)
    back_up = full_up
    grad_up = part_rows(wide, normed_m, d_hidden_m)
    grad_up, grad_down = scatter(wide, (grad_up, grad_down), 3)
    d_normed_m = project_back(d_hidden_m, back_up)
    unused_mlp, mlp_back = jax.vjp(modulate, third, shift_m, scale_m)
    d_third, d_shift_m, d_scale_m = mlp_back(d_normed_m)
    gradient = gradient + d_third
    d_gate_t = jnp.sum(gradient * branch_t, 0)
    d_branch_t = (gate_t * gradient).astype(jnp.bfloat16)
    back_temp_qkv, back_temp_out = full_temp_qkv, full_temp_out
    grad_temp_out = part_rows(wide, attn_t, d_branch_t)
    d_attn_t = (
        project_back(d_branch_t, back_temp_out)
        .astype(jnp.bfloat16)
        .reshape(frames, patches, head_count, head_size)
    )
    d_prob_list = [
        jnp.einsum(
            "fphd,fphd->fph", d_attn_t, window_values(offset), preferred_element_type=jnp.float32
        )
        for offset in range(5)
    ]
    d_probs_t = jnp.stack(d_prob_list, -1)
    inner_t = jnp.sum(probs_t * d_probs_t, -1, keepdims=True)
    d_scores_t = probs_t * (d_probs_t - inner_t) * score_scale
    d_query_t = jnp.zeros((frames, patches, head_count, head_size), jnp.float32)
    d_nearby = jnp.zeros((frames + 4, patches, 2 * model_width), jnp.float32)
    for offset in range(5):
        d_query_t = d_query_t + d_scores_t[..., offset, None] * window_keys(offset)
        d_keys_w = (d_scores_t[..., offset, None] * query_t).reshape(frames, patches, model_width)
        d_values_w = (
            probs_low_t[..., offset, None].astype(jnp.float32) * d_attn_t.astype(jnp.float32)
        ).reshape(frames, patches, model_width)
        piece = jnp.concatenate([d_keys_w, d_values_w], -1)
        d_nearby = d_nearby + jnp.pad(piece, ((offset, 4 - offset), (0, 0), (0, 0)))
    edge_grads = jnp.concatenate([d_nearby[:2], d_nearby[frames + 2 :]], 0)
    arrived = with_halo(edge_grads.astype(jnp.bfloat16), (("wide", 0),), 2).astype(edge_grads.dtype)
    d_kv_t = d_nearby[2 : frames + 2]
    d_kv_t = d_kv_t + jnp.pad(arrived[:2], ((0, frames - 2), (0, 0), (0, 0)))
    d_kv_t = d_kv_t + jnp.pad(arrived[6:], ((frames - 2, 0), (0, 0), (0, 0)))
    d_qkv_t = jnp.concatenate([d_query_t.reshape(frames, patches, model_width), d_kv_t], -1)
    d_qkv_t = d_qkv_t.reshape(row_count, 3 * model_width).astype(jnp.bfloat16)
    grad_temp_qkv = part_rows(wide, normed_t, d_qkv_t)
    d_normed_t = project_back(d_qkv_t, back_temp_qkv)
    unused_temp, temp_back = jax.vjp(modulate, second, shift_t, scale_t)
    d_second, d_shift_t, d_scale_t = temp_back(d_normed_t)
    gradient = gradient + d_second
    d_branch_c = gradient.astype(jnp.bfloat16)
    back_cross_q, back_cross_out = full_cross_q, full_cross_out
    grad_cross_out = part_rows(wide, attn_c, d_branch_c)
    d_attn_c = (
        project_back(d_branch_c, back_cross_out)
        .astype(jnp.bfloat16)
        .reshape(row_count, head_count, head_size)
    )
    probs_full_c = jnp.exp(scores_c - total_c)
    d_probs_c = jnp.einsum("nhd,lhd->hnl", d_attn_c, values_c, preferred_element_type=jnp.float32)
    inner_c = jnp.sum(probs_full_c * d_probs_c, -1, keepdims=True)
    d_scores_c = (probs_full_c * (d_probs_c - inner_c)).astype(jnp.bfloat16)
    d_query_c = (
        jnp.einsum("hnl,lhd->nhd", d_scores_c, keys_c, preferred_element_type=jnp.float32)
        * score_scale
    )
    d_query_c = d_query_c.reshape(row_count, model_width).astype(jnp.bfloat16)
    d_keys_c = (
        jnp.einsum("hnl,nhd->lhd", d_scores_c, query_c, preferred_element_type=jnp.float32)
        * score_scale
    )
    d_values_c = jnp.einsum("hnl,nhd->lhd", probs_c, d_attn_c, preferred_element_type=jnp.float32)
    d_kv_part = jnp.concatenate(
        [d_keys_c.reshape(text_count, model_width), d_values_c.reshape(text_count, model_width)], -1
    )
    grad_cross_q = part_rows(wide, normed_c, d_query_c)
    grad_cross_q, grad_cross_out, grad_temp_qkv, grad_temp_out = scatter(
        wide, (grad_cross_q, grad_cross_out, grad_temp_qkv, grad_temp_out), 4
    )
    d_normed_c = project_back(d_query_c, back_cross_q)
    unused_cross, cross_back = jax.vjp(scaled_norm, first, cross_gain)
    d_first, d_gain_part = cross_back(d_normed_c)
    gradient = gradient + d_first
    d_gate_a = jnp.sum(gradient * branch_a, 0)
    d_branch_a = (gate_a * gradient).astype(jnp.bfloat16)
    back_qkv, back_out = full_qkv, full_out
    grad_out = part_rows(wide, attn_a, d_branch_a)
    d_attn_a = (
        project_back(d_branch_a, back_out)
        .astype(jnp.bfloat16)
        .reshape(frames, patches, head_count, head_size)
    )
    probs_full_a = jnp.exp(scores_a - total_a)
    d_probs_a = jnp.einsum(
        "fphd,fqhd->fhpq", d_attn_a, values_a, preferred_element_type=jnp.float32
    )
    inner_a = jnp.sum(probs_full_a * d_probs_a, -1, keepdims=True)
    d_scores_a = (probs_full_a * (d_probs_a - inner_a)).astype(jnp.bfloat16)
    d_query_a = (
        jnp.einsum("fhpq,fqhd->fphd", d_scores_a, keys_a, preferred_element_type=jnp.float32)
        * score_scale
    )
    d_keys_a = (
        jnp.einsum("fhpq,fphd->fqhd", d_scores_a, query_a, preferred_element_type=jnp.float32)
        * score_scale
    )
    d_values_a = jnp.einsum(
        "fhpq,fphd->fqhd", probs_a, d_attn_a, preferred_element_type=jnp.float32
    )
    d_qkv_a = (
        jnp.stack([d_query_a, d_keys_a, d_values_a], 2)
        .reshape(row_count, 3 * model_width)
        .astype(jnp.bfloat16)
    )
    grad_qkv = part_rows(wide, normed_a, d_qkv_a)
    grad_qkv, grad_out = scatter(wide, (grad_qkv, grad_out), 5)
    d_normed_a = project_back(d_qkv_a, back_qkv)
    unused_spatial, spatial_back = jax.vjp(modulate, tokens, shift_a, scale_a)
    d_start, d_shift_a, d_scale_a = spatial_back(d_normed_a)
    grad_hidden = (gradient + d_start).astype(jnp.bfloat16).reshape(1, frames, patches, model_width)
    vectors = jnp.concatenate(
        [
            d_shift_a,
            d_scale_a,
            d_gate_a,
            d_shift_t,
            d_scale_t,
            d_gate_t,
            d_shift_m,
            d_scale_m,
            d_gate_m,
            d_gain_part,
        ]
    )
    vec_all, d_kv_all, d_prompt_all = finish(
        wide, vectors.reshape(wide, 1, -1), blocks(d_kv_part).astype(jnp.bfloat16), kv_rows, 6
    )
    vec_all = vec_all.reshape(2, -1)
    d_modulation, d_gain = vec_all[:, : 9 * model_width], vec_all[:, 9 * model_width :]

    def merged(value):
        return value.transpose(0, 2, 1, 3).reshape(2 * text_count, -1)

    both_cols = by_plane(prompt_cols, swap(prompt_cols)).reshape(2 * text_count, -1)
    both_rows = by_plane(prompt_rows, swap(prompt_rows)).reshape(2 * text_count, -1)
    both_signal = by_plane(signal_rows, swap(signal_rows)).astype(jnp.float32)
    grad_kv = project_rows(both_cols, merged(d_kv_all))
    grad_text = project_rows(both_rows, merged(d_prompt_all))
    grad_ada = (
        both_signal[0][:, None] * d_modulation[0][None, :]
        + both_signal[1][:, None] * d_modulation[1][None, :]
    )
    grad_gain = d_gain[0] + d_gain[1]
    grad_qkv, grad_out, grad_cross_q, grad_cross_out = (
        grad_qkv.astype(jnp.float32), grad_out.astype(jnp.float32),
        grad_cross_q.astype(jnp.float32), grad_cross_out.astype(jnp.float32),
    )
    grad_temp_qkv, grad_temp_out, grad_up, grad_down = (
        grad_temp_qkv.astype(jnp.float32), grad_temp_out.astype(jnp.float32),
        grad_up.astype(jnp.float32), grad_down.astype(jnp.float32),
    )
    return (
        block_out,
        grad_hidden,
        grad_ada,
        grad_text,
        grad_kv,
        grad_qkv,
        grad_out,
        grad_cross_q,
        grad_cross_out,
        grad_temp_qkv,
        grad_temp_out,
        grad_up,
        grad_down,
        grad_gain,
    )


def solution(mesh):
    return jax.shard_map(
        body,
        mesh=mesh,
        in_specs=(
            P("narrow", "wide", None, None),
            P("narrow", "wide", None, None),
            P("narrow", None, None),
            P("narrow"),
            P("narrow", None),
            P("narrow"),
            P("wide", None),
            P("wide", None),
            P("wide", None),
            P("wide", None),
            P("wide", None),
            P("wide", None),
            P("wide", None),
            P("wide", None),
            P("wide", None),
            P("wide", None),
            P("wide", None),
            P(),
        ),
        out_specs=(
            P("narrow", "wide", None, None),
            P("narrow", "wide", None, None),
            P("wide", None),
            P("wide", None),
            P("wide", None),
            P("wide", None),
            P("wide", None),
            P("wide", None),
            P("wide", None),
            P("wide", None),
            P("wide", None),
            P("wide", None),
            P("wide", None),
            P(),
        ),
        check_vma=False,
    )
```

```python
import functools
import math

import jax
import jax.numpy as jnp
from jax import lax
from jax.experimental import pallas as pl
from jax.experimental.pallas import tpu as pltpu
from jax.sharding import PartitionSpec as P

HEADS = 16
LIMIT = 60 * 2**20
MESH = pl.DeviceIdType.MESH
DMA = pltpu.SemaphoreType.DMA
VM = pl.BlockSpec(memory_space=pltpu.VMEM)
ANY = pl.BlockSpec(memory_space=pl.ANY)
f32, bf16 = jnp.float32, jnp.bfloat16
NN, NT, TN = (((1,), (0,)), ((), ())), (((1,), (1,)), ((), ())), (((0,), (0,)), ((), ()))


def dot(a, b, dims=NN):
    return lax.dot_general(a, b, dims, preferred_element_type=jnp.float32)


def row_blocks(count, size, step, carry=0, unroll=1):
    def one(r, value):
        return step(pl.ds(pl.multiple_of(r * size, size), size), value)
    return lax.fori_loop(0, count // size, one, carry, unroll=unroll)


def normal(value):
    centred = value - jnp.mean(value, -1, keepdims=True)
    scale = lax.rsqrt(jnp.mean(centred * centred, -1, keepdims=True) + 1e-06)
    return centred * scale, scale


def windows(width):
    size = width // HEADS
    found = []
    for head in range(HEADS):
        low, high = head * size, (head + 1) * size
        start = low // 128 * 128
        found.append((start, -(-high // 128) * 128 - start))
    return found


def head_mask(heads_ref, head, start, size):
    return heads_ref[head : head + 1, start : start + size]


def softmax_down(scores):
    exps = jnp.exp(scores - jnp.max(scores, 0, keepdims=True))
    return exps * (1.0 / jnp.sum(exps, 0, keepdims=True))


GROUPS = 4


def by_heads(frames, patches, width, step, tick):
    spans = list(enumerate(windows(width)))
    size = HEADS // GROUPS
    for group in range(GROUPS):

        def frame(f, _):
            rows = pl.ds(pl.multiple_of(f * patches, 16), patches)
            for head, (start, lanes_taken) in spans[group * size : (group + 1) * size]:
                step(rows, head, start, lanes_taken)
            tick.inside(f, 0, frames)
            return 0

        lax.fori_loop(0, frames, frame, 0)


def clear(ref):
    ref[...] = jnp.zeros_like(ref)


def spatial_attention(tick, qkv, heads, attn, frames, patches):
    width = attn.shape[-1]
    scale = (width // HEADS) ** -0.5
    clear(attn)

    def step(rows, head, start, size):
        mask = head_mask(heads, head, start, size)
        query = qkv[rows, start : start + size] * mask
        keys = qkv[rows, width + start : width + start + size]
        values = qkv[rows, 2 * width + start : 2 * width + start + size] * mask
        probs = softmax_down(dot(keys, query, NT) * scale).astype(bf16)
        attn[rows, start : start + size] += dot(probs, values, TN).astype(bf16)

    by_heads(frames, patches, width, step, tick)


def spatial_attention_back(tick, qkv, d_attn, heads, d_qkv, frames, patches):
    width = d_attn.shape[-1]
    scale = (width // HEADS) ** -0.5
    clear(d_qkv)

    def step(rows, head, start, size):
        mask = head_mask(heads, head, start, size)
        query = qkv[rows, start : start + size] * mask
        keys = qkv[rows, width + start : width + start + size]
        values = qkv[rows, 2 * width + start : 2 * width + start + size]
        grad = d_attn[rows, start : start + size] * mask
        probs = softmax_down(dot(keys, query, NT) * scale)
        d_probs = dot(values, grad, NT)
        inner = jnp.sum(probs * d_probs, 0, keepdims=True)
        d_scores = (probs * (d_probs - inner)).astype(bf16)
        d_qkv[rows, start : start + size] += (dot(d_scores, keys * mask, TN) * scale).astype(bf16)
        d_qkv[rows, width + start : width + start + size] += (dot(d_scores, query) * scale).astype(bf16)
        d_qkv[rows, 2 * width + start : 2 * width + start + size] += dot(probs.astype(bf16), grad).astype(bf16)

    by_heads(frames, patches, width, step, tick)


def matmul(x, w, out, tick, unit=1152):
    for c in range(0, w.shape[1], unit):
        out[:, c : c + unit] = dot(x[...], w[:, c : c + unit]).astype(out.dtype)
        tick()


def spatial_kernel(frames, patches, tick, x, mod, heads, w_qkv, w_out, normed, qkv, attn, branch, first):
    rows = frames * patches

    def norm(at, _):
        hat, _unused = normal(x[at, :].astype(f32))
        normed[at, :] = (hat * (1.0 + mod[1:2, :]) + mod[0:1, :]).astype(bf16)
        return 0

    row_blocks(rows, 16, norm, unroll=3)
    tick()
    matmul(normed, w_qkv, qkv, tick)
    spatial_attention(tick, qkv, heads, attn, frames, patches)
    product = dot(attn[...], w_out[...])
    branch[...] = product.astype(bf16)
    first[...] = x[...].astype(f32) + mod[2:3, :] * product


def back_norm(rows, hat_of, gain_row, d_normed, add_to, sums, size=16):
    width = d_normed.shape[-1]

    def one(at, carry):
        total, weighted = carry
        hat, scale = normal(hat_of(at))
        grad = d_normed[at, :]
        total += grad.reshape(size // 8, 8, width).sum(0)
        product = grad * hat
        weighted += product.reshape(size // 8, 8, width).sum(0)
        d_hat = grad * gain_row
        d_value = scale * (d_hat - jnp.mean(d_hat, -1, keepdims=True)
                           - hat * jnp.mean(d_hat * hat, -1, keepdims=True))
        add_to(at, d_value)
        return total, weighted

    zero = jnp.zeros((8, width), f32)
    total, weighted = row_blocks(rows, size, one, (zero, zero))
    return jnp.sum(total, 0, keepdims=True), jnp.sum(weighted, 0, keepdims=True)


def gate_back(rows, gradient, branch, gate_row, d_branch, size=16):
    width = gradient.shape[-1]

    def one(at, total):
        grad = gradient[at, :]
        d_branch[at, :] = (gate_row * grad).astype(bf16)
        return total + (grad * branch[at, :].astype(f32)).reshape(size // 8, 8, width).sum(0)

    total = row_blocks(rows, size, one, jnp.zeros((8, width), f32))
    return jnp.sum(total, 0, keepdims=True)


def spatial_back_kernel(frames, patches, tick, gradient, x, mod, heads, w_qkv, w_out, normed, qkv, attn, branch,
                        d_hidden, g_qkv, g_out, d_mod, d_branch, d_attn, d_qkv, d_normed, part, load):
    rows, width = x.shape

    def fetch(n):
        return pltpu.make_async_copy(w_qkv.at[:, pl.ds(n * width, width)], part.at[n % 2], load.at[n % 2])

    fetch(0).start()
    fetch(1).start()
    d_mod[2:3, :] = gate_back(rows, gradient, branch, mod[2:3, :], d_branch)
    tick()
    g_out[...] = dot(attn[...], d_branch[...], TN).astype(bf16)
    tick()
    d_attn[...] = dot(d_branch[...], w_out[...], NT).astype(bf16)
    tick()
    spatial_attention_back(tick, qkv, d_attn, heads, d_qkv, frames, patches)
    for n in range(3):
        cols = slice(n * width, (n + 1) * width)
        g_qkv[:, cols] = dot(normed[...], d_qkv[:, cols], TN).astype(bf16)
        tick()
        fetch(n).wait()
        product = dot(d_qkv[:, cols], part[n % 2], NT)
        if n == 0:
            d_normed[...] = product
            fetch(2).start()
        else:
            d_normed[...] += product
        tick()

    def add_to(at, value):
        d_hidden[at, :] = (gradient[at, :] + value).astype(bf16)

    d_mod[0:1, :], d_mod[1:2, :] = back_norm(
        rows, lambda at: x[at, :].astype(f32), 1.0 + mod[1:2, :], d_normed, add_to, None)


class Halo:
    def __init__(self, place, sems):
        n, me = place.wide, place.index
        self.sems = sems
        self.beyond = ((place.plane, lax.rem(me + 1, n)), (place.plane, lax.rem(me + n - 1, n)))

    def copy(self, way, source, target):
        return remote(source, target, self.sems.at[0, way], self.sems.at[1, way], self.beyond[way])


def cross_kernel(wide, frames, patches, tick, first, gain, mod, heads, valid, text_kv, w_q, w_out, w_tqkv,
                 normed, query, attn, second, normed_t, qkv_t, near, outer, sems):
    rows, width = first.shape
    scale = (width // HEADS) ** -0.5
    halo = Halo(Place(wide), sems)

    def norm(at, _):
        hat, _unused = normal(first[at, :])
        normed[at, :] = (hat * gain[...]).astype(bf16)
        return 0

    row_blocks(rows, 16, norm, unroll=3)
    tick()
    query[...] = dot(normed[...], w_q[...]).astype(bf16)
    clear(attn)
    tick()

    def step(at, head, start, size):
        mask = head_mask(heads, head, start, size)
        q = query[at, start : start + size] * mask
        keys = text_kv[:, start : start + size]
        values = text_kv[:, width + start : width + start + size] * mask
        scores = jnp.where(valid[...] > 0, dot(keys, q, NT) * scale, -1e30)
        attn[at, start : start + size] += dot(softmax_down(scores).astype(bf16), values, TN).astype(bf16)

    by_heads(frames, patches, width, step, tick)
    second[...] = first[...] + dot(attn[...], w_out[...])
    tick()

    def norm_t(at, _):
        hat, _unused = normal(second[at, :])
        normed_t[at, :] = (hat * (1.0 + mod[4:5, :]) + mod[3:4, :]).astype(bf16)
        return 0

    row_blocks(rows, 16, norm_t, unroll=3)
    edge = 2 * patches
    sends = [halo.copy(0, normed_t.at[rows - edge :, :], outer.at[:edge, :]),
             halo.copy(1, normed_t.at[:edge, :], outer.at[edge:, :])]
    for copy in sends:
        copy.start()
    tick()
    matmul(normed_t, w_tqkv, qkv_t, tick)
    for f in range(frames):
        near[2 + f] = qkv_t[f * patches : (f + 1) * patches, width:]
    tick.finish()
    for n, copy in enumerate(sends):
        copy.wait_recv()
        side = outer[n * edge : (n + 1) * edge, :]
        for c in (width, 2 * width):
            found = dot(side, w_tqkv[:, c : c + width]).astype(bf16)
            for f in range(2):
                near[n * (frames + 2) + f, :, c - width : c] = found[f * patches : (f + 1) * patches]
            tick()
    for copy in sends:
        copy.wait_send()


def cross_back_kernel(frames, patches, tick, gradient, first, gain, heads, valid, text_kv, w_q, w_out, normed, query,
                      attn, gradient_out, g_q, g_out, d_gain, d_kv, d_branch, d_attn, d_query, d_normed):
    rows, width = first.shape
    scale = (width // HEADS) ** -0.5
    d_branch[...] = gradient[...].astype(bf16)
    clear(d_query)
    clear(d_kv)
    tick()
    g_out[...] = dot(attn[...], d_branch[...], TN).astype(bf16)
    tick()
    d_attn[...] = dot(d_branch[...], w_out[...], NT).astype(bf16)
    tick()

    def step(at, head, start, size):
        mask = head_mask(heads, head, start, size)
        q = query[at, start : start + size] * mask
        keys = text_kv[:, start : start + size]
        values = text_kv[:, width + start : width + start + size]
        grad = d_attn[at, start : start + size] * mask
        scores = jnp.where(valid[...] > 0, dot(keys, q, NT) * scale, -1e30)
        probs = softmax_down(scores)
        d_probs = dot(values, grad, NT)
        inner = jnp.sum(probs * d_probs, 0, keepdims=True)
        d_scores = (probs * (d_probs - inner)).astype(bf16)
        d_query[at, start : start + size] += (dot(d_scores, keys * mask, TN) * scale).astype(bf16)
        d_kv[:, start : start + size] += dot(d_scores, q) * scale
        d_kv[:, width + start : width + start + size] += dot(probs.astype(bf16), grad)

    by_heads(frames, patches, width, step, tick)
    g_q[...] = dot(normed[...], d_query[...], TN).astype(bf16)
    tick()
    d_normed[...] = dot(d_query[...], w_q[...], NT)
    tick()

    def add_to(at, value):
        gradient_out[at, :] = gradient[at, :] + value

    _unused, d_gain[...] = back_norm(rows, lambda at: first[at, :], gain[...], d_normed, add_to, None)


SLAB = 16


def slab_rows(start):
    return pl.ds(pl.multiple_of(start, SLAB), SLAB)


def slabs(patches, step, tick):
    count = patches // SLAB

    def one(b, _):
        step(pl.multiple_of(b * SLAB, SLAB))
        tick.inside(b, 0, count)
        return 0

    lax.fori_loop(0, count, one, 0)


def head_sums(products, spread):
    high = products.astype(bf16)
    low = (products - high.astype(f32)).astype(bf16)
    return dot(high, spread) + dot(low, spread)


def slab_probs(at, qkv, near, width, allowed, spread, frames, patches):
    scale = (width // HEADS) ** -0.5
    queries = [qkv[slab_rows(f * patches + at), :width].astype(f32) for f in range(frames)]
    products = jnp.concatenate(
        [queries[f] * near[f + o, slab_rows(at), :width].astype(f32) for o in range(5) for f in range(frames)], 0
    )
    every = head_sums(products, spread[...]) * scale
    every = jnp.where(allowed[...] > 0, every, -1e30)
    size = frames * SLAB
    scores = [every[o * size : (o + 1) * size] for o in range(5)]
    top = functools.reduce(jnp.maximum, scores)
    exps = [jnp.exp(s - top) for s in scores]
    share = 1.0 / functools.reduce(jnp.add, exps)
    return queries, [e * share for e in exps]


def slab_part(value, o, f, frames):
    n = (o * frames + f) * SLAB
    return value[n : n + SLAB]


def temporal_kernel(frames, patches, tick, qkv, near, allowed, spread, heads, second, mod, w_out, attn, branch, third):
    rows, width = second.shape

    def step(at):
        _queries, probs = slab_probs(at, qkv, near, width, allowed, spread, frames, patches)
        weights = dot(jnp.concatenate(probs, 0).astype(bf16), heads[...])
        for f in range(frames):
            total = jnp.zeros((SLAB, width), f32)
            for o in range(5):
                total += slab_part(weights, o, f, frames) * near[f + o, slab_rows(at), width:].astype(f32)
            attn[slab_rows(f * patches + at), :] = total.astype(bf16)

    slabs(patches, step, tick)
    product = dot(attn[...], w_out[...])
    branch[...] = product.astype(bf16)
    third[...] = second[...] + mod[5:6, :] * product


def temporal_back_kernel(wide, frames, patches, tick, gradient, qkv, near, allowed, spread, heads, mod, w_out, attn,
                         branch, g_out, d_qkv, d_gate, d_branch, d_attn, edges, arrived, sems):
    rows, width = gradient.shape
    scale = (width // HEADS) ** -0.5
    halo = Halo(Place(wide), sems)
    d_gate[...] = gate_back(rows, gradient, branch, mod[5:6, :], d_branch)
    tick()
    d_attn[...] = dot(d_branch[...], w_out[...], NT).astype(bf16)
    tick()

    def step(at):
        queries, probs = slab_probs(at, qkv, near, width, allowed, spread, frames, patches)
        grads = [d_attn[slab_rows(f * patches + at), :].astype(f32) for f in range(frames)]
        products = jnp.concatenate(
            [grads[f] * near[f + o, slab_rows(at), width:].astype(f32) for o in range(5) for f in range(frames)], 0
        )
        every = head_sums(products, spread[...])
        size = frames * SLAB
        d_probs = [every[o * size : (o + 1) * size] for o in range(5)]
        inner = functools.reduce(jnp.add, [p * d for p, d in zip(probs, d_probs)])
        d_scores = [p * (d - inner) * scale for p, d in zip(probs, d_probs)]
        wide_scores = dot(jnp.concatenate(d_scores, 0).astype(bf16), heads[...])
        wide_probs = dot(jnp.concatenate(probs, 0).astype(bf16), heads[...])
        for f in range(frames):
            total = jnp.zeros((SLAB, width), f32)
            for o in range(5):
                total += slab_part(wide_scores, o, f, frames) * near[f + o, slab_rows(at), :width].astype(f32)
            d_qkv[slab_rows(f * patches + at), :width] = total.astype(bf16)
        for g in range(frames + 4):
            pairs = [(g - f, f) for f in range(frames) if 0 <= g - f < 5]
            d_keys = functools.reduce(jnp.add, [slab_part(wide_scores, o, f, frames) * queries[f] for o, f in pairs])
            d_values = functools.reduce(jnp.add, [slab_part(wide_probs, o, f, frames) * grads[f] for o, f in pairs])
            if 2 <= g < frames + 2:
                here = slab_rows((g - 2) * patches + at)
                d_qkv[here, width : 2 * width] = d_keys.astype(bf16)
                d_qkv[here, 2 * width :] = d_values.astype(bf16)
            else:
                here = slab_rows((g if g < 2 else g - frames) * patches + at)
                edges[here, :width] = d_keys.astype(bf16)
                edges[here, width:] = d_values.astype(bf16)

    slabs(patches, step, tick)
    edge = 2 * patches
    sends = [halo.copy(0, edges.at[edge:, :], arrived.at[:edge, :]), halo.copy(1, edges.at[:edge, :], arrived.at[edge:, :])]
    for copy in sends:
        copy.start()
    tick()
    g_out[...] = dot(attn[...], d_branch[...], TN).astype(bf16)
    tick()
    tick.finish()
    for n, copy in enumerate(sends):
        copy.wait_recv()
        base = 0 if n == 0 else rows - edge

        def add(at, _, n=n, base=base):
            here = slab_rows(base + at.start)
            there = slab_rows(n * edge + at.start)
            d_qkv[here, width:] = (d_qkv[here, width:].astype(f32) + arrived[there, :].astype(f32)).astype(bf16)
            return 0

        row_blocks(edge, 16, add)
        tick()
    for copy in sends:
        copy.wait_send()


def temporal_rows_kernel(tick, gradient, second, mod, d_qkv, normed, w_qkv, gradient_out, g_qkv, d_mod, d_normed):
    rows, width = gradient.shape
    for c in range(0, 3 * width, width):
        g_qkv[:, c : c + width] = dot(normed[...], d_qkv[:, c : c + width], TN).astype(bf16)
        tick()
    d_normed[...] = dot(d_qkv[...], w_qkv[...], NT)
    tick()

    def add_to(at, value):
        gradient_out[at, :] = gradient[at, :] + value

    d_mod[0:1, :], d_mod[1:2, :] = back_norm(
        rows, lambda at: second[at, :], 1.0 + mod[4:5, :], d_normed, add_to, None)


def gelu_both(value):
    c = math.sqrt(2.0 / math.pi)
    square = value * value
    tanh = jnp.tanh(c * (value + 0.044715 * value * square))
    half = 0.5 * (1.0 + tanh)
    slope = half + 0.5 * value * (1.0 - tanh * tanh) * (c * (1.0 + 3 * 0.044715 * square))
    return value * half, slope


def mlp_kernel(tick, third, cotangent, mod, w_up, w_down, block_out, gradient, g_up, g_down, d_mod,
               normed, d_branch, hidden, d_act, act, d_hidden, branch, up, down, gu, gd, load, store):
    rows, width = third.shape
    count = w_up.shape[1] // width

    def loads(j):
        cols = pl.ds(j * width, width)
        return [pltpu.make_async_copy(w_up.at[:, cols], up.at[j % 2], load.at[0, j % 2]),
                pltpu.make_async_copy(w_down.at[cols, :], down.at[j % 2], load.at[1, j % 2])]

    def stores(j):
        cols = pl.ds(j * width, width)
        return (lambda: pltpu.make_async_copy(gu, g_up.at[:, cols], store.at[0]),
                lambda: pltpu.make_async_copy(gd, g_down.at[cols, :], store.at[1]))

    for copy in loads(0):
        copy.start()

    def norm(at, _):
        hat, _unused = normal(third[at, :])
        normed[at, :] = (hat * (1.0 + mod[7:8, :]) + mod[6:7, :]).astype(bf16)
        d_branch[at, :] = (mod[8:9, :] * cotangent[at, :].astype(f32)).astype(bf16)
        return 0

    row_blocks(rows, 16, norm, unroll=3)

    def activate(at, _):
        value, slope = gelu_both(hidden[at, :])
        act[at, :] = value.astype(bf16)
        d_hidden[at, :] = (slope * d_act[at, :]).astype(bf16)
        return 0

    d_normed = gradient
    for j in range(count):
        b = j % 2
        if j + 1 < count:
            for copy in loads(j + 1):
                copy.start()
        for copy in loads(j):
            copy.wait()
        hidden[...] = dot(normed[...], up[b])
        tick()
        d_act[...] = dot(d_branch[...], down[b], NT)
        tick()
        row_blocks(rows, 16, activate, unroll=3)
        if j > 0:
            for copy in stores(j - 1):
                copy().wait()
        gu[...] = dot(normed[...], d_hidden[...], TN).astype(bf16)
        stores(j)[0]().start()
        tick()
        gd[...] = dot(act[...], d_branch[...], TN).astype(bf16)
        stores(j)[1]().start()
        tick()
        if j == 0:
            branch[...] = dot(act[...], down[b])
            tick()
            d_normed[...] = dot(d_hidden[...], up[b], NT)
        else:
            branch[...] += dot(act[...], down[b])
            tick()
            d_normed[...] += dot(d_hidden[...], up[b], NT)
        tick()
    gate_row = mod[8:9, :]

    def last(at, total):
        value = branch[at, :]
        block_out[at, :] = (third[at, :] + gate_row * value).astype(bf16)
        return total + (cotangent[at, :].astype(f32) * value).reshape(2, 8, width).sum(0)

    d_mod[2:3, :] = jnp.sum(row_blocks(rows, 16, last, jnp.zeros((8, width), f32)), 0, keepdims=True)
    tick()

    def add_to(at, value):
        gradient[at, :] = cotangent[at, :].astype(f32) + value

    d_mod[0:1, :], d_mod[1:2, :] = back_norm(rows, lambda at: third[at, :], 1.0 + mod[7:8, :], d_normed, add_to, None)
    for copy in stores(count - 1):
        copy().wait()


class Place:
    def __init__(self, wide):
        self.wide = wide
        self.chips = wide // 2
        self.plane = lax.axis_index("narrow")
        self.index = lax.axis_index("wide")
        self.core = lax.rem(self.index, 2)
        chip = lax.div(self.index, 2)
        odd = lax.rem(chip, 2)
        half = lax.div(chip, 2)
        self.pos = (1 - odd) * half + odd * (self.chips - 1 - half)

    def chip(self, step):
        n = self.chips
        q = lax.rem(self.pos + (step % n), n)
        high = lax.div(q, n // 2)
        return (1 - high) * (2 * q) + high * (2 * (n - q) - 1)

    def member(self, step, core=None):
        return 2 * self.chip(step) + (self.core if core is None else core)

    def near(self):
        return ((self.plane, self.member(1)), (self.plane, self.member(-1)),
                (1 - self.plane, self.index), (self.plane, self.index + 1 - 2 * self.core))

    def beside(self):
        n = self.wide
        return ((self.plane, lax.rem(self.index + 1, n)), (self.plane, lax.rem(self.index + n - 1, n)))

def greet(devices):
    barrier = pltpu.get_barrier_semaphore()
    for device in devices:
        pl.semaphore_signal(barrier, inc=1, device_id=device, device_id_type=MESH)
    pl.semaphore_wait(barrier, len(devices))

def remote(src, dst, send, recv, device):
    return pltpu.make_async_remote_copy(src_ref=src, dst_ref=dst, send_sem=send, recv_sem=recv,
                                        device_id=device, device_id_type=MESH)

def lanes(start, size):
    return pl.ds(pl.multiple_of(start, 128), size)

def gather_scratch(wide, count):
    chips = wide // 2; reach = chips // 2
    return [DMA((count, 2, reach, 2)), DMA((count, 2, reach, 2)), DMA((count, chips - 1)), DMA((count, chips - 1)),
            DMA((count, chips)), DMA((count, chips)), DMA((count,))]

class Sends:
    def __init__(self):
        self.made = []

    def go(self, make, *args):
        make(*args).start()
        self.made.append((make, args))

    def close(self):
        for make, args in self.made:
            make(*args).wait_send()


def pieces_of(arrays):
    found = []
    for n, a in enumerate(arrays):
        rows, width = a.shape[-2:]
        row_step = 96 if rows % 96 == 0 else rows
        col_step = 1152 if width % 1152 == 0 else width
        found += [(n, r, row_step, c, col_step) for r in range(0, rows, row_step) for c in range(0, width, col_step)]
    return found


def gather_steps(place, own, full, sems, pieces):
    ring_s, ring_r, side_s, side_r, twin_s, twin_r, loc = sems
    count = len(pieces)
    chips = place.chips
    reach = chips // 2
    right, left, across, twin = range(4)
    y = place.plane
    sends = Sends()

    def here(i, part=None):
        n, r, rows, c, width = pieces[i]
        a = width // 3
        if part is None:
            return own[n].at[pl.ds(r, rows), pl.ds(c, width)]
        start, size = ((y * (width - a), a), (a, width - 2 * a), ((1 - y) * (width - a), a))[part]
        return own[n].at[pl.ds(r, rows), lanes(c + start, size)]

    def there(i, j, part=None):
        n, r, rows, c, width = pieces[i]
        a = width // 3
        if part is None:
            return full[n].at[j, pl.ds(r, rows), pl.ds(c, width)]
        start, size = ((y * (width - a), a), (a, width - 2 * a), ((1 - y) * (width - a), a))[part]
        return full[n].at[j, pl.ds(r, rows), lanes(c + start, size)]

    def ring(i, d, s, part, step):
        ref = there(i, place.member(step), part)
        return remote(
            here(i, part) if step == 0 else ref, ref, ring_s.at[i, d, s - 1, part], ring_r.at[i, d, s - 1, part],
            place.near()[d],
        )

    def side(i, slot, step, part):
        ref = there(i, place.member(step), part)
        return remote(ref, ref, side_s.at[i, slot], side_r.at[i, slot], place.near()[across])

    def core_copy(i, slot, step, core=None):
        ref = there(i, place.member(step, core))
        return remote(here(i) if step == 0 and core is None else ref, ref, twin_s.at[i, slot], twin_r.at[i, slot],
                      place.near()[twin])

    def local(i):
        return pltpu.make_async_copy(here(i), there(i, place.index), loc.at[i])

    for part in (0, 1):
        for i in range(count):
            for d in (0, 1):
                sends.go(ring, i, d, 1, part, 0)
    for i in range(count):
        local(i).start()
        sends.go(core_copy, i, chips - 1, 0)
    yield

    def shards(s):
        if s == reach:
            return [(2 * s - 2, s)]
        return [(2 * s - 2, -s), (2 * s - 1, s)]

    def finish(s, i):
        for slot, step in shards(s):
            side(i, slot, step, 2).wait_recv()
            sends.go(core_copy, i, slot, step)

    for s in range(1, reach + 1):
        for i in range(count):
            for part in (0, 1):
                for d in (0, 1):
                    if s == reach and part != d:
                        continue
                    step = -s if d == 0 else s
                    ring(i, d, s, part, step).wait_recv()
                    if s + 1 < reach or (s + 1 == reach and part == d):
                        sends.go(ring, i, d, s + 1, part, step)
                    if part == 0:
                        sends.go(side, i, 2 * s - 2 + (0 if s == reach else d), step, 0)
            if s > 1:
                finish(s - 1, i)
            yield
    for i in range(count):
        finish(reach, i)
        yield
    for i in range(count):
        for s in range(1, reach + 1):
            for slot, step in shards(s):
                core_copy(i, slot, step, 1 - place.core).wait_recv()
        core_copy(i, chips - 1, 0, 1 - place.core).wait_recv()
        local(i).wait()
    sends.close()


def scatter_scratch(wide, shapes):
    chips = wide // 2; reach = chips // 2; count = len(shapes)
    bufs = []
    for rows, width in shapes:
        bufs += [pltpu.VMEM((chips, rows, width), bf16),
                 pltpu.VMEM((chips, rows, width), bf16),
                 pltpu.VMEM((chips, rows, 2 * (width // 9)), bf16),
                 pltpu.VMEM((2, reach, rows, width - 2 * (width // 9)), bf16),
                 pltpu.VMEM((rows, width), bf16)]
    sems = [DMA((count, chips)), DMA((count, chips)), DMA((count, chips)), DMA((count, chips)), DMA((count, chips)),
            DMA((count, 2, reach)), DMA((count, 2, reach)), DMA((count,)), DMA((count,))]
    return bufs + sems

def scatter_steps(place, parts, outs, bufs, sems, pieces):
    load, twin_s, twin_r, side_s, side_r, ring_s, ring_r, last_s, last_r = sems
    count = len(pieces)
    chips = place.chips
    reach = chips // 2
    right, left, across, twin = range(4)
    y = place.plane
    other = 1 - place.core
    sends = Sends()
    go = sends.go
    own = [bufs[5*i] for i in range(count)]; tw = [bufs[5*i+1] for i in range(count)]
    sd = [bufs[5*i+2] for i in range(count)]; rg = [bufs[5*i+3] for i in range(count)]; lt = [bufs[5*i+4] for i in range(count)]
    steps = [reach] + [x for s in range(reach - 1, 0, -1) for x in (s, -s)] + [0]
    slot_of = {s: k for k, s in enumerate(steps)}
    slot_of[-reach] = slot_of[reach]
    w = [o.shape[-1] // 9 for o in own]
    def ringcols(i, d, s):
        base = y * 2 * w[i]
        if s > 1: return base, 7 * w[i]
        k = 4 if (d + i) % 2 == 0 else 3
        return (base, 4 * w[i]) if k == 4 else (base + 4 * w[i], 3 * w[i])
    def taken(i, j):
        n, r, rows, col, width = pieces[i]
        return parts[n].at[j, pl.ds(r, rows), pl.ds(col, width)]
    def twin_copy(i, k):
        return remote(taken(i, place.member(steps[k], other)), tw[i].at[k], twin_s.at[i, k], twin_r.at[i, k], place.near()[twin])
    def load_copy(i, k):
        return pltpu.make_async_copy(taken(i, place.member(steps[k])), own[i].at[k], load.at[i, k])
    def side(i, k):
        return remote(own[i].at[k, :, lanes((1 - y) * 7 * w[i], 2 * w[i])], sd[i].at[k], side_s.at[i, k], side_r.at[i, k], place.near()[across])
    def ring(i, d, s):
        start, size = ringcols(i, d, s)
        k = slot_of[(reach + 1 - s) if d == 0 else -(reach + 1 - s)]
        return remote(own[i].at[k, :, lanes(start, size)], rg[i].at[d, s-1, :, lanes(start - y * 2 * w[i], size)],
                      ring_s.at[i, d, s-1], ring_r.at[i, d, s-1], place.near()[d])
    def last(i):
        sl = lanes(y * 2 * w[i], 7 * w[i])
        return remote(own[i].at[slot_of[0], :, sl], lt[i].at[:, sl], last_s.at[i], last_r.at[i], place.near()[across])
    def add(i, dst_k, start, src, src_start, pieces):
        def one(t, _):
            to = lanes(start + t * w[i], w[i])
            value = own[i][dst_k, :, to].astype(f32)
            value += src[:, lanes(src_start + t * w[i], w[i])].astype(f32)
            own[i][dst_k, :, to] = value.astype(bf16)
            return 0
        lax.fori_loop(0, pieces, one, 0)
    for k in range(chips):
        for i in range(count):
            go(twin_copy, i, k); load_copy(i, k).start()
    yield
    def pair(k):
        for i in range(count):
            load_copy(i, k).wait(); twin_copy(i, k).wait_recv()
            add(i, k, 0, tw[i].at[k], 0, 9)
            go(side, i, k)
    def planes(k):
        for i in range(count):
            side(i, k).wait_recv()
            add(i, k, y * 7 * w[i], sd[i].at[k], 0, 2)
    def ring_in(i, d, s):
        ring(i, d, s).wait_recv()
        start, size = ringcols(i, d, s)
        t = reach - s
        add(i, slot_of[t if d == 0 else -t], start, rg[i].at[d, s-1], start - y * 2 * w[i], size // w[i])
    def need(s):
        far = reach + 1 - s
        return [slot_of[far]] if s == 1 or far == 0 else [slot_of[far], slot_of[-far]]
    done = 0
    for s in range(1, reach + 1):
        ready = need(s)
        while done < min(chips, max(ready) + 3):
            pair(done); done += 1
            yield
        for k in ready: planes(k)
        yield
        for i in range(count):
            for d in (0, 1):
                if s > 1: ring_in(i, d, s - 1)
                go(ring, i, d, s)
            yield
    while done < chips:
        pair(done); done += 1
    planes(slot_of[0])
    yield
    for i in range(count):
        for d in (0, 1): ring_in(i, d, reach)
        go(last, i)
        yield
    for i in range(count):
        last(i).wait_recv()
        k = slot_of[0]
        n, r, rows, col, width = pieces[i]
        mine, theirs = y * 7 * w[i], (1 - y) * 7 * w[i]
        for t in range(2):
            a, b = t * w[i] + mine, t * w[i] + theirs
            outs[n][pl.ds(r, rows), lanes(col + a, w[i])] = own[i][k, :, lanes(a, w[i])]
            outs[n][pl.ds(r, rows), lanes(col + b, w[i])] = lt[i][:, lanes(b, w[i])]
        for t in range(2, 7):
            at = pl.ds(t * w[i], w[i])
            outs[n][pl.ds(r, rows), pl.ds(col + t * w[i], w[i])] = (
                own[i][k, :, at].astype(f32) + lt[i][:, at].astype(f32)
            ).astype(bf16)
        yield
    sends.close()


def peers(place):
    n = place.wide
    return [(t, lax.rem(place.index + t, n)) for t in range(1, n)]


class Exchange:
    def __init__(self, place, parts, inbox, every, sems):
        self.place, self.parts, self.inbox, self.every = place, parts, inbox, every
        self.sems = sems
        self.sends = Sends()

    @staticmethod
    def scratch(wide, block, dtype):
        return [pltpu.VMEM((wide,) + block, dtype)] + [DMA((wide,))] * 4

    def device(self, t):
        return lax.rem(self.place.index + t, self.place.wide)

    def out(self, t):
        j = self.device(t)
        return remote(self.parts.at[j], self.inbox.at[t], self.sems[0].at[t], self.sems[1].at[t], (self.place.plane, j))

    def back(self, t, own):
        block = self.place.index if own else self.device(self.place.wide - t)
        ref = self.every.at[block]
        return remote(ref, ref, self.sems[2].at[t], self.sems[3].at[t], (self.place.plane, self.device(t)))

    def send(self):
        for t in range(1, self.place.wide):
            self.sends.go(self.out, t)

    def total(self):
        value = self.parts[self.place.index].astype(f32)
        for t in range(1, self.place.wide):
            self.out(t).wait_recv()
            value += self.inbox[t].astype(f32)
        return value

    def spread(self, value):
        self.every[self.place.index] = value.astype(self.every.dtype)
        for t in range(1, self.place.wide):
            self.sends.go(self.back, t, True)

    def arrive(self):
        for t in range(1, self.place.wide):
            self.back(t, False).wait_recv()

    def close(self):
        self.sends.close()


class Ring:
    def __init__(self, place, parts, every, scratch):
        self.place, self.parts, self.every = place, parts, every
        self.twin, self.inbox, self.outbox = scratch[:3]
        self.sems = scratch[3:]
        self.sends = Sends()

    @staticmethod
    def scratch(wide, block):
        chips = wide // 2
        reach = chips // 2
        return [pltpu.VMEM((chips,) + block, bf16), pltpu.VMEM((2, reach) + block, bf16),
                pltpu.VMEM((2, reach) + block, bf16), DMA((2,)), DMA((2, reach)), DMA((2, reach)),
                DMA((2,)), DMA((2, reach)), DMA((2, reach))]

    def go(self, make, *args):
        self.sends.go(make, *args)

    def reaches(self):
        half = self.place.chips // 2
        return (half, half - 1)

    def value(self, step):
        chip = self.place.chip(step)
        return self.parts[chip, self.place.core].astype(f32) + self.twin[chip].astype(f32)

    def pair(self):
        twin = self.place.near()[3]
        return remote(self.parts.at[:, 1 - self.place.core], self.twin, self.sems[0].at[0], self.sems[0].at[1], twin)

    def hop(self, d, s):
        return remote(self.outbox.at[d, s - 1], self.inbox.at[d, s - 1], self.sems[1].at[d, s - 1],
                      self.sems[2].at[d, s - 1], self.place.near()[d])

    def sum_steps(self):
        self.go(self.pair)
        yield
        self.pair().wait_recv()
        reaches = self.reaches()
        for s in range(1, max(reaches) + 1):
            for d in (0, 1):
                if s > reaches[d]:
                    continue
                step = reaches[d] + 1 - s
                total = self.value(step if d == 0 else -step)
                if s > 1:
                    self.hop(d, s - 1).wait_recv()
                    total += self.inbox[d, s - 2].astype(f32)
                self.outbox[d, s - 1] = total.astype(bf16)
                self.go(self.hop, d, s)
            yield
        self.total = self.value(0)
        for d in (0, 1):
            self.hop(d, reaches[d]).wait_recv()
            self.total += self.inbox[d, reaches[d] - 1].astype(f32)

    def spread(self, d, s, step):
        ref = self.every.at[self.place.chip(step), self.place.core]
        return remote(ref, ref, self.sems[4].at[d, s - 1], self.sems[5].at[d, s - 1], self.place.near()[d])

    def halves(self, own):
        ref = self.every.at[:, self.place.core if own else 1 - self.place.core]
        return remote(ref, ref, self.sems[3].at[0], self.sems[3].at[1], self.place.near()[3])

    def spread_steps(self, value):
        reaches = self.reaches()
        core = self.place.core
        self.every[self.place.chip(0), core] = value.astype(bf16)
        for d in (0, 1):
            self.go(self.spread, d, 1, 0)
        yield
        for s in range(1, max(reaches) + 1):
            for d in (0, 1):
                if s > reaches[d]:
                    continue
                step = -s if d == 0 else s
                self.spread(d, s, step).wait_recv()
                if s < reaches[d]:
                    self.go(self.spread, d, s + 1, step)
            yield
        self.go(self.halves, True)
        yield
        self.halves(False).wait_recv()

    def close(self):
        self.sends.close()


def by_chip(value):
    return value.reshape((value.shape[0] // 2, 2) + value.shape[1:])


def front_steps(modulation, text, prompt):
    modulation.send()
    yield from text.sum_steps()
    prompt[...] = text.total.astype(bf16)
    modulation.spread(modulation.total())
    yield
    modulation.arrive()
    modulation.close()
    text.close()


def text_steps(keys, prompt, kv_cols):
    def block(j, _):
        for core in (0, 1):
            keys.parts[j, core] = dot(kv_cols[j, core], prompt[...]).astype(bf16)
        return 0

    lax.fori_loop(0, keys.place.chips, block, 0)
    yield from keys.sum_steps()
    yield from keys.spread_steps(keys.total)
    keys.close()


def text_back_steps(keys, prompts, kv_rows, sems):
    place = keys.place

    def over(ref, k, own):
        half = ref.at[place.plane if own else 1 - place.plane]
        return remote(half, half, sems.at[k, 0], sems.at[k, 1], place.near()[2])

    yield from keys.sum_steps()
    yield from keys.spread_steps(keys.total)
    over(keys.both, 0, True).start()

    def block(j, total):
        for core in (0, 1):
            total += dot(kv_rows[j, core], keys.every[j, core])
        return total

    rows = lax.fori_loop(0, place.chips, block, jnp.zeros(prompts.every.shape[2:], f32))
    yield from prompts.spread_steps(rows)
    over(prompts.both, 1, True).start()
    yield
    for k, part in ((0, keys), (1, prompts)):
        over(part.both, k, False).wait_recv()
        over(part.both, k, True).wait_send()
        part.close()


def vector_steps(vectors, sems):
    place = vectors.place
    vectors.send()
    yield
    vectors.spread(vectors.total())
    yield
    vectors.arrive()

    def over(own):
        half = vectors.both.at[place.plane if own else 1 - place.plane]
        return remote(half, half, sems.at[0], sems.at[1], place.near()[2])

    over(True).start()
    yield
    over(False).wait_recv()
    over(True).wait_send()
    vectors.close()


def together(generators):
    running = list(generators)
    while running:
        for one in list(running):
            if next(one, running) is running:
                running.remove(one)
        yield


MOST_CHIPS = 8


class Gather:
    direct = False

    def __init__(self, wide, arrays):
        self.inputs = [(a, ANY) for a in arrays]
        self.outputs = [(((wide,) + a.shape, a.dtype), ANY) for a in arrays]
        self.arrays = arrays
        self.pieces = pieces_of(arrays)
        self.scratch = gather_scratch(wide, len(self.pieces))

    def steps(self, place, ins, outs, scratch):
        return gather_steps(place, ins, outs, scratch, self.pieces)

    def plain(self):
        return [lax.all_gather(a, "wide") for a in self.arrays]


class Scatter:
    direct = False

    def __init__(self, wide, arrays):
        self.arrays = arrays
        self.pieces = pieces_of(arrays)
        self.inputs = [(a, ANY) for a in arrays]
        self.outputs = [((a.shape[1:], bf16), VM) for a in arrays]
        self.scratch = scatter_scratch(wide, [(p[2], p[4]) for p in self.pieces])

    def steps(self, place, ins, outs, scratch):
        buffers = 5 * len(self.pieces)
        return scatter_steps(place, ins, outs, scratch[:buffers], scratch[buffers:], self.pieces)

    def plain(self):
        sums = [lax.psum_scatter(a.astype(f32), "wide") for a in self.arrays]
        return [lax.psum(a, "narrow").astype(bf16) for a in sums]


class Front:
    direct = True

    def __init__(self, wide, mod_parts, text_parts):
        self.inputs = [(mod_parts, VM), (by_chip(text_parts), VM)]
        self.outputs = [((mod_parts.shape, f32), VM), ((text_parts.shape[1:], bf16), VM)]
        self.scratch = Exchange.scratch(wide, mod_parts.shape[1:], f32) + Ring.scratch(wide, text_parts.shape[1:])

    def steps(self, place, ins, outs, scratch):
        modulation = Exchange(place, ins[0], scratch[0], outs[0], scratch[1:5])
        return front_steps(modulation, Ring(place, ins[1], None, scratch[5:]), outs[1])

    def plain(self):
        mod_parts, text_parts = (value for value, _ in self.inputs)
        rows = text_parts.reshape((-1,) + text_parts.shape[2:]).astype(f32)
        return [lax.psum(mod_parts, "wide"), lax.psum_scatter(rows, "wide").astype(bf16)]


class Text:
    direct = False

    def __init__(self, wide, prompt, kv_cols):
        block = (kv_cols.shape[1], prompt.shape[1])
        self.inputs = [(prompt, VM), (by_chip(kv_cols), VM)]
        self.outputs = [(((wide // 2, 2) + block, bf16), VM)]
        self.scratch = [pltpu.VMEM((wide // 2, 2) + block, bf16)] + Ring.scratch(wide, block)

    def steps(self, place, ins, outs, scratch):
        return text_steps(Ring(place, scratch[0], outs[0], scratch[1:]), ins[0], ins[1])

    def plain(self):
        prompt, kv_cols = (value for value, _ in self.inputs)
        product = lax.dot_general(kv_cols, prompt, (((3,), (0,)), ((), ())), preferred_element_type=f32)
        return [lax.psum(product, "wide").astype(bf16)]


class TextBack:
    direct = False

    def __init__(self, wide, kv_parts, kv_rows):
        chips = (wide // 2, 2)
        kv_block, block = kv_parts.shape[1:], (kv_rows.shape[1], kv_parts.shape[2])
        self.inputs = [(by_chip(kv_parts), VM), (by_chip(kv_rows), VM)]
        self.outputs = [(((2,) + chips + kv_block, bf16), VM), (((2,) + chips + block, bf16), VM)]
        self.scratch = Ring.scratch(wide, kv_block) + Ring.scratch(wide, block) + [DMA((2, 2))]

    def steps(self, place, ins, outs, scratch):
        keys = Ring(place, ins[0], outs[0].at[place.plane], scratch[:9])
        keys.both = outs[0]
        prompts = Ring(place, None, outs[1].at[place.plane], scratch[9:18])
        prompts.both = outs[1]
        return text_back_steps(keys, prompts, ins[1], scratch[18])

    def plain(self):
        kv_parts, kv_rows = (value for value, _ in self.inputs)
        every = lax.psum(kv_parts.astype(f32), "wide").astype(bf16)
        rows = jnp.einsum("jcrk,jckt->rt", kv_rows, every, preferred_element_type=f32).astype(bf16)
        return [lax.all_gather(every, "narrow"), lax.all_gather(by_chip(lax.all_gather(rows, "wide")), "narrow")]


class Vectors:
    direct = True

    def __init__(self, wide, parts):
        self.inputs = [(parts, VM)]
        self.outputs = [(((2,) + parts.shape, f32), VM)]
        self.scratch = Exchange.scratch(wide, parts.shape[1:], f32) + [DMA((2,))]

    def steps(self, place, ins, outs, scratch):
        vectors = Exchange(place, ins[0], scratch[0], outs[0].at[place.plane], scratch[1:5])
        vectors.both = outs[0]
        return vector_steps(vectors, scratch[5])

    def plain(self):
        return [lax.all_gather(lax.psum(self.inputs[0][0], "wide"), "narrow")]


class Pump:
    def __init__(self, steps, pace):
        self.steps, self.pace = steps, pace
        self.ended = False
        self.calls = self.rounds = 0

    def __call__(self):
        self.calls += 1
        for _ in range(self.pace):
            if not self.ended:
                self.ended = next(self.steps, self) is self
                self.rounds += 1

    def inside(self, index, low, high):
        for n in range(low, high):
            if not self.ended:
                pl.when(index == n)(lambda: self())

    def finish(self):
        while not self.ended:
            self()


def take(refs, *counts):
    found, at = [], 0
    for count in counts:
        found.append(refs[at : at + count])
        at += count
    return found


def fused_kernel(wide, talks, compute, counts, parts, pace, *refs):
    sizes = list(counts) + [n for p in parts for n in (len(p.inputs), len(p.outputs), len(p.scratch))]
    order = [0] + [3 + 3 * i for i in range(len(parts))]
    order += [1] + [4 + 3 * i for i in range(len(parts))]
    order += [2] + [5 + 3 * i for i in range(len(parts))]
    found = dict(zip(order, take(refs, *[sizes[i] for i in order])))
    if talks:
        place = Place(wide)
        greet(all_near(place) if any(p.direct for p in parts) else place.near() + place.beside())
        running = together(
            [p.steps(place, found[3 + 3 * i], found[4 + 3 * i], found[5 + 3 * i]) for i, p in enumerate(parts)]
        )
        pump = Pump(running, pace)
        pump()
    else:
        pump = Pump(iter(()), 1)
    if compute is not None:
        compute(pump, *found[0], *found[1], *found[2])
    pump.finish()


def fused(name, wide, compute, inputs, outputs, scratch, parts=(), pace=1, collective_id=None):
    if wide > 2 * MOST_CHIPS and parts:
        done = [[]] if compute is None else fused(
            name, wide, compute, inputs, outputs, scratch, collective_id=collective_id)
        return done + [part.plain() for part in parts]
    ins = inputs + [x for p in parts for x in p.inputs]
    outs = outputs + [x for p in parts for x in p.outputs]
    talks = collective_id is not None
    options = dict(collective_id=collective_id, has_side_effects=True) if talks else {}
    found = pl.pallas_call(
        functools.partial(fused_kernel, wide, talks, compute, (len(inputs), len(outputs), len(scratch)), parts, pace),
        out_shape=[jax.ShapeDtypeStruct(shape, dtype) for (shape, dtype), _ in outs],
        in_specs=[spec for _, spec in ins],
        out_specs=[spec for _, spec in outs],
        scratch_shapes=scratch + [x for p in parts for x in p.scratch],
        compiler_params=pltpu.CompilerParams(vmem_limit_bytes=LIMIT, **options),
        name=name,
    )(*[value for value, _ in ins])
    return take(found, len(outputs), *[len(p.outputs) for p in parts])


def on_chip(*values):
    return [(value, VM) for value in values]


def all_near(place):
    return [place.near()[2]] + [(place.plane, j) for t, j in peers(place)]


def spatial(wide, frames, patches, x, mod, heads, w_qkv, w_out, **rest):
    rows, width = x.shape
    return fused(
        "spatial", wide, functools.partial(spatial_kernel, frames, patches),
        on_chip(x, mod, heads, w_qkv, w_out),
        on_chip(*[((rows, n * width), d) for n, d in ((1, bf16), (3, bf16), (1, bf16), (1, bf16), (1, f32))]),
        [], **rest,
    )


def spatial_back(wide, frames, patches, gradient, x, mod, heads, w_qkv, w_out, normed, qkv, attn, branch, **rest):
    rows, width = x.shape
    V = pltpu.VMEM
    return fused(
        "spatial_back", wide, functools.partial(spatial_back_kernel, frames, patches),
        on_chip(gradient, x, mod, heads) + [(w_qkv, ANY)] + on_chip(w_out, normed, qkv, attn, branch),
        on_chip(((rows, width), bf16), ((width, 3 * width), bf16), ((width, width), bf16), ((3, width), f32)),
        [V((rows, width), bf16), V((rows, width), bf16), V((rows, 3 * width), bf16),
         V((rows, width), f32), V((2, width, width), bf16), DMA((2,))], **rest,
    )


def cross(wide, frames, patches, first, gain, mod, heads, valid, text_kv, w_q, w_out, w_tqkv, **rest):
    rows, width = first.shape
    return fused(
        "cross", wide, functools.partial(cross_kernel, wide, frames, patches),
        on_chip(first, gain, mod, heads, valid, text_kv, w_q, w_out, w_tqkv),
        on_chip(*[((rows, n * width), d) for n, d in ((1, bf16), (1, bf16), (1, bf16), (1, f32), (1, bf16), (3, bf16))])
        + on_chip(((frames + 4, patches, 2 * width), bf16)),
        [pltpu.VMEM((4 * patches, width), bf16), DMA((2, 2))], **rest,
    )


def cross_back(wide, frames, patches, gradient, first, gain, heads, valid, text_kv, w_q, w_out, normed, query, attn, **rest):
    rows, width = first.shape
    V = pltpu.VMEM
    return fused(
        "cross_back", wide, functools.partial(cross_back_kernel, frames, patches),
        on_chip(gradient, first, gain, heads, valid, text_kv, w_q, w_out, normed, query, attn),
        on_chip(((rows, width), f32), ((width, width), bf16), ((width, width), bf16), ((1, width), f32), (text_kv.shape, f32)),
        [V((rows, width), bf16)] * 3 + [V((rows, width), f32)], **rest,
    )


def temporal(wide, frames, patches, qkv, near, allowed, spread, heads, second, mod, w_out, **rest):
    rows, width = second.shape
    return fused(
        "temporal", wide, functools.partial(temporal_kernel, frames, patches),
        on_chip(qkv, near, allowed, spread, heads, second, mod, w_out),
        on_chip(((rows, width), bf16), ((rows, width), bf16), ((rows, width), f32)), [], **rest,
    )


def temporal_back(wide, frames, patches, gradient, qkv, near, allowed, spread, heads, mod, w_out, attn, branch, **rest):
    rows, width = gradient.shape
    V = pltpu.VMEM
    edges = (4 * patches, 2 * width)
    return fused(
        "temporal_back", wide, functools.partial(temporal_back_kernel, wide, frames, patches),
        on_chip(gradient, qkv, near, allowed, spread, heads, mod, w_out, attn, branch),
        on_chip(((width, width), bf16), ((rows, 3 * width), bf16), ((1, width), f32)),
        [V((rows, width), bf16)] * 2 + [V(edges, bf16)] * 2 + [DMA((2, 2))], **rest,
    )


def temporal_rows(wide, gradient, second, mod, d_qkv, normed, w_qkv, **rest):
    rows, width = gradient.shape
    return fused(
        "temporal_rows", wide, temporal_rows_kernel,
        on_chip(gradient, second, mod, d_qkv, normed, w_qkv),
        on_chip(((rows, width), f32), ((width, 3 * width), bf16), ((2, width), f32)),
        [pltpu.VMEM((rows, width), f32)], **rest,
    )


def mlp(wide, third, cotangent, mod, w_up, w_down, **rest):
    rows, width = third.shape
    V = pltpu.VMEM
    return fused(
        "mlp", wide, mlp_kernel,
        on_chip(third, cotangent, mod) + [(w_up, ANY), (w_down, ANY)],
        on_chip(((rows, width), bf16), ((rows, width), f32)) + [((w_up.shape, bf16), ANY), ((w_down.shape, bf16), ANY)]
        + on_chip(((3, width), f32)),
        [V((rows, width), bf16)] * 2 + [V((rows, width), f32)] * 2 + [V((rows, width), bf16)] * 2
        + [V((rows, width), f32)] + [V((2, width, width), bf16)] * 2 + [V((width, width), bf16)] * 2
        + [DMA((2, 2)), DMA((2,))], **rest,
    )


def time_embed(steps, model_width):
    half_width = model_width // 2
    freqs = jnp.exp(-math.log(10000.0) * jnp.arange(half_width, dtype=jnp.float32) / half_width)
    angles = steps.astype(jnp.float32)[:, None] * freqs[None, :]
    return jnp.concatenate([jnp.cos(angles), jnp.sin(angles)], -1)


def body(
    hidden,
    cotangent,
    text,
    timesteps,
    seg_ids,
    text_len,
    ada_weight,
    text_weight,
    kv_weight,
    qkv_weight,
    out_weight,
    cross_q_weight,
    cross_out_weight,
    temp_qkv_weight,
    temp_out_weight,
    up_weight,
    down_weight,
    cross_gain,
):
    frames, patches, width = hidden.shape[1:]
    rows = frames * patches
    text_count = text.shape[1]
    plane = lax.axis_index("narrow")
    position = lax.axis_index("wide")
    wide = lax.axis_size("wide")
    rows_model, rows_text = ada_weight.shape[0], text_weight.shape[0]
    head_of = jnp.arange(width) // (width // HEADS)
    heads = (head_of[None, :] == jnp.arange(HEADS)[:, None]).astype(bf16)
    spread = (head_of[:, None] == jnp.arange(HEADS)[None, :]).astype(bf16)

    def swap(value):
        return lax.ppermute(value, "narrow", [(0, 1), (1, 0)])

    def by_plane(own, other):
        return jnp.where(plane == 0, jnp.stack([own, other]), jnp.stack([other, own]))

    def whole(value):
        return value.reshape(-1, value.shape[-1])

    def blocks(value):
        return value.reshape(wide, -1, value.shape[-1])

    signal = jax.nn.silu(time_embed(timesteps, width)[0]).astype(bf16)
    signal_rows = lax.dynamic_slice_in_dim(signal, position * rows_model, rows_model)
    mod_part = dot(signal_rows[None, :], ada_weight)
    prompt_rows = lax.dynamic_slice_in_dim(text[0], position * rows_text, rows_text, 1)
    text_part = dot(text_weight, prompt_rows, (((0,), (1,)), ((), ())))
    kv_cols = blocks(kv_weight.T)
    kv_rows = kv_weight.reshape(rows_model, wide, -1).transpose(1, 0, 2)
    front = Front(wide, mod_part.reshape(wide, 1, -1), blocks(text_part.astype(bf16)))
    _none, (modulation, prompt), (full_qkv, full_out) = fused(
        "start", wide, None, [], [], [], parts=[front, Gather(wide, [qkv_weight, out_weight])], collective_id=0
    )
    full_qkv, full_out = whole(full_qkv), whole(full_out)
    mod = modulation.reshape(9, width)

    tokens = hidden[0].reshape(rows, width)
    (normed_a, qkv_a, attn_a, branch_a, first), (kv_all,), gathered = spatial(
        wide, frames, patches, tokens, mod, heads, full_qkv, full_out, collective_id=1, pace=2,
        parts=[
            Text(wide, prompt, kv_cols),
            Gather(wide, [cross_q_weight, cross_out_weight, temp_qkv_weight, temp_out_weight]),
        ],
    )
    full_cross_q, full_cross_out, full_temp_qkv, full_temp_out = map(whole, gathered)
    text_kv = whole(kv_all).T
    valid = (jnp.arange(text_count) < text_len[0]).astype(f32)[:, None]
    gain = cross_gain[None, :]
    (normed_c, query_c, attn_c, second, normed_t, qkv_t, near), (full_down,) = cross(
        wide, frames, patches, first, gain, mod, heads, valid, text_kv, full_cross_q, full_cross_out, full_temp_qkv,
        parts=[Gather(wide, [down_weight])], collective_id=2,
    )
    clip_pad = jnp.pad(seg_ids[0], 2, constant_values=-1)
    clip_local = lax.dynamic_slice_in_dim(clip_pad, position * frames, frames + 4)
    allowed = jnp.stack(
        [clip_local[offset : offset + frames] == clip_local[2 : frames + 2] for offset in range(5)]
    )
    allowed = jnp.broadcast_to(allowed[:, :, None, None], (5, frames, SLAB, HEADS)).reshape(-1, HEADS).astype(f32)
    (attn_t, branch_t, third), (full_up,) = temporal(
        wide, frames, patches, qkv_t, near, allowed, spread, heads, second, mod, full_temp_out,
        parts=[Gather(wide, [up_weight])], collective_id=3, pace=2,
    )

    upstream = cotangent[0].reshape(rows, width)
    ((block_out, gradient, grad_up, grad_down, d_mod_m),) = mlp(
        wide, third, upstream, mod, whole(full_up), whole(full_down)
    )

    (grad_temp_out, d_qkv_t, d_gate_t), (grad_up,) = temporal_back(
        wide, frames, patches, gradient, qkv_t, near, allowed, spread, heads, mod, full_temp_out, attn_t, branch_t,
        parts=[Scatter(wide, [blocks(grad_up)])], collective_id=4, pace=2,
    )
    (gradient, grad_temp_qkv, d_mod_t), (grad_down,) = temporal_rows(
        wide, gradient, second, mod, d_qkv_t, normed_t, full_temp_qkv,
        parts=[Scatter(wide, [blocks(grad_down)])], collective_id=5, pace=6,
    )
    (gradient, grad_cross_q, grad_cross_out, d_gain, d_text_kv), (grad_temp_qkv, grad_temp_out) = cross_back(
        wide, frames, patches, gradient, first, gain, heads, valid, text_kv,
        full_cross_q, full_cross_out, normed_c, query_c, attn_c,
        parts=[Scatter(wide, [blocks(grad_temp_qkv), blocks(grad_temp_out)])], collective_id=6, pace=2,
    )
    found = spatial_back(
        wide, frames, patches, gradient, tokens, mod, heads, full_qkv, full_out, normed_a, qkv_a, attn_a, branch_a,
        parts=[
            TextBack(wide, blocks(d_text_kv.T.astype(bf16)), kv_rows),
            Scatter(wide, [blocks(grad_cross_q), blocks(grad_cross_out)]),
        ],
        collective_id=7,
    )
    (grad_hidden, grad_qkv, grad_out, d_mod_a), (d_kv_both, d_prompt_both), (grad_cross_q, grad_cross_out) = found
    vectors = jnp.concatenate([d_mod_a, d_mod_t, d_gate_t, d_mod_m, d_gain], 0)
    _none, (vec_both,), (grad_qkv, grad_out) = fused(
        "end", wide, None, [], [], [], collective_id=8,
        parts=[Vectors(wide, vectors.reshape(wide, 1, -1)), Scatter(wide, [blocks(grad_qkv), blocks(grad_out)])],
    )
    vec_both = vec_both.reshape(2, 10, width)

    d_modulation = vec_both[:, :9].reshape(2, 9 * width)
    grad_gain = vec_both[0, 9] + vec_both[1, 9]
    both_signal = by_plane(signal_rows, swap(signal_rows)).astype(f32)
    grad_ada = (
        both_signal[0][:, None] * d_modulation[0][None, :] + both_signal[1][:, None] * d_modulation[1][None, :]
    )
    both_prompt = by_plane(prompt, swap(prompt))
    both_rows = by_plane(prompt_rows, swap(prompt_rows)).reshape(2 * text_count, -1)
    pairs = (((0, 2), (0, 2)), ((), ()))
    grad_kv = lax.dot_general(
        both_prompt, d_kv_both.reshape(2, 2 * width, text_count), pairs, preferred_element_type=f32
    )
    d_prompt = d_prompt_both.reshape(2, width, text_count).transpose(0, 2, 1).reshape(2 * text_count, width)
    grad_text = dot(both_rows, d_prompt, TN)
    shape = (1, frames, patches, width)
    return (
        block_out.reshape(shape),
        grad_hidden.reshape(shape),
        grad_ada,
        grad_text,
        grad_kv,
        grad_qkv.astype(f32),
        grad_out.astype(f32),
        grad_cross_q.astype(f32),
        grad_cross_out.astype(f32),
        grad_temp_qkv.astype(f32),
        grad_temp_out.astype(f32),
        grad_up.astype(f32),
        grad_down.astype(f32),
        grad_gain,
    )


def solution(mesh):
    return jax.shard_map(
        body,
        mesh=mesh,
        in_specs=(
            P("narrow", "wide", None, None),
            P("narrow", "wide", None, None),
            P("narrow", None, None),
            P("narrow"),
            P("narrow", None),
            P("narrow"),
            P("wide", None),
            P("wide", None),
            P("wide", None),
            P("wide", None),
            P("wide", None),
            P("wide", None),
            P("wide", None),
            P("wide", None),
            P("wide", None),
            P("wide", None),
            P("wide", None),
            P(),
        ),
        out_specs=(
            P("narrow", "wide", None, None),
            P("narrow", "wide", None, None),
            P("wide", None),
            P("wide", None),
            P("wide", None),
            P("wide", None),
            P("wide", None),
            P("wide", None),
            P("wide", None),
            P("wide", None),
            P("wide", None),
            P("wide", None),
            P("wide", None),
            P(),
        ),
        check_vma=False,
    )
```

```python
import functools
import math

import jax
import jax.numpy as jnp
from jax import lax
from jax.experimental import pallas as pl
from jax.experimental.pallas import tpu as pltpu
from jax.sharding import PartitionSpec as P

HEADS = 16
LIMIT = 62 * 2**20
MESH = pl.DeviceIdType.MESH
DMA = pltpu.SemaphoreType.DMA
VM = pl.BlockSpec(memory_space=pltpu.VMEM)
ANY = pl.BlockSpec(memory_space=pl.ANY)
f32, bf16 = jnp.float32, jnp.bfloat16
NN, NT, TN = (((1,), (0,)), ((), ())), (((1,), (1,)), ((), ())), (((0,), (0,)), ((), ()))


def dot(a, b, dims=NN):
    return lax.dot_general(a, b, dims, preferred_element_type=jnp.float32)


def row_blocks(count, size, step, carry=0, unroll=1):
    def one(r, value):
        return step(pl.ds(pl.multiple_of(r * size, size), size), value)
    return lax.fori_loop(0, count // size, one, carry, unroll=unroll)


def normal(value):
    centred = value - jnp.mean(value, -1, keepdims=True)
    scale = lax.rsqrt(jnp.mean(centred * centred, -1, keepdims=True) + 1e-06)
    return centred * scale, scale


def windows(width):
    size = width // HEADS
    found = []
    for head in range(HEADS):
        low, high = head * size, (head + 1) * size
        start = low // 128 * 128
        found.append((start, -(-high // 128) * 128 - start))
    return found


def head_mask(heads_ref, head, start, size):
    return heads_ref[head : head + 1, start : start + size]


def softmax_down(scores):
    exps = jnp.exp(scores - jnp.max(scores, 0, keepdims=True))
    return exps * (1.0 / jnp.sum(exps, 0, keepdims=True))


GROUPS = 4


def by_heads(frames, patches, width, step, tick):
    spans = list(enumerate(windows(width)))
    size = HEADS // GROUPS
    for group in range(GROUPS):

        def frame(f, _):
            rows = pl.ds(pl.multiple_of(f * patches, 16), patches)
            for head, (start, lanes_taken) in spans[group * size : (group + 1) * size]:
                step(rows, head, start, lanes_taken)
            tick.inside(f, 0, frames)
            return 0

        lax.fori_loop(0, frames, frame, 0)


def clear(ref):
    ref[...] = jnp.zeros_like(ref)


def spatial_attention(tick, qkv, heads, attn, frames, patches):
    width = attn.shape[-1]
    scale = (width // HEADS) ** -0.5
    clear(attn)

    def step(rows, head, start, size):
        mask = head_mask(heads, head, start, size)
        query = qkv[rows, start : start + size] * mask
        keys = qkv[rows, width + start : width + start + size]
        values = qkv[rows, 2 * width + start : 2 * width + start + size] * mask
        probs = softmax_down(dot(keys, query, NT) * scale).astype(bf16)
        attn[rows, start : start + size] += dot(probs, values, TN).astype(bf16)

    by_heads(frames, patches, width, step, tick)


def spatial_attention_back(tick, qkv, d_attn, heads, d_qkv, frames, patches):
    width = d_attn.shape[-1]
    scale = (width // HEADS) ** -0.5
    clear(d_qkv)

    def step(rows, head, start, size):
        mask = head_mask(heads, head, start, size)
        query = qkv[rows, start : start + size] * mask
        keys = qkv[rows, width + start : width + start + size]
        values = qkv[rows, 2 * width + start : 2 * width + start + size]
        grad = d_attn[rows, start : start + size] * mask
        probs = softmax_down(dot(keys, query, NT) * scale)
        d_probs = dot(values, grad, NT)
        inner = jnp.sum(probs * d_probs, 0, keepdims=True)
        d_scores = (probs * (d_probs - inner)).astype(bf16)
        d_qkv[rows, start : start + size] += (dot(d_scores, keys * mask, TN) * scale).astype(bf16)
        d_qkv[rows, width + start : width + start + size] += (dot(d_scores, query) * scale).astype(bf16)
        d_qkv[rows, 2 * width + start : 2 * width + start + size] += dot(probs.astype(bf16), grad).astype(bf16)

    by_heads(frames, patches, width, step, tick)


def fetch_columns(source, target, sems):
    width = source.shape[1] // 3

    def copy(n):
        cols = pl.ds(n * width, width)
        return pltpu.make_async_copy(source.at[:, cols], target.at[:, cols], sems.at[n])

    for n in range(3):
        copy(n).start()
    return lambda n: copy(n).wait()


def matmul(x, w, out, tick, arrive):
    width = w.shape[1] // 3
    for n in range(3):
        arrive(n)
        cols = slice(n * width, (n + 1) * width)
        out[:, cols] = dot(x[...], w[:, cols]).astype(out.dtype)
        tick()


def spatial_kernel(frames, patches, tick, x, mod, heads, w_all, w_out, normed, qkv, attn, branch, first, w_qkv, sems):
    rows = frames * patches
    arrive = fetch_columns(w_all, w_qkv, sems)

    def norm(at, _):
        hat, _unused = normal(x[at, :].astype(f32))
        normed[at, :] = (hat * (1.0 + mod[1:2, :]) + mod[0:1, :]).astype(bf16)
        return 0

    row_blocks(rows, 16, norm, unroll=3)
    tick()
    matmul(normed, w_qkv, qkv, tick, arrive)
    spatial_attention(tick, qkv, heads, attn, frames, patches)
    product = dot(attn[...], w_out[...])
    branch[...] = product.astype(bf16)
    first[...] = x[...].astype(f32) + mod[2:3, :] * product


def back_norm(tick, rows, hat_of, gain_row, d_normed, add_to, size=16):
    width = d_normed.shape[-1]

    def one(at, carry):
        total, weighted = carry
        hat, scale = normal(hat_of(at))
        grad = d_normed[at, :]
        total += grad.reshape(size // 8, 8, width).sum(0)
        product = grad * hat
        weighted += product.reshape(size // 8, 8, width).sum(0)
        d_hat = grad * gain_row
        d_value = scale * (d_hat - jnp.mean(d_hat, -1, keepdims=True)
                           - hat * jnp.mean(d_hat * hat, -1, keepdims=True))
        add_to(at, d_value)
        tick.along(at.start // size, rows // size, 4)
        return total, weighted

    zero = jnp.zeros((8, width), f32)
    total, weighted = row_blocks(rows, size, one, (zero, zero))
    return jnp.sum(total, 0, keepdims=True), jnp.sum(weighted, 0, keepdims=True)


def gate_back(rows, gradient, branch, gate_row, d_branch, size=16):
    width = gradient.shape[-1]

    def one(at, total):
        grad = gradient[at, :]
        d_branch[at, :] = (gate_row * grad).astype(bf16)
        return total + (grad * branch[at, :].astype(f32)).reshape(size // 8, 8, width).sum(0)

    total = row_blocks(rows, size, one, jnp.zeros((8, width), f32))
    return jnp.sum(total, 0, keepdims=True)


def rows_back(tick, normed, d_qkv, w_all, g_qkv, d_normed, part, load):
    width = d_normed.shape[1]

    def fetch(n):
        return pltpu.make_async_copy(w_all.at[:, pl.ds(n * width, width)], part.at[n % 2], load.at[n % 2])

    fetch(0).start()
    fetch(1).start()
    yield
    for n in range(3):
        cols = slice(n * width, (n + 1) * width)
        g_qkv[:, cols] = dot(normed[...], d_qkv[:, cols], TN).astype(bf16)
        tick()
        fetch(n).wait()
        product = dot(d_qkv[:, cols], part[n % 2], NT)
        if n == 0:
            d_normed[...] = product
            fetch(2).start()
        else:
            d_normed[...] += product
        tick()


def spatial_back_kernel(frames, patches, tick, gradient, x, mod, heads, w_qkv, w_out, normed, qkv, attn, branch,
                        d_hidden, g_qkv, g_out, d_mod, d_branch, d_attn, d_qkv, d_normed, part, load):
    rows, width = x.shape
    through = rows_back(tick, normed, d_qkv, w_qkv, g_qkv, d_normed, part, load)
    next(through)
    d_mod[2:3, :] = gate_back(rows, gradient, branch, mod[2:3, :], d_branch)
    tick()
    g_out[...] = dot(attn[...], d_branch[...], TN).astype(bf16)
    tick()
    d_attn[...] = dot(d_branch[...], w_out[...], NT).astype(bf16)
    tick()
    spatial_attention_back(tick, qkv, d_attn, heads, d_qkv, frames, patches)
    for _ in through:
        pass

    def add_to(at, value):
        d_hidden[at, :] = (gradient[at, :] + value).astype(bf16)

    d_mod[0:1, :], d_mod[1:2, :] = back_norm(tick, rows, lambda at: x[at, :].astype(f32), 1.0 + mod[1:2, :], d_normed, add_to)


class Halo:
    def __init__(self, place, sems):
        n, me = place.wide, place.index
        self.sems = sems
        self.beyond = ((place.plane, lax.rem(me + 1, n)), (place.plane, lax.rem(me + n - 1, n)))

    def copy(self, way, source, target):
        return remote(source, target, self.sems.at[0, way], self.sems.at[1, way], self.beyond[way])


def cross_kernel(wide, frames, patches, tick, first, gain, mod, heads, valid, text_kv, w_q, w_out, w_all,
                 normed, query, attn, second, normed_t, qkv_t, near, outer, sems, w_tqkv, load):
    rows, width = first.shape
    arrive = fetch_columns(w_all, w_tqkv, load)
    scale = (width // HEADS) ** -0.5
    halo = Halo(Place(wide), sems)

    def norm(at, _):
        hat, _unused = normal(first[at, :])
        normed[at, :] = (hat * gain[...]).astype(bf16)
        return 0

    row_blocks(rows, 16, norm, unroll=3)
    tick()
    query[...] = dot(normed[...], w_q[...]).astype(bf16)
    clear(attn)
    tick()

    def step(at, head, start, size):
        mask = head_mask(heads, head, start, size)
        q = query[at, start : start + size] * mask
        keys = text_kv[:, start : start + size]
        values = text_kv[:, width + start : width + start + size] * mask
        scores = jnp.where(valid[...] > 0, dot(keys, q, NT) * scale, -1e30)
        attn[at, start : start + size] += dot(softmax_down(scores).astype(bf16), values, TN).astype(bf16)

    by_heads(frames, patches, width, step, tick)
    second[...] = first[...] + dot(attn[...], w_out[...])
    tick()

    def norm_t(at, _):
        hat, _unused = normal(second[at, :])
        normed_t[at, :] = (hat * (1.0 + mod[4:5, :]) + mod[3:4, :]).astype(bf16)
        return 0

    row_blocks(rows, 16, norm_t, unroll=3)
    edge = 2 * patches
    sends = [halo.copy(0, normed_t.at[rows - edge :, :], outer.at[:edge, :]),
             halo.copy(1, normed_t.at[:edge, :], outer.at[edge:, :])]
    for copy in sends:
        copy.start()
    tick()
    matmul(normed_t, w_tqkv, qkv_t, tick, arrive)
    for f in range(frames):
        near[2 + f] = qkv_t[f * patches : (f + 1) * patches, width:]
    tick.finish()
    for n, copy in enumerate(sends):
        copy.wait_recv()
        side = outer[n * edge : (n + 1) * edge, :]
        for c in (width, 2 * width):
            found = dot(side, w_tqkv[:, c : c + width]).astype(bf16)
            for f in range(2):
                near[n * (frames + 2) + f, :, c - width : c] = found[f * patches : (f + 1) * patches]
            tick()
    for copy in sends:
        copy.wait_send()


def cross_back_kernel(frames, patches, tick, gradient, first, gain, heads, valid, text_kv, w_q, w_out, normed, query,
                      attn, gradient_out, g_q, g_out, d_gain, d_kv, d_branch, d_attn, d_query, d_normed):
    rows, width = first.shape
    scale = (width // HEADS) ** -0.5
    d_branch[...] = gradient[...].astype(bf16)
    clear(d_query)
    clear(d_kv)
    tick()
    g_out[...] = dot(attn[...], d_branch[...], TN).astype(bf16)
    tick()
    d_attn[...] = dot(d_branch[...], w_out[...], NT).astype(bf16)
    tick()

    def step(at, head, start, size):
        mask = head_mask(heads, head, start, size)
        q = query[at, start : start + size] * mask
        keys = text_kv[:, start : start + size]
        values = text_kv[:, width + start : width + start + size]
        grad = d_attn[at, start : start + size] * mask
        scores = jnp.where(valid[...] > 0, dot(keys, q, NT) * scale, -1e30)
        probs = softmax_down(scores)
        d_probs = dot(values, grad, NT)
        inner = jnp.sum(probs * d_probs, 0, keepdims=True)
        d_scores = (probs * (d_probs - inner)).astype(bf16)
        d_query[at, start : start + size] += (dot(d_scores, keys * mask, TN) * scale).astype(bf16)
        d_kv[:, start : start + size] += dot(d_scores, q) * scale
        d_kv[:, width + start : width + start + size] += dot(probs.astype(bf16), grad)

    by_heads(frames, patches, width, step, tick)
    g_q[...] = dot(normed[...], d_query[...], TN).astype(bf16)
    tick()
    d_normed[...] = dot(d_query[...], w_q[...], NT)
    tick()

    def add_to(at, value):
        gradient_out[at, :] = gradient[at, :] + value

    _unused, d_gain[...] = back_norm(tick, rows, lambda at: first[at, :], gain[...], d_normed, add_to)


SLAB = 16


def slab_rows(start):
    return pl.ds(pl.multiple_of(start, SLAB), SLAB)


def slabs(patches, step, tick):
    count = patches // SLAB

    def one(b, _):
        step(pl.multiple_of(b * SLAB, SLAB))
        tick.inside(b, 0, count)
        return 0

    lax.fori_loop(0, count, one, 0)


def head_sums(products, spread):
    high = products.astype(bf16)
    low = (products - high.astype(f32)).astype(bf16)
    return dot(high, spread) + dot(low, spread)


def slab_probs(at, qkv, near, width, allowed, spread, frames, patches):
    scale = (width // HEADS) ** -0.5
    queries = [qkv[slab_rows(f * patches + at), :width].astype(f32) for f in range(frames)]
    products = jnp.concatenate(
        [queries[f] * near[f + o, slab_rows(at), :width].astype(f32) for o in range(5) for f in range(frames)], 0
    )
    every = head_sums(products, spread[...]) * scale
    every = jnp.where(allowed[...] > 0, every, -1e30)
    size = frames * SLAB
    scores = [every[o * size : (o + 1) * size] for o in range(5)]
    top = functools.reduce(jnp.maximum, scores)
    exps = [jnp.exp(s - top) for s in scores]
    share = 1.0 / functools.reduce(jnp.add, exps)
    return queries, [e * share for e in exps]


def slab_part(value, o, f, frames):
    n = (o * frames + f) * SLAB
    return value[n : n + SLAB]


def temporal_kernel(frames, patches, tick, qkv, near, allowed, spread, heads, second, mod, w_out, attn, branch, third):
    rows, width = second.shape

    def step(at):
        _queries, probs = slab_probs(at, qkv, near, width, allowed, spread, frames, patches)
        weights = dot(jnp.concatenate(probs, 0).astype(bf16), heads[...])
        for f in range(frames):
            total = jnp.zeros((SLAB, width), f32)
            for o in range(5):
                total += slab_part(weights, o, f, frames) * near[f + o, slab_rows(at), width:].astype(f32)
            attn[slab_rows(f * patches + at), :] = total.astype(bf16)

    slabs(patches, step, tick)
    product = dot(attn[...], w_out[...])
    branch[...] = product.astype(bf16)
    third[...] = second[...] + mod[5:6, :] * product


def temporal_back_kernel(wide, frames, patches, tick, gradient, qkv, near, allowed, spread, heads, mod, w_out, attn,
                         branch, g_out, d_qkv, d_gate, d_branch, d_attn, edges, arrived, sems):
    rows, width = gradient.shape
    scale = (width // HEADS) ** -0.5
    halo = Halo(Place(wide), sems)
    d_gate[...] = gate_back(rows, gradient, branch, mod[5:6, :], d_branch)
    tick()
    d_attn[...] = dot(d_branch[...], w_out[...], NT).astype(bf16)
    tick()

    ends = [(way, f) for way in (0, 1) for f in (0, 1)]

    def shipped(way, f, at):
        source = edges.at[slab_rows(((1 - way) * 2 + f) * patches + at), :]
        target = arrived.at[slab_rows((2 * way + f) * patches + at), :]
        slab = lax.div(at, SLAB)
        return remote(source, target, sems.at[0, way, f, slab], sems.at[1, way, f, slab], halo.beyond[way])

    def step(at):
        queries, probs = slab_probs(at, qkv, near, width, allowed, spread, frames, patches)
        grads = [d_attn[slab_rows(f * patches + at), :].astype(f32) for f in range(frames)]
        products = jnp.concatenate(
            [grads[f] * near[f + o, slab_rows(at), width:].astype(f32) for o in range(5) for f in range(frames)], 0
        )
        every = head_sums(products, spread[...])
        size = frames * SLAB
        d_probs = [every[o * size : (o + 1) * size] for o in range(5)]
        inner = functools.reduce(jnp.add, [p * d for p, d in zip(probs, d_probs)])
        d_scores = [p * (d - inner) * scale for p, d in zip(probs, d_probs)]
        wide_scores = dot(jnp.concatenate(d_scores, 0).astype(bf16), heads[...])
        wide_probs = dot(jnp.concatenate(probs, 0).astype(bf16), heads[...])
        for f in range(frames):
            total = jnp.zeros((SLAB, width), f32)
            for o in range(5):
                total += slab_part(wide_scores, o, f, frames) * near[f + o, slab_rows(at), :width].astype(f32)
            d_qkv[slab_rows(f * patches + at), :width] = total.astype(bf16)
        for g in range(frames + 4):
            pairs = [(g - f, f) for f in range(frames) if 0 <= g - f < 5]
            d_keys = functools.reduce(jnp.add, [slab_part(wide_scores, o, f, frames) * queries[f] for o, f in pairs])
            d_values = functools.reduce(jnp.add, [slab_part(wide_probs, o, f, frames) * grads[f] for o, f in pairs])
            if 2 <= g < frames + 2:
                here = slab_rows((g - 2) * patches + at)
                d_qkv[here, width : 2 * width] = d_keys.astype(bf16)
                d_qkv[here, 2 * width :] = d_values.astype(bf16)
            else:
                here = slab_rows((g if g < 2 else g - frames) * patches + at)
                edges[here, :width] = d_keys.astype(bf16)
                edges[here, width:] = d_values.astype(bf16)
        for way, f in ends:
            shipped(way, f, at).start()

    slabs(patches, step, tick)
    tick()
    g_out[...] = dot(attn[...], d_branch[...], TN).astype(bf16)
    tick.finish()
    for way, f in ends:
        base = f * patches if way == 0 else (frames - 2 + f) * patches

        def add(b, _, way=way, f=f, base=base):
            at = b * SLAB
            shipped(way, f, at).wait_recv()
            here = slab_rows(base + at)
            there = slab_rows((2 * way + f) * patches + at)
            d_qkv[here, width:] = (d_qkv[here, width:].astype(f32) + arrived[there, :].astype(f32)).astype(bf16)
            return 0

        lax.fori_loop(0, patches // SLAB, add, 0)

    def close(b, _):
        for way, f in ends:
            shipped(way, f, b * SLAB).wait_send()
        return 0

    lax.fori_loop(0, patches // SLAB, close, 0)


def temporal_rows_kernel(tick, gradient, second, mod, d_qkv, normed, w_qkv, gradient_out, g_qkv, d_mod, d_normed, part, load):
    rows, width = gradient.shape
    for _ in rows_back(tick, normed, d_qkv, w_qkv, g_qkv, d_normed, part, load):
        pass

    def add_to(at, value):
        gradient_out[at, :] = gradient[at, :] + value

    d_mod[0:1, :], d_mod[1:2, :] = back_norm(tick, rows, lambda at: second[at, :], 1.0 + mod[4:5, :], d_normed, add_to)


def gelu_both(value):
    c = math.sqrt(2.0 / math.pi)
    square = value * value
    tanh = jnp.tanh(c * (value + 0.044715 * value * square))
    half = 0.5 * (1.0 + tanh)
    slope = half + 0.5 * value * (1.0 - tanh * tanh) * (c * (1.0 + 3 * 0.044715 * square))
    return value * half, slope


def mlp_kernel(tick, third, cotangent, mod, w_up, w_down, block_out, gradient, g_up, g_down, d_mod,
               normed, d_branch, hidden, d_act, act, d_hidden, branch, up, down, gu, gd, load, store):
    rows, width = third.shape
    count = w_up.shape[1] // width

    def loads(j):
        cols = pl.ds(j * width, width)
        return [pltpu.make_async_copy(w_up.at[:, cols], up.at[j % 2], load.at[0, j % 2]),
                pltpu.make_async_copy(w_down.at[cols, :], down.at[j % 2], load.at[1, j % 2])]

    def stores(j):
        cols = pl.ds(j * width, width)
        return (lambda: pltpu.make_async_copy(gu, g_up.at[:, cols], store.at[0]),
                lambda: pltpu.make_async_copy(gd, g_down.at[cols, :], store.at[1]))

    for copy in loads(0):
        copy.start()

    def norm(at, _):
        hat, _unused = normal(third[at, :])
        normed[at, :] = (hat * (1.0 + mod[7:8, :]) + mod[6:7, :]).astype(bf16)
        d_branch[at, :] = (mod[8:9, :] * cotangent[at, :].astype(f32)).astype(bf16)
        return 0

    row_blocks(rows, 16, norm, unroll=3)

    def activate(at, _):
        value, slope = gelu_both(hidden[at, :])
        act[at, :] = value.astype(bf16)
        d_hidden[at, :] = (slope * d_act[at, :]).astype(bf16)
        return 0

    d_normed = gradient
    for j in range(count):
        b = j % 2
        if j + 1 < count:
            for copy in loads(j + 1):
                copy.start()
        for copy in loads(j):
            copy.wait()
        hidden[...] = dot(normed[...], up[b])
        tick()
        d_act[...] = dot(d_branch[...], down[b], NT)
        tick()
        row_blocks(rows, 16, activate, unroll=3)
        if j > 0:
            stores(j - 1)[0]().wait()
        gu[...] = dot(normed[...], d_hidden[...], TN).astype(bf16)
        stores(j)[0]().start()
        tick()
        if j > 0:
            stores(j - 1)[1]().wait()
        gd[...] = dot(act[...], d_branch[...], TN).astype(bf16)
        stores(j)[1]().start()
        tick()
        if j == 0:
            branch[...] = dot(act[...], down[b])
            tick()
            d_normed[...] = dot(d_hidden[...], up[b], NT)
        else:
            branch[...] += dot(act[...], down[b])
            tick()
            d_normed[...] += dot(d_hidden[...], up[b], NT)
        tick()
    gate_row = mod[8:9, :]

    def last(at, total):
        value = branch[at, :]
        block_out[at, :] = (third[at, :] + gate_row * value).astype(bf16)
        return total + (cotangent[at, :].astype(f32) * value).reshape(2, 8, width).sum(0)

    d_mod[2:3, :] = jnp.sum(row_blocks(rows, 16, last, jnp.zeros((8, width), f32)), 0, keepdims=True)
    tick()

    def add_to(at, value):
        gradient[at, :] = cotangent[at, :].astype(f32) + value

    d_mod[0:1, :], d_mod[1:2, :] = back_norm(tick, rows, lambda at: third[at, :], 1.0 + mod[7:8, :], d_normed, add_to)
    for copy in stores(count - 1):
        copy().wait()


class Place:
    def __init__(self, wide):
        self.wide = wide
        self.chips = wide // 2
        self.plane = lax.axis_index("narrow")
        self.index = lax.axis_index("wide")
        self.core = lax.rem(self.index, 2)
        chip = lax.div(self.index, 2)
        odd = lax.rem(chip, 2)
        half = lax.div(chip, 2)
        self.pos = (1 - odd) * half + odd * (self.chips - 1 - half)
        self._chips = {}
        for step in range(self.chips) if self.chips <= 16 else ():
            self._chips[step] = self.chip(step)
        self._near = ((self.plane, self.member(1)), (self.plane, self.member(-1)),
                      (1 - self.plane, self.index), (self.plane, self.index + 1 - 2 * self.core))

    def chip(self, step):
        n = self.chips
        if step % n in self._chips:
            return self._chips[step % n]
        q = lax.rem(self.pos + (step % n), n)
        high = lax.div(q, n // 2)
        return (1 - high) * (2 * q) + high * (2 * (n - q) - 1)

    def member(self, step, core=None):
        return 2 * self.chip(step) + (self.core if core is None else core)

    def near(self):
        return self._near

    def beside(self):
        n = self.wide
        return ((self.plane, lax.rem(self.index + 1, n)), (self.plane, lax.rem(self.index + n - 1, n)))

def greet(devices):
    barrier = pltpu.get_barrier_semaphore()
    for device in devices:
        pl.semaphore_signal(barrier, inc=1, device_id=device, device_id_type=MESH)
    pl.semaphore_wait(barrier, len(devices))

def remote(src, dst, send, recv, device):
    return pltpu.make_async_remote_copy(src_ref=src, dst_ref=dst, send_sem=send, recv_sem=recv,
                                        device_id=device, device_id_type=MESH)

def lanes(start, size):
    return pl.ds(pl.multiple_of(start, 128), size)

def gather_scratch(wide, count):
    chips = wide // 2; reach = chips // 2
    return [DMA((count, 2, reach, 2)), DMA((count, 2, reach, 2)), DMA((count, chips - 1)), DMA((count, chips - 1)),
            DMA((count, chips)), DMA((count, chips)), DMA((count,))]

class Sends:
    def __init__(self):
        self.made = []

    def go(self, make, *args):
        make(*args).start()
        self.made.append((make, args))

    def close(self):
        for make, args in self.made:
            make(*args).wait_send()


def pieces_of(arrays):
    found = []
    for n, a in enumerate(arrays):
        rows, width = a.shape[-2:]
        row_step = 96 if rows % 96 == 0 else rows
        col_step = 1152 if width % 1152 == 0 else width
        found += [(n, r, row_step, c, col_step) for r in range(0, rows, row_step) for c in range(0, width, col_step)]
    return found


def gather_steps(place, own, full, sems, pieces):
    ring_s, ring_r, side_s, side_r, twin_s, twin_r, loc = sems
    count = len(pieces)
    chips = place.chips
    reach = chips // 2
    right, left, across, twin = range(4)
    y = place.plane
    sends = Sends()

    def here(i, part=None):
        n, r, rows, c, width = pieces[i]
        a = width // 3
        if part is None:
            return own[n].at[pl.ds(r, rows), pl.ds(c, width)]
        start, size = ((y * (width - a), a), (a, width - 2 * a), ((1 - y) * (width - a), a))[part]
        return own[n].at[pl.ds(r, rows), lanes(c + start, size)]

    def there(i, j, part=None):
        n, r, rows, c, width = pieces[i]
        a = width // 3
        if part is None:
            return full[n].at[j, pl.ds(r, rows), pl.ds(c, width)]
        start, size = ((y * (width - a), a), (a, width - 2 * a), ((1 - y) * (width - a), a))[part]
        return full[n].at[j, pl.ds(r, rows), lanes(c + start, size)]

    def ring(i, d, s, part, step):
        ref = there(i, place.member(step), part)
        return remote(
            here(i, part) if step == 0 else ref, ref, ring_s.at[i, d, s - 1, part], ring_r.at[i, d, s - 1, part],
            place.near()[d],
        )

    def side(i, slot, step, part):
        ref = there(i, place.member(step), part)
        return remote(ref, ref, side_s.at[i, slot], side_r.at[i, slot], place.near()[across])

    def core_copy(i, slot, step, core=None):
        ref = there(i, place.member(step, core))
        return remote(here(i) if step == 0 and core is None else ref, ref, twin_s.at[i, slot], twin_r.at[i, slot],
                      place.near()[twin])

    def local(i):
        return pltpu.make_async_copy(here(i), there(i, place.index), loc.at[i])

    for part in (0, 1):
        for i in range(count):
            for d in (0, 1):
                sends.go(ring, i, d, 1, part, 0)
    for i in range(count):
        local(i).start()
        sends.go(core_copy, i, chips - 1, 0)
    yield

    def shards(s):
        if s == reach:
            return [(2 * s - 2, s)]
        return [(2 * s - 2, -s), (2 * s - 1, s)]

    def finish(s, i):
        for slot, step in shards(s):
            side(i, slot, step, 2).wait_recv()
            sends.go(core_copy, i, slot, step)

    for s in range(1, reach + 1):
        for i in range(count):
            for part in (0, 1):
                for d in (0, 1):
                    if s == reach and part != d:
                        continue
                    step = -s if d == 0 else s
                    ring(i, d, s, part, step).wait_recv()
                    if s + 1 < reach or (s + 1 == reach and part == d):
                        sends.go(ring, i, d, s + 1, part, step)
                    if part == 0:
                        sends.go(side, i, 2 * s - 2 + (0 if s == reach else d), step, 0)
            if s > 1:
                finish(s - 1, i)
            yield
    for i in range(count):
        finish(reach, i)
        yield
    for i in range(count):
        for s in range(1, reach + 1):
            for slot, step in shards(s):
                core_copy(i, slot, step, 1 - place.core).wait_recv()
        core_copy(i, chips - 1, 0, 1 - place.core).wait_recv()
        local(i).wait()
    sends.close()


def scatter_scratch(wide, shapes):
    chips = wide // 2; reach = chips // 2; count = len(shapes)
    bufs = []
    for rows, width in shapes:
        bufs += [pltpu.VMEM((chips, rows, width), bf16),
                 pltpu.VMEM((chips, rows, width), bf16),
                 pltpu.VMEM((chips, rows, 2 * (width // 9)), bf16),
                 pltpu.VMEM((2, reach, rows, width - 2 * (width // 9)), bf16),
                 pltpu.VMEM((rows, width), bf16)]
    sems = [DMA((count, chips)), DMA((count, chips)), DMA((count, chips)), DMA((count, chips)), DMA((count, chips)),
            DMA((count, 2, reach)), DMA((count, 2, reach)), DMA((count,)), DMA((count,))]
    return bufs + sems

def scatter_steps(place, parts, outs, bufs, sems, pieces):
    load, twin_s, twin_r, side_s, side_r, ring_s, ring_r, last_s, last_r = sems
    count = len(pieces)
    chips = place.chips
    reach = chips // 2
    right, left, across, twin = range(4)
    y = place.plane
    other = 1 - place.core
    sends = Sends()
    go = sends.go
    own = [bufs[5*i] for i in range(count)]; tw = [bufs[5*i+1] for i in range(count)]
    sd = [bufs[5*i+2] for i in range(count)]; rg = [bufs[5*i+3] for i in range(count)]; lt = [bufs[5*i+4] for i in range(count)]
    steps = [reach] + [x for s in range(reach - 1, 0, -1) for x in (s, -s)] + [0]
    slot_of = {s: k for k, s in enumerate(steps)}
    slot_of[-reach] = slot_of[reach]
    w = [o.shape[-1] // 9 for o in own]
    def ringcols(i, d, s):
        base = y * 2 * w[i]
        if s > 1: return base, 7 * w[i]
        k = 4 if (d + i) % 2 == 0 else 3
        return (base, 4 * w[i]) if k == 4 else (base + 4 * w[i], 3 * w[i])
    def taken(i, j):
        n, r, rows, col, width = pieces[i]
        return parts[n].at[j, pl.ds(r, rows), pl.ds(col, width)]
    def twin_copy(i, k):
        return remote(taken(i, place.member(steps[k], other)), tw[i].at[k], twin_s.at[i, k], twin_r.at[i, k], place.near()[twin])
    def load_copy(i, k):
        return pltpu.make_async_copy(taken(i, place.member(steps[k])), own[i].at[k], load.at[i, k])
    def side(i, k):
        return remote(own[i].at[k, :, lanes((1 - y) * 7 * w[i], 2 * w[i])], sd[i].at[k], side_s.at[i, k], side_r.at[i, k], place.near()[across])
    def ring(i, d, s):
        start, size = ringcols(i, d, s)
        k = slot_of[(reach + 1 - s) if d == 0 else -(reach + 1 - s)]
        return remote(own[i].at[k, :, lanes(start, size)], rg[i].at[d, s-1, :, lanes(start - y * 2 * w[i], size)],
                      ring_s.at[i, d, s-1], ring_r.at[i, d, s-1], place.near()[d])
    def last(i):
        sl = lanes(y * 2 * w[i], 7 * w[i])
        return remote(own[i].at[slot_of[0], :, sl], lt[i].at[:, sl], last_s.at[i], last_r.at[i], place.near()[across])
    def add(i, dst_k, start, src, src_start, pieces):
        to, size = lanes(start, pieces * w[i]), pieces * w[i]
        own[i][dst_k, :, to] += src[:, lanes(src_start, size)]
    for k in range(chips):
        for i in range(count):
            go(twin_copy, i, k); load_copy(i, k).start()
    yield
    def pair(k):
        for i in range(count):
            load_copy(i, k).wait(); twin_copy(i, k).wait_recv()
            add(i, k, 0, tw[i].at[k], 0, 9)
            go(side, i, k)
    def planes(k):
        for i in range(count):
            side(i, k).wait_recv()
            add(i, k, y * 7 * w[i], sd[i].at[k], 0, 2)
    def ring_in(i, d, s):
        ring(i, d, s).wait_recv()
        start, size = ringcols(i, d, s)
        t = reach - s
        add(i, slot_of[t if d == 0 else -t], start, rg[i].at[d, s-1], start - y * 2 * w[i], size // w[i])
    def need(s):
        far = reach + 1 - s
        return [slot_of[far]] if s == 1 or far == 0 else [slot_of[far], slot_of[-far]]
    done = 0
    for s in range(1, reach + 1):
        ready = need(s)
        while done < min(chips, max(ready) + 3):
            pair(done); done += 1
        for k in ready: planes(k)
        yield
        for i in range(count):
            for d in (0, 1):
                if s > 1: ring_in(i, d, s - 1)
                go(ring, i, d, s)
            yield
    while done < chips:
        pair(done); done += 1
    planes(slot_of[0])
    yield
    for i in range(count):
        for d in (0, 1): ring_in(i, d, reach)
        go(last, i)
        yield
    for i in range(count):
        last(i).wait_recv()
        k = slot_of[0]
        mine, theirs = y * 7 * w[i], (1 - y) * 7 * w[i]
        for t in range(2):
            a, b = t * w[i] + mine, t * w[i] + theirs
            outs[i][:, lanes(a, w[i])] = own[i][k, :, lanes(a, w[i])]
            outs[i][:, lanes(b, w[i])] = lt[i][:, lanes(b, w[i])]
        for t in range(2, 7):
            at = pl.ds(t * w[i], w[i])
            outs[i][:, at] = own[i][k, :, at] + lt[i][:, at]
        yield
    sends.close()


def peers(place):
    n = place.wide
    return [(t, lax.rem(place.index + t, n)) for t in range(1, n)]


class Exchange:
    def __init__(self, place, parts, inbox, every, sems):
        self.place, self.parts, self.inbox, self.every = place, parts, inbox, every
        self.sems = sems
        self.sends = Sends()

    @staticmethod
    def scratch(wide, block, dtype):
        return [pltpu.VMEM((wide,) + block, dtype)] + [DMA((wide,))] * 4

    def device(self, t):
        return lax.rem(self.place.index + t, self.place.wide)

    def out(self, t):
        j = self.device(t)
        return remote(self.parts.at[j], self.inbox.at[t], self.sems[0].at[t], self.sems[1].at[t], (self.place.plane, j))

    def back(self, t, own):
        block = self.place.index if own else self.device(self.place.wide - t)
        ref = self.every.at[block]
        return remote(ref, ref, self.sems[2].at[t], self.sems[3].at[t], (self.place.plane, self.device(t)))

    def send(self):
        for t in range(1, self.place.wide):
            self.sends.go(self.out, t)

    def total(self):
        value = self.parts[self.place.index].astype(f32)
        for t in range(1, self.place.wide):
            self.out(t).wait_recv()
            value += self.inbox[t].astype(f32)
        return value

    def spread(self, value):
        self.every[self.place.index] = value.astype(self.every.dtype)
        for t in range(1, self.place.wide):
            self.sends.go(self.back, t, True)

    def arrive(self):
        for t in range(1, self.place.wide):
            self.back(t, False).wait_recv()

    def close(self):
        self.sends.close()


class Ring:
    def __init__(self, place, parts, every, scratch):
        self.place, self.parts, self.every = place, parts, every
        self.twin, self.inbox, self.outbox = scratch[:3]
        self.sems = scratch[3:]
        self.sends = Sends()

    @staticmethod
    def scratch(wide, block):
        chips = wide // 2
        reach = chips // 2
        return [pltpu.VMEM((chips,) + block, bf16), pltpu.VMEM((2, reach) + block, bf16),
                pltpu.VMEM((2, reach) + block, bf16), DMA((2,)), DMA((2, reach)), DMA((2, reach)),
                DMA((2,)), DMA((2, reach)), DMA((2, reach))]

    def go(self, make, *args):
        self.sends.go(make, *args)

    def reaches(self):
        half = self.place.chips // 2
        return (half, half - 1)

    def value(self, step):
        chip = self.place.chip(step)
        return self.parts[chip, self.place.core].astype(f32) + self.twin[chip].astype(f32)

    def pair(self):
        twin = self.place.near()[3]
        return remote(self.parts.at[:, 1 - self.place.core], self.twin, self.sems[0].at[0], self.sems[0].at[1], twin)

    def hop(self, d, s):
        return remote(self.outbox.at[d, s - 1], self.inbox.at[d, s - 1], self.sems[1].at[d, s - 1],
                      self.sems[2].at[d, s - 1], self.place.near()[d])

    def sum_steps(self):
        self.go(self.pair)
        yield
        self.pair().wait_recv()
        reaches = self.reaches()
        for s in range(1, max(reaches) + 1):
            for d in (0, 1):
                if s > reaches[d]:
                    continue
                step = reaches[d] + 1 - s
                total = self.value(step if d == 0 else -step)
                if s > 1:
                    self.hop(d, s - 1).wait_recv()
                    total += self.inbox[d, s - 2].astype(f32)
                self.outbox[d, s - 1] = total.astype(bf16)
                self.go(self.hop, d, s)
            yield
        self.total = self.value(0)
        for d in (0, 1):
            self.hop(d, reaches[d]).wait_recv()
            self.total += self.inbox[d, reaches[d] - 1].astype(f32)

    def spread(self, d, s, step):
        ref = self.every.at[self.place.chip(step), self.place.core]
        return remote(ref, ref, self.sems[4].at[d, s - 1], self.sems[5].at[d, s - 1], self.place.near()[d])

    def halves(self, own):
        ref = self.every.at[:, self.place.core if own else 1 - self.place.core]
        return remote(ref, ref, self.sems[3].at[0], self.sems[3].at[1], self.place.near()[3])

    def spread_steps(self, value):
        reaches = self.reaches()
        core = self.place.core
        self.every[self.place.chip(0), core] = value.astype(bf16)
        for d in (0, 1):
            self.go(self.spread, d, 1, 0)
        yield
        for s in range(1, max(reaches) + 1):
            for d in (0, 1):
                if s > reaches[d]:
                    continue
                step = -s if d == 0 else s
                self.spread(d, s, step).wait_recv()
                if s < reaches[d]:
                    self.go(self.spread, d, s + 1, step)
            yield
        self.go(self.halves, True)
        yield
        self.halves(False).wait_recv()

    def close(self):
        self.sends.close()


def by_chip(value):
    return value.reshape((value.shape[0] // 2, 2) + value.shape[1:])


def front_steps(modulation, text, prompt):
    modulation.send()
    yield from text.sum_steps()
    prompt[...] = text.total.astype(bf16)
    modulation.spread(modulation.total())
    yield
    modulation.arrive()
    modulation.close()
    text.close()


def text_steps(keys, prompt, kv_cols):
    def block(j, _):
        for core in (0, 1):
            keys.parts[j, core] = dot(kv_cols[j, core], prompt[...]).astype(bf16)
        return 0

    lax.fori_loop(0, keys.place.chips, block, 0)
    yield from keys.sum_steps()
    yield from keys.spread_steps(keys.total)
    keys.close()


def text_back_steps(keys, prompts, kv_rows, sems):
    place = keys.place

    def over(ref, k, own):
        half = ref.at[place.plane if own else 1 - place.plane]
        return remote(half, half, sems.at[k, 0], sems.at[k, 1], place.near()[2])

    yield from keys.sum_steps()
    yield from keys.spread_steps(keys.total)
    over(keys.both, 0, True).start()
    every = keys.every[...]
    yield from prompts.spread_steps(dot(kv_rows[...], every.reshape(-1, every.shape[-1])))
    over(prompts.both, 1, True).start()
    yield
    for k, part in ((0, keys), (1, prompts)):
        over(part.both, k, False).wait_recv()
        over(part.both, k, True).wait_send()
        part.close()


def vector_steps(vectors, sems):
    place = vectors.place
    vectors.send()
    yield
    vectors.spread(vectors.total())
    yield
    vectors.arrive()

    def over(own):
        half = vectors.both.at[place.plane if own else 1 - place.plane]
        return remote(half, half, sems.at[0], sems.at[1], place.near()[2])

    over(True).start()
    yield
    over(False).wait_recv()
    over(True).wait_send()
    vectors.close()


MOST_CHIPS = 8


class Gather:
    direct = False

    def __init__(self, wide, arrays, turns=1):
        self.turns = turns
        self.inputs = [(a, ANY) for a in arrays]
        self.outputs = [(((wide,) + a.shape, a.dtype), ANY) for a in arrays]
        self.arrays = arrays
        self.pieces = pieces_of(arrays)
        self.scratch = gather_scratch(wide, len(self.pieces))

    def steps(self, place, ins, outs, scratch):
        return gather_steps(place, ins, outs, scratch, self.pieces)

    def plain(self, _outputs):
        return [lax.all_gather(a, "wide") for a in self.arrays]


class Scatter:
    direct = False
    turns = 1

    def __init__(self, wide, pieces, turns=1):
        self.turns = turns
        arrays = []
        for piece in pieces:
            if not any(piece[0] is a for a in arrays):
                arrays.append(piece[0])
        self.given = pieces
        self.pieces = [([piece[0] is a for a in arrays].index(True),) + piece[1:] for piece in pieces]
        self.inputs = [(a, ANY) for a in arrays]
        self.outputs = [(((p[2], p[4]), bf16), VM) for p in pieces]
        self.scratch = scatter_scratch(wide, [(p[2], p[4]) for p in pieces])

    def steps(self, place, ins, outs, scratch):
        buffers = 5 * len(self.pieces)
        return scatter_steps(place, ins, outs, scratch[:buffers], scratch[buffers:], self.pieces)

    def plain(self, _outputs):
        return [plain_scatter(*piece) for piece in self.given]


def plain_scatter(array, row, rows, col, cols):
    part = array[:, row : row + rows, col : col + cols].astype(f32)
    return lax.psum(lax.psum_scatter(part, "wide"), "narrow").astype(bf16)


def pieces_in(array):
    return [(array,) + p[1:] for p in pieces_of([array])]


class Front:
    turns = 1
    direct = True

    def __init__(self, wide, mod_parts, text_parts):
        self.inputs = [(mod_parts, VM), (by_chip(text_parts), VM)]
        self.outputs = [((mod_parts.shape, f32), VM), ((text_parts.shape[1:], bf16), VM)]
        self.scratch = Exchange.scratch(wide, mod_parts.shape[1:], f32) + Ring.scratch(wide, text_parts.shape[1:])

    def steps(self, place, ins, outs, scratch):
        modulation = Exchange(place, ins[0], scratch[0], outs[0], scratch[1:5])
        return front_steps(modulation, Ring(place, ins[1], None, scratch[5:]), outs[1])

    def plain(self, _outputs):
        mod_parts, text_parts = (value for value, _ in self.inputs)
        rows = text_parts.reshape((-1,) + text_parts.shape[2:]).astype(f32)
        return [lax.psum(mod_parts, "wide"), lax.psum_scatter(rows, "wide").astype(bf16)]


class Text:
    turns = 1
    direct = False

    def __init__(self, wide, prompt, kv_cols):
        block = (kv_cols.shape[1], prompt.shape[1])
        self.inputs = [(prompt, VM), (by_chip(kv_cols), VM)]
        self.outputs = [(((wide // 2, 2) + block, bf16), VM)]
        self.scratch = [pltpu.VMEM((wide // 2, 2) + block, bf16)] + Ring.scratch(wide, block)

    def steps(self, place, ins, outs, scratch):
        return text_steps(Ring(place, scratch[0], outs[0], scratch[1:]), ins[0], ins[1])

    def plain(self, _outputs):
        prompt, kv_cols = (value for value, _ in self.inputs)
        product = lax.dot_general(kv_cols, prompt, (((3,), (0,)), ((), ())), preferred_element_type=f32)
        return [lax.psum(product, "wide").astype(bf16)]


class TextBack:
    turns = 1
    direct = False

    def __init__(self, wide, kv_parts, kv_rows):
        chips = (wide // 2, 2)
        kv_block, block = kv_parts.shape[1:], (kv_rows.shape[0], kv_parts.shape[2])
        self.inputs = [(by_chip(kv_parts), VM), (kv_rows, VM)]
        self.outputs = [(((2,) + chips + kv_block, bf16), VM), (((2,) + chips + block, bf16), VM)]
        self.scratch = Ring.scratch(wide, kv_block) + Ring.scratch(wide, block) + [DMA((2, 2))]

    def steps(self, place, ins, outs, scratch):
        keys = Ring(place, ins[0], outs[0].at[place.plane], scratch[:9])
        keys.both = outs[0]
        prompts = Ring(place, None, outs[1].at[place.plane], scratch[9:18])
        prompts.both = outs[1]
        return text_back_steps(keys, prompts, ins[1], scratch[18])

    def plain(self, _outputs):
        kv_parts, kv_rows = (value for value, _ in self.inputs)
        every = lax.psum(kv_parts.astype(f32), "wide").astype(bf16)
        rows = dot(kv_rows, every.reshape(-1, every.shape[-1])).astype(bf16)
        return [lax.all_gather(every, "narrow"), lax.all_gather(by_chip(lax.all_gather(rows, "wide")), "narrow")]


class Vectors:
    turns = 1
    direct = True

    def __init__(self, wide, parts):
        self.inputs = [(parts, VM)]
        self.outputs = [(((2,) + parts.shape, f32), VM)]
        self.scratch = Exchange.scratch(wide, parts.shape[1:], f32) + [DMA((2,))]

    def steps(self, place, ins, outs, scratch):
        vectors = Exchange(place, ins[0], scratch[0], outs[0].at[place.plane], scratch[1:5])
        vectors.both = outs[0]
        return vector_steps(vectors, scratch[5])

    def plain(self, _outputs):
        return [lax.all_gather(lax.psum(self.inputs[0][0], "wide"), "narrow")]


class Pump:
    def __init__(self, pace=1, every=1):
        self.running, self.pace, self.every = [], pace, every
        self.calls = 0

    def due(self):
        self.calls += 1
        return self.calls % self.every == 0

    def __call__(self):
        if self.due():
            self.move()

    def move(self):
        for _ in range(self.pace):
            for steps, turns in list(self.running):
                for _ in range(turns):
                    if next(steps, self) is self:
                        self.running.remove((steps, turns))
                        break

    def inside(self, index, low, high):
        for n in range(low, high):
            if self.due() and self.running:
                pl.when(index == n)(lambda: self.move())

    def along(self, index, count, calls):
        if count < 2 * calls:
            return
        for n in range(calls):
            if self.due() and self.running:
                pl.when(index == (n + 1) * count // (calls + 1))(lambda: self.move())

    def finish(self):
        while self.running:
            self.move()


def take(refs, *counts):
    found, at = [], 0
    for count in counts:
        found.append(refs[at : at + count])
        at += count
    return found


def fused_kernel(wide, talks, compute, counts, parts, pace, burst, every, *refs):
    sizes = list(counts) + [n for p in parts for n in (len(p.inputs), len(p.outputs), len(p.scratch))]
    order = [0] + [3 + 3 * i for i in range(len(parts))]
    order += [1] + [4 + 3 * i for i in range(len(parts))]
    order += [2] + [5 + 3 * i for i in range(len(parts))]
    found = dict(zip(order, take(refs, *[sizes[i] for i in order])))
    pump = Pump(pace, every)
    if talks:
        place = Place(wide)
        greet(all_near(place) if any(p.direct for p in parts) else place.near() + place.beside())
        for i, p in enumerate(parts):
            steps = p.steps(place, found[3 + 3 * i], found[4 + 3 * i], found[5 + 3 * i])
            pump.running.append((steps, p.turns))
        for _ in range(burst):
            pump.move()
    if compute is not None:
        compute(pump, *found[0], *found[1], *found[2])
    pump.finish()


def fused(name, wide, compute, inputs, outputs, scratch, parts=(), pace=1, collective_id=None, burst=1, every=1):
    if wide > 2 * MOST_CHIPS and parts:
        done = [[]] if compute is None else fused(
            name, wide, compute, inputs, outputs, scratch, collective_id=collective_id)
        return done + [part.plain(done[0]) for part in parts]
    ins = inputs + [x for p in parts for x in p.inputs]
    outs = outputs + [x for p in parts for x in p.outputs]
    talks = collective_id is not None
    options = dict(collective_id=collective_id, has_side_effects=True) if talks else {}
    found = pl.pallas_call(
        functools.partial(fused_kernel, wide, talks, compute, (len(inputs), len(outputs), len(scratch)), parts, pace, burst, every),
        out_shape=[jax.ShapeDtypeStruct(shape, dtype) for (shape, dtype), _ in outs],
        in_specs=[spec for _, spec in ins],
        out_specs=[spec for _, spec in outs],
        scratch_shapes=scratch + [x for p in parts for x in p.scratch],
        compiler_params=pltpu.CompilerParams(vmem_limit_bytes=LIMIT, **options),
        name=name,
    )(*[value for value, _ in ins])
    return take(found, len(outputs), *[len(p.outputs) for p in parts])


def on_chip(*values):
    return [(value, VM) for value in values]


def all_near(place):
    return [place.near()[2]] + [(place.plane, j) for t, j in peers(place)]


def spatial(wide, frames, patches, x, mod, heads, w_qkv, w_out, **rest):
    rows, width = x.shape
    return fused(
        "spatial", wide, functools.partial(spatial_kernel, frames, patches),
        on_chip(x, mod, heads) + [(w_qkv, ANY)] + on_chip(w_out),
        on_chip(*[((rows, n * width), d) for n, d in ((1, bf16), (3, bf16), (1, bf16), (1, bf16), (1, f32))]),
        [pltpu.VMEM(w_qkv.shape, bf16), DMA((3,))], **rest,
    )


def spatial_back(wide, frames, patches, gradient, x, mod, heads, w_qkv, w_out, normed, qkv, attn, branch, **rest):
    rows, width = x.shape
    V = pltpu.VMEM
    return fused(
        "spatial_back", wide, functools.partial(spatial_back_kernel, frames, patches),
        on_chip(gradient, x, mod, heads) + [(w_qkv, ANY)] + on_chip(w_out, normed, qkv, attn, branch),
        on_chip(((rows, width), bf16), ((width, 3 * width), bf16), ((width, width), bf16), ((3, width), f32)),
        [V((rows, width), bf16), V((rows, width), bf16), V((rows, 3 * width), bf16),
         V((rows, width), f32), V((2, width, width), bf16), DMA((2,))], **rest,
    )


def cross(wide, frames, patches, first, gain, mod, heads, valid, text_kv, w_q, w_out, w_tqkv, **rest):
    rows, width = first.shape
    return fused(
        "cross", wide, functools.partial(cross_kernel, wide, frames, patches),
        on_chip(first, gain, mod, heads, valid, text_kv, w_q, w_out) + [(w_tqkv, ANY)],
        on_chip(*[((rows, n * width), d) for n, d in ((1, bf16), (1, bf16), (1, bf16), (1, f32), (1, bf16), (3, bf16))])
        + on_chip(((frames + 4, patches, 2 * width), bf16)),
        [pltpu.VMEM((4 * patches, width), bf16), DMA((2, 2)), pltpu.VMEM(w_tqkv.shape, bf16), DMA((3,))], **rest,
    )


def cross_back(wide, frames, patches, gradient, first, gain, heads, valid, text_kv, w_q, w_out, normed, query, attn, **rest):
    rows, width = first.shape
    V = pltpu.VMEM
    return fused(
        "cross_back", wide, functools.partial(cross_back_kernel, frames, patches),
        on_chip(gradient, first, gain, heads, valid, text_kv, w_q, w_out, normed, query, attn),
        on_chip(((rows, width), f32), ((width, width), bf16), ((width, width), bf16), ((1, width), f32), (text_kv.shape, f32)),
        [V((rows, width), bf16)] * 3 + [V((rows, width), f32)], **rest,
    )


def temporal(wide, frames, patches, qkv, near, allowed, spread, heads, second, mod, w_out, **rest):
    rows, width = second.shape
    return fused(
        "temporal", wide, functools.partial(temporal_kernel, frames, patches),
        on_chip(qkv, near, allowed, spread, heads, second, mod, w_out),
        on_chip(((rows, width), bf16), ((rows, width), bf16), ((rows, width), f32)), [], **rest,
    )


def temporal_back(wide, frames, patches, gradient, qkv, near, allowed, spread, heads, mod, w_out, attn, branch, **rest):
    rows, width = gradient.shape
    V = pltpu.VMEM
    edges = (4 * patches, 2 * width)
    return fused(
        "temporal_back", wide, functools.partial(temporal_back_kernel, wide, frames, patches),
        on_chip(gradient, qkv, near, allowed, spread, heads, mod, w_out, attn, branch),
        on_chip(((width, width), bf16), ((rows, 3 * width), bf16), ((1, width), f32)),
        [V((rows, width), bf16)] * 2 + [V(edges, bf16)] * 2 + [DMA((2, 2, 2, patches // SLAB))], **rest,
    )


def temporal_rows(wide, gradient, second, mod, d_qkv, normed, w_qkv, **rest):
    rows, width = gradient.shape
    return fused(
        "temporal_rows", wide, temporal_rows_kernel,
        on_chip(gradient, second, mod, d_qkv, normed) + [(w_qkv, ANY)],
        on_chip(((rows, width), f32), ((width, 3 * width), bf16), ((2, width), f32)),
        [pltpu.VMEM((rows, width), f32), pltpu.VMEM((2, width, width), bf16), DMA((2,))], **rest,
    )


def mlp(wide, third, cotangent, mod, w_up, w_down, **rest):
    rows, width = third.shape
    V = pltpu.VMEM
    return fused(
        "mlp", wide, mlp_kernel,
        on_chip(third, cotangent, mod) + [(w_up, ANY), (w_down, ANY)],
        on_chip(((rows, width), bf16), ((rows, width), f32)) + [((w_up.shape, bf16), ANY), ((w_down.shape, bf16), ANY)]
        + on_chip(((3, width), f32)),
        [V((rows, width), bf16)] * 2 + [V((rows, width), f32)] * 2 + [V((rows, width), bf16)] * 2
        + [V((rows, width), f32)] + [V((2, width, width), bf16)] * 2 + [V((width, width), bf16)] * 2
        + [DMA((2, 2)), DMA((2,))], **rest,
    )


def time_embed(steps, model_width):
    half_width = model_width // 2
    freqs = jnp.exp(-math.log(10000.0) * jnp.arange(half_width, dtype=jnp.float32) / half_width)
    angles = steps.astype(jnp.float32)[:, None] * freqs[None, :]
    return jnp.concatenate([jnp.cos(angles), jnp.sin(angles)], -1)


def body(
    hidden,
    cotangent,
    text,
    timesteps,
    seg_ids,
    text_len,
    ada_weight,
    text_weight,
    kv_weight,
    qkv_weight,
    out_weight,
    cross_q_weight,
    cross_out_weight,
    temp_qkv_weight,
    temp_out_weight,
    up_weight,
    down_weight,
    cross_gain,
):
    frames, patches, width = hidden.shape[1:]
    rows = frames * patches
    text_count = text.shape[1]
    plane = lax.axis_index("narrow")
    position = lax.axis_index("wide")
    wide = lax.axis_size("wide")
    rows_model, rows_text = ada_weight.shape[0], text_weight.shape[0]
    head_of = jnp.arange(width) // (width // HEADS)
    heads = (head_of[None, :] == jnp.arange(HEADS)[:, None]).astype(bf16)
    spread = (head_of[:, None] == jnp.arange(HEADS)[None, :]).astype(bf16)

    def swap(value):
        return lax.ppermute(value, "narrow", [(0, 1), (1, 0)])

    def by_plane(own, other):
        return jnp.where(plane == 0, jnp.stack([own, other]), jnp.stack([other, own]))

    def whole(value):
        return value.reshape(-1, value.shape[-1])

    def joined(parts, axis):
        return jnp.concatenate([part.astype(f32) for part in parts], axis)

    def blocks(value):
        return value.reshape(wide, -1, value.shape[-1])

    signal = jax.nn.silu(time_embed(timesteps, width)[0]).astype(bf16)
    signal_rows = lax.dynamic_slice_in_dim(signal, position * rows_model, rows_model)
    mod_part = dot(signal_rows[None, :], ada_weight)
    prompt_rows = lax.dynamic_slice_in_dim(text[0], position * rows_text, rows_text, 1)
    text_part = dot(text_weight, prompt_rows, (((0,), (1,)), ((), ())))
    kv_cols = blocks(kv_weight.T)
    front = Front(wide, mod_part.reshape(wide, 1, -1), blocks(text_part.astype(bf16)))
    _none, (modulation, prompt), (full_qkv, full_out) = fused(
        "start", wide, None, [], [], [], parts=[front, Gather(wide, [qkv_weight, out_weight], turns=3)], collective_id=0
    )
    full_qkv, full_out = whole(full_qkv), whole(full_out)
    mod = modulation.reshape(9, width)

    tokens = hidden[0].reshape(rows, width)
    (normed_a, qkv_a, attn_a, branch_a, first), (kv_all,), gathered = spatial(
        wide, frames, patches, tokens, mod, heads, full_qkv, full_out, collective_id=1,
        parts=[
            Text(wide, prompt, kv_cols),
            Gather(wide, [cross_q_weight, cross_out_weight, temp_qkv_weight, temp_out_weight], turns=3),
        ],
    )
    full_cross_q, full_cross_out, full_temp_qkv, full_temp_out = map(whole, gathered)
    text_kv = whole(kv_all).T
    valid = (jnp.arange(text_count) < text_len[0]).astype(f32)[:, None]
    gain = cross_gain[None, :]
    (normed_c, query_c, attn_c, second, normed_t, qkv_t, near), (full_down,) = cross(
        wide, frames, patches, first, gain, mod, heads, valid, text_kv, full_cross_q, full_cross_out, full_temp_qkv,
        parts=[Gather(wide, [down_weight])], collective_id=2, every=2,
    )
    clip_pad = jnp.pad(seg_ids[0], 2, constant_values=-1)
    clip_local = lax.dynamic_slice_in_dim(clip_pad, position * frames, frames + 4)
    allowed = jnp.stack(
        [clip_local[offset : offset + frames] == clip_local[2 : frames + 2] for offset in range(5)]
    )
    allowed = jnp.broadcast_to(allowed[:, :, None, None], (5, frames, SLAB, HEADS)).reshape(-1, HEADS).astype(f32)
    (attn_t, branch_t, third), (full_up,) = temporal(
        wide, frames, patches, qkv_t, near, allowed, spread, heads, second, mod, full_temp_out,
        parts=[Gather(wide, [up_weight])], collective_id=3,
    )

    upstream = cotangent[0].reshape(rows, width)
    ((block_out, gradient, grad_up, grad_down, d_mod_m),) = mlp(
        wide, third, upstream, mod, whole(full_up), whole(full_down)
    )
    grad_up = grad_up.reshape(wide, rows_model, -1)

    (grad_temp_out, d_qkv_t, d_gate_t), up_parts = temporal_back(
        wide, frames, patches, gradient, qkv_t, near, allowed, spread, heads, mod, full_temp_out, attn_t, branch_t,
        parts=[Scatter(wide, pieces_in(grad_up))], collective_id=4,
    )
    (gradient, grad_temp_qkv, d_mod_t), down_parts = temporal_rows(
        wide, gradient, second, mod, d_qkv_t, normed_t, full_temp_qkv,
        parts=[Scatter(wide, pieces_in(blocks(grad_down)))], collective_id=5, pace=2, burst=3,
    )
    (gradient, grad_cross_q, grad_cross_out, d_gain, d_text_kv), (*temp_qkv_parts, grad_temp_out) = cross_back(
        wide, frames, patches, gradient, first, gain, heads, valid, text_kv,
        full_cross_q, full_cross_out, normed_c, query_c, attn_c,
        parts=[Scatter(wide, pieces_in(blocks(grad_temp_qkv)) + pieces_in(blocks(grad_temp_out)))], collective_id=6, burst=4,
    )
    found = spatial_back(
        wide, frames, patches, gradient, tokens, mod, heads, full_qkv, full_out, normed_a, qkv_a, attn_a, branch_a,
        parts=[
            TextBack(wide, blocks(d_text_kv.T.astype(bf16)), kv_weight),
            Scatter(wide, [p for g in (grad_cross_q, grad_cross_out) for p in pieces_in(blocks(g))]),
        ],
        collective_id=7,
    )
    (grad_hidden, grad_qkv, grad_out, d_mod_a), (d_kv_both, d_prompt_both), (grad_cross_q, grad_cross_out) = found
    vectors = jnp.concatenate([d_mod_a, d_mod_t, d_gate_t, d_mod_m, d_gain], 0)
    _none, (vec_both,), (*qkv_parts, grad_out) = fused(
        "end", wide, None, [], [], [], collective_id=8,
        parts=[
            Vectors(wide, vectors.reshape(wide, 1, -1)),
            Scatter(wide, pieces_in(blocks(grad_qkv)) + pieces_in(blocks(grad_out)), turns=2),
        ],
    )
    vec_both = vec_both.reshape(2, 10, width)

    d_modulation = vec_both[:, :9].reshape(2, 9 * width)
    grad_gain = vec_both[0, 9] + vec_both[1, 9]
    both_signal = by_plane(signal_rows, swap(signal_rows)).astype(f32)
    grad_ada = (
        both_signal[0][:, None] * d_modulation[0][None, :] + both_signal[1][:, None] * d_modulation[1][None, :]
    )
    both_prompt = by_plane(prompt, swap(prompt))
    both_rows = by_plane(prompt_rows, swap(prompt_rows)).reshape(2 * text_count, -1)
    pairs = (((0, 2), (0, 2)), ((), ()))
    grad_kv = lax.dot_general(
        both_prompt, d_kv_both.reshape(2, 2 * width, text_count), pairs, preferred_element_type=f32
    )
    d_prompt = d_prompt_both.reshape(2, width, text_count).transpose(0, 2, 1).reshape(2 * text_count, width)
    grad_text = dot(both_rows, d_prompt, TN)
    shape = (1, frames, patches, width)
    return (
        block_out.reshape(shape),
        grad_hidden.reshape(shape),
        grad_ada,
        grad_text,
        grad_kv,
        joined(qkv_parts, 1),
        grad_out.astype(f32),
        grad_cross_q.astype(f32),
        grad_cross_out.astype(f32),
        joined(temp_qkv_parts, 1),
        grad_temp_out.astype(f32),
        joined(up_parts, 1),
        joined(down_parts, 0),
        grad_gain,
    )


def solution(mesh):
    return jax.shard_map(
        body,
        mesh=mesh,
        in_specs=(
            P("narrow", "wide", None, None),
            P("narrow", "wide", None, None),
            P("narrow", None, None),
            P("narrow"),
            P("narrow", None),
            P("narrow"),
            P("wide", None),
            P("wide", None),
            P("wide", None),
            P("wide", None),
            P("wide", None),
            P("wide", None),
            P("wide", None),
            P("wide", None),
            P("wide", None),
            P("wide", None),
            P("wide", None),
            P(),
        ),
        out_specs=(
            P("narrow", "wide", None, None),
            P("narrow", "wide", None, None),
            P("wide", None),
            P("wide", None),
            P("wide", None),
            P("wide", None),
            P("wide", None),
            P("wide", None),
            P("wide", None),
            P("wide", None),
            P("wide", None),
            P("wide", None),
            P("wide", None),
            P(),
        ),
        check_vma=False,
    )
```

```python
import functools
import math

import jax
import jax.numpy as jnp
from jax import lax
from jax.experimental import pallas as pl
from jax.experimental.pallas import tpu as pltpu
from jax.sharding import PartitionSpec as P

HEADS = 16
LIMIT = 62 * 2**20
MESH = pl.DeviceIdType.MESH
DMA = pltpu.SemaphoreType.DMA
VM = pl.BlockSpec(memory_space=pltpu.VMEM)
ANY = pl.BlockSpec(memory_space=pl.ANY)
f32, bf16 = jnp.float32, jnp.bfloat16
NN, NT, TN = (((1,), (0,)), ((), ())), (((1,), (1,)), ((), ())), (((0,), (0,)), ((), ()))


def dot(a, b, dims=NN):
    return lax.dot_general(a, b, dims, preferred_element_type=jnp.float32)


def row_blocks(count, size, step, carry=0, unroll=1):
    def one(r, value):
        return step(pl.ds(pl.multiple_of(r * size, size), size), value)
    return lax.fori_loop(0, count // size, one, carry, unroll=unroll)


def normal(value):
    centred = value - jnp.mean(value, -1, keepdims=True)
    scale = lax.rsqrt(jnp.mean(centred * centred, -1, keepdims=True) + 1e-06)
    return centred * scale, scale


def windows(width):
    size = width // HEADS
    found = []
    for head in range(HEADS):
        low, high = head * size, (head + 1) * size
        start = low // 128 * 128
        found.append((start, -(-high // 128) * 128 - start))
    return found


def head_mask(heads_ref, head, start, size):
    return heads_ref[head : head + 1, start : start + size]


def softmax_down(scores):
    exps = jnp.exp(scores - jnp.max(scores, 0, keepdims=True))
    return exps * (1.0 / jnp.sum(exps, 0, keepdims=True))


GROUPS = 4


def by_heads(frames, patches, width, step, tick):
    spans = list(enumerate(windows(width)))
    size = HEADS // GROUPS
    for group in range(GROUPS):

        def frame(f, _):
            rows = pl.ds(pl.multiple_of(f * patches, 16), patches)
            for head, (start, lanes_taken) in spans[group * size : (group + 1) * size]:
                step(rows, head, start, lanes_taken)
            tick.inside(f, 0, frames)
            return 0

        lax.fori_loop(0, frames, frame, 0)


def clear(ref):
    ref[...] = jnp.zeros_like(ref)


def spatial_attention(tick, qkv, heads, attn, frames, patches):
    width = attn.shape[-1]
    scale = (width // HEADS) ** -0.5
    clear(attn)

    def step(rows, head, start, size):
        mask = head_mask(heads, head, start, size)
        query = qkv[rows, start : start + size] * mask
        keys = qkv[rows, width + start : width + start + size]
        values = qkv[rows, 2 * width + start : 2 * width + start + size] * mask
        probs = softmax_down(dot(keys, query, NT) * scale).astype(bf16)
        attn[rows, start : start + size] += dot(probs, values, TN).astype(bf16)

    by_heads(frames, patches, width, step, tick)


def spatial_attention_back(tick, qkv, d_attn, heads, d_qkv, frames, patches):
    width = d_attn.shape[-1]
    scale = (width // HEADS) ** -0.5
    clear(d_qkv)

    def step(rows, head, start, size):
        mask = head_mask(heads, head, start, size)
        query = qkv[rows, start : start + size] * mask
        keys = qkv[rows, width + start : width + start + size]
        values = qkv[rows, 2 * width + start : 2 * width + start + size]
        grad = d_attn[rows, start : start + size] * mask
        probs = softmax_down(dot(keys, query, NT) * scale)
        d_probs = dot(values, grad, NT)
        inner = jnp.sum(probs * d_probs, 0, keepdims=True)
        d_scores = (probs * (d_probs - inner)).astype(bf16)
        d_qkv[rows, start : start + size] += (dot(d_scores, keys * mask, TN) * scale).astype(bf16)
        d_qkv[rows, width + start : width + start + size] += (dot(d_scores, query) * scale).astype(bf16)
        d_qkv[rows, 2 * width + start : 2 * width + start + size] += dot(probs.astype(bf16), grad).astype(bf16)

    by_heads(frames, patches, width, step, tick)


def fetch_columns(source, target, sems):
    width = source.shape[1] // 3

    def copy(n):
        cols = pl.ds(n * width, width)
        return pltpu.make_async_copy(source.at[:, cols], target.at[:, cols], sems.at[n])

    for n in range(3):
        copy(n).start()
    return lambda n: copy(n).wait()


def matmul(x, w, out, tick, arrive):
    width = w.shape[1] // 3
    for n in range(3):
        arrive(n)
        cols = slice(n * width, (n + 1) * width)
        out[:, cols] = dot(x[...], w[:, cols]).astype(out.dtype)
        tick()


def spatial_kernel(frames, patches, tick, x, mod, heads, w_all, w_out, normed, qkv, attn, branch, first, w_qkv, sems):
    rows = frames * patches
    arrive = fetch_columns(w_all, w_qkv, sems)

    def norm(at, _):
        hat, _unused = normal(x[at, :].astype(f32))
        normed[at, :] = (hat * (1.0 + mod[1:2, :]) + mod[0:1, :]).astype(bf16)
        return 0

    row_blocks(rows, 16, norm, unroll=3)
    tick()
    matmul(normed, w_qkv, qkv, tick, arrive)
    spatial_attention(tick, qkv, heads, attn, frames, patches)
    product = dot(attn[...], w_out[...])
    branch[...] = product.astype(bf16)
    first[...] = x[...].astype(f32) + mod[2:3, :] * product


def back_norm(tick, rows, hat_of, gain_row, d_normed, add_to, size=16):
    width = d_normed.shape[-1]

    def one(at, carry):
        total, weighted = carry
        hat, scale = normal(hat_of(at))
        grad = d_normed[at, :]
        total += grad.reshape(size // 8, 8, width).sum(0)
        product = grad * hat
        weighted += product.reshape(size // 8, 8, width).sum(0)
        d_hat = grad * gain_row
        d_value = scale * (d_hat - jnp.mean(d_hat, -1, keepdims=True)
                           - hat * jnp.mean(d_hat * hat, -1, keepdims=True))
        add_to(at, d_value)
        tick.along(at.start // size, rows // size, 4)
        return total, weighted

    zero = jnp.zeros((8, width), f32)
    total, weighted = row_blocks(rows, size, one, (zero, zero))
    return jnp.sum(total, 0, keepdims=True), jnp.sum(weighted, 0, keepdims=True)


def gate_back(rows, gradient, branch, gate_row, d_branch, size=16):
    width = gradient.shape[-1]

    def one(at, total):
        grad = gradient[at, :]
        d_branch[at, :] = (gate_row * grad).astype(bf16)
        return total + (grad * branch[at, :].astype(f32)).reshape(size // 8, 8, width).sum(0)

    total = row_blocks(rows, size, one, jnp.zeros((8, width), f32))
    return jnp.sum(total, 0, keepdims=True)


def rows_back(tick, normed, d_qkv, w_all, g_qkv, d_normed, part, load):
    width = d_normed.shape[1]

    def fetch(n):
        return pltpu.make_async_copy(w_all.at[:, pl.ds(n * width, width)], part.at[n % 2], load.at[n % 2])

    fetch(0).start()
    fetch(1).start()
    yield
    for n in range(3):
        cols = slice(n * width, (n + 1) * width)
        g_qkv[:, cols] = dot(normed[...], d_qkv[:, cols], TN).astype(bf16)
        tick()
        fetch(n).wait()
        product = dot(d_qkv[:, cols], part[n % 2], NT)
        if n == 0:
            d_normed[...] = product
            fetch(2).start()
        else:
            d_normed[...] += product
        tick()


def spatial_back_kernel(frames, patches, tick, gradient, x, mod, heads, w_qkv, w_out, normed, qkv, attn, branch,
                        d_hidden, g_qkv, g_out, d_mod, d_branch, d_attn, d_qkv, d_normed, part, load):
    rows, width = x.shape
    through = rows_back(tick, normed, d_qkv, w_qkv, g_qkv, d_normed, part, load)
    next(through)
    d_mod[2:3, :] = gate_back(rows, gradient, branch, mod[2:3, :], d_branch)
    tick()
    g_out[...] = dot(attn[...], d_branch[...], TN).astype(bf16)
    tick()
    d_attn[...] = dot(d_branch[...], w_out[...], NT).astype(bf16)
    tick()
    spatial_attention_back(tick, qkv, d_attn, heads, d_qkv, frames, patches)
    for _ in through:
        pass

    def add_to(at, value):
        d_hidden[at, :] = (gradient[at, :] + value).astype(bf16)

    d_mod[0:1, :], d_mod[1:2, :] = back_norm(tick, rows, lambda at: x[at, :].astype(f32), 1.0 + mod[1:2, :], d_normed, add_to)


class Halo:
    def __init__(self, place, sems):
        n, me = place.wide, place.index
        self.sems = sems
        self.leaves = (me < n - 1, me > 0)
        self.comes = (me > 0, me < n - 1)
        self.beyond = ((place.plane, lax.rem(me + 1, n)), (place.plane, lax.rem(me + n - 1, n)))

    def copy(self, way, source, target):
        return remote(source, target, self.sems.at[0, way], self.sems.at[1, way], self.beyond[way])


def cross_kernel(wide, frames, patches, tick, first, gain, mod, heads, valid, text_kv, w_q, w_out, w_all,
                 normed, query, attn, second, normed_t, qkv_t, near, outer, sems, w_tqkv, load):
    rows, width = first.shape
    arrive = fetch_columns(w_all, w_tqkv, load)
    scale = (width // HEADS) ** -0.5
    halo = Halo(Place(wide), sems)

    def norm(at, _):
        hat, _unused = normal(first[at, :])
        normed[at, :] = (hat * gain[...]).astype(bf16)
        return 0

    row_blocks(rows, 16, norm, unroll=3)
    tick()
    query[...] = dot(normed[...], w_q[...]).astype(bf16)
    clear(attn)
    tick()

    def step(at, head, start, size):
        mask = head_mask(heads, head, start, size)
        q = query[at, start : start + size] * mask
        keys = text_kv[:, start : start + size]
        values = text_kv[:, width + start : width + start + size] * mask
        scores = jnp.where(valid[...] > 0, dot(keys, q, NT) * scale, -1e30)
        attn[at, start : start + size] += dot(softmax_down(scores).astype(bf16), values, TN).astype(bf16)

    by_heads(frames, patches, width, step, tick)
    second[...] = first[...] + dot(attn[...], w_out[...])
    tick()

    def norm_t(at, _):
        hat, _unused = normal(second[at, :])
        normed_t[at, :] = (hat * (1.0 + mod[4:5, :]) + mod[3:4, :]).astype(bf16)
        return 0

    row_blocks(rows, 16, norm_t, unroll=3)
    edge = 2 * patches
    sends = [halo.copy(0, normed_t.at[rows - edge :, :], outer.at[:edge, :]),
             halo.copy(1, normed_t.at[:edge, :], outer.at[edge:, :])]
    for n, copy in enumerate(sends):
        pl.when(halo.leaves[n])(copy.start)
    tick()
    matmul(normed_t, w_tqkv, qkv_t, tick, arrive)
    for f in range(frames):
        near[2 + f] = qkv_t[f * patches : (f + 1) * patches, width:]
    tick.finish()
    for n, copy in enumerate(sends):
        pl.when(halo.comes[n])(copy.wait_recv)

        @pl.when(jnp.logical_not(halo.comes[n]))
        def _(n=n):
            outer[n * edge : (n + 1) * edge, :] = jnp.zeros((edge, width), bf16)

        side = outer[n * edge : (n + 1) * edge, :]
        for c in (width, 2 * width):
            found = dot(side, w_tqkv[:, c : c + width]).astype(bf16)
            for f in range(2):
                near[n * (frames + 2) + f, :, c - width : c] = found[f * patches : (f + 1) * patches]
            tick()
    for n, copy in enumerate(sends):
        pl.when(halo.leaves[n])(copy.wait_send)


def cross_back_kernel(frames, patches, tick, gradient, first, gain, heads, valid, text_kv, w_q, w_out, normed, query,
                      attn, gradient_out, g_q, g_out, d_gain, d_kv, d_branch, d_attn, d_query, d_normed):
    rows, width = first.shape
    scale = (width // HEADS) ** -0.5
    d_branch[...] = gradient[...].astype(bf16)
    clear(d_query)
    clear(d_kv)
    tick()
    g_out[...] = dot(attn[...], d_branch[...], TN).astype(bf16)
    tick()
    d_attn[...] = dot(d_branch[...], w_out[...], NT).astype(bf16)
    tick()

    def step(at, head, start, size):
        mask = head_mask(heads, head, start, size)
        q = query[at, start : start + size] * mask
        keys = text_kv[:, start : start + size]
        values = text_kv[:, width + start : width + start + size]
        grad = d_attn[at, start : start + size] * mask
        scores = jnp.where(valid[...] > 0, dot(keys, q, NT) * scale, -1e30)
        probs = softmax_down(scores)
        d_probs = dot(values, grad, NT)
        inner = jnp.sum(probs * d_probs, 0, keepdims=True)
        d_scores = (probs * (d_probs - inner)).astype(bf16)
        d_query[at, start : start + size] += (dot(d_scores, keys * mask, TN) * scale).astype(bf16)
        d_kv[:, start : start + size] += dot(d_scores, q) * scale
        d_kv[:, width + start : width + start + size] += dot(probs.astype(bf16), grad)

    by_heads(frames, patches, width, step, tick)
    g_q[...] = dot(normed[...], d_query[...], TN).astype(bf16)
    tick()
    d_normed[...] = dot(d_query[...], w_q[...], NT)
    tick()

    def add_to(at, value):
        gradient_out[at, :] = gradient[at, :] + value

    _unused, d_gain[...] = back_norm(tick, rows, lambda at: first[at, :], gain[...], d_normed, add_to)


SLAB = 16


def slab_rows(start):
    return pl.ds(pl.multiple_of(start, SLAB), SLAB)


def slabs(patches, step, tick):
    count = patches // SLAB

    def one(b, _):
        step(pl.multiple_of(b * SLAB, SLAB))
        tick.inside(b, 0, count)
        return 0

    lax.fori_loop(0, count, one, 0)


def head_sums(products, spread):
    high = products.astype(bf16)
    low = (products - high.astype(f32)).astype(bf16)
    return dot(high, spread) + dot(low, spread)


def slab_probs(at, qkv, near, width, allowed, spread, frames, patches):
    scale = (width // HEADS) ** -0.5
    queries = [qkv[slab_rows(f * patches + at), :width].astype(f32) for f in range(frames)]
    products = jnp.concatenate(
        [queries[f] * near[f + o, slab_rows(at), :width].astype(f32) for o in range(5) for f in range(frames)], 0
    )
    every = head_sums(products, spread[...]) * scale
    every = jnp.where(allowed[...] > 0, every, -1e30)
    size = frames * SLAB
    scores = [every[o * size : (o + 1) * size] for o in range(5)]
    top = functools.reduce(jnp.maximum, scores)
    exps = [jnp.exp(s - top) for s in scores]
    share = 1.0 / functools.reduce(jnp.add, exps)
    return queries, [e * share for e in exps]


def slab_part(value, o, f, frames):
    n = (o * frames + f) * SLAB
    return value[n : n + SLAB]


def temporal_kernel(frames, patches, tick, qkv, near, allowed, spread, heads, second, mod, w_out, attn, branch, third):
    rows, width = second.shape

    def step(at):
        _queries, probs = slab_probs(at, qkv, near, width, allowed, spread, frames, patches)
        weights = dot(jnp.concatenate(probs, 0).astype(bf16), heads[...])
        for f in range(frames):
            total = jnp.zeros((SLAB, width), f32)
            for o in range(5):
                total += slab_part(weights, o, f, frames) * near[f + o, slab_rows(at), width:].astype(f32)
            attn[slab_rows(f * patches + at), :] = total.astype(bf16)

    slabs(patches, step, tick)
    product = dot(attn[...], w_out[...])
    branch[...] = product.astype(bf16)
    third[...] = second[...] + mod[5:6, :] * product


def temporal_back_kernel(wide, frames, patches, tick, gradient, qkv, near, allowed, spread, heads, mod, w_out, attn,
                         branch, g_out, d_qkv, d_gate, d_branch, d_attn, edges, arrived, sems):
    rows, width = gradient.shape
    scale = (width // HEADS) ** -0.5
    halo = Halo(Place(wide), sems)
    d_gate[...] = gate_back(rows, gradient, branch, mod[5:6, :], d_branch)
    tick()
    d_attn[...] = dot(d_branch[...], w_out[...], NT).astype(bf16)
    tick()

    def shipped(way, f, at):
        source = edges.at[slab_rows(((1 - way) * 2 + f) * patches + at), :]
        target = arrived.at[slab_rows((2 * way + f) * patches + at), :]
        slab = lax.div(at, SLAB)
        return remote(source, target, sems.at[0, way, f, slab], sems.at[1, way, f, slab], halo.beyond[way])

    def step(at):
        queries, probs = slab_probs(at, qkv, near, width, allowed, spread, frames, patches)
        grads = [d_attn[slab_rows(f * patches + at), :].astype(f32) for f in range(frames)]
        products = jnp.concatenate(
            [grads[f] * near[f + o, slab_rows(at), width:].astype(f32) for o in range(5) for f in range(frames)], 0
        )
        every = head_sums(products, spread[...])
        size = frames * SLAB
        d_probs = [every[o * size : (o + 1) * size] for o in range(5)]
        inner = functools.reduce(jnp.add, [p * d for p, d in zip(probs, d_probs)])
        d_scores = [p * (d - inner) * scale for p, d in zip(probs, d_probs)]
        wide_scores = dot(jnp.concatenate(d_scores, 0).astype(bf16), heads[...])
        wide_probs = dot(jnp.concatenate(probs, 0).astype(bf16), heads[...])
        for f in range(frames):
            total = jnp.zeros((SLAB, width), f32)
            for o in range(5):
                total += slab_part(wide_scores, o, f, frames) * near[f + o, slab_rows(at), :width].astype(f32)
            d_qkv[slab_rows(f * patches + at), :width] = total.astype(bf16)
        for g in range(frames + 4):
            pairs = [(g - f, f) for f in range(frames) if 0 <= g - f < 5]
            d_keys = functools.reduce(jnp.add, [slab_part(wide_scores, o, f, frames) * queries[f] for o, f in pairs])
            d_values = functools.reduce(jnp.add, [slab_part(wide_probs, o, f, frames) * grads[f] for o, f in pairs])
            if 2 <= g < frames + 2:
                here = slab_rows((g - 2) * patches + at)
                d_qkv[here, width : 2 * width] = d_keys.astype(bf16)
                d_qkv[here, 2 * width :] = d_values.astype(bf16)
            else:
                here = slab_rows((g if g < 2 else g - frames) * patches + at)
                edges[here, :width] = d_keys.astype(bf16)
                edges[here, width:] = d_values.astype(bf16)
        for way in (0, 1):

            @pl.when(halo.leaves[way])
            def _(way=way):
                for f in (0, 1):
                    shipped(way, f, at).start()

    slabs(patches, step, tick)
    tick()
    g_out[...] = dot(attn[...], d_branch[...], TN).astype(bf16)
    tick.finish()
    slab_count = patches // SLAB
    for way in (0, 1):

        @pl.when(halo.comes[way])
        def _(way=way):
            for f in (0, 1):
                base = f * patches if way == 0 else (frames - 2 + f) * patches

                def add(b, _, way=way, f=f, base=base):
                    at = b * SLAB
                    shipped(way, f, at).wait_recv()
                    here = slab_rows(base + at)
                    there = slab_rows((2 * way + f) * patches + at)
                    d_qkv[here, width:] = (
                        d_qkv[here, width:].astype(f32) + arrived[there, :].astype(f32)
                    ).astype(bf16)
                    return 0

                lax.fori_loop(0, slab_count, add, 0)

    for way in (0, 1):

        @pl.when(halo.leaves[way])
        def _(way=way):
            def close(b, _):
                for f in (0, 1):
                    shipped(way, f, b * SLAB).wait_send()
                return 0

            lax.fori_loop(0, slab_count, close, 0)


def temporal_rows_kernel(tick, gradient, second, mod, d_qkv, normed, w_qkv, gradient_out, g_qkv, d_mod, d_normed, part, load):
    rows, width = gradient.shape
    for _ in rows_back(tick, normed, d_qkv, w_qkv, g_qkv, d_normed, part, load):
        pass

    def add_to(at, value):
        gradient_out[at, :] = gradient[at, :] + value

    d_mod[0:1, :], d_mod[1:2, :] = back_norm(tick, rows, lambda at: second[at, :], 1.0 + mod[4:5, :], d_normed, add_to)


def gelu_both(value):
    c = math.sqrt(2.0 / math.pi)
    square = value * value
    tanh = jnp.tanh(c * (value + 0.044715 * value * square))
    half = 0.5 * (1.0 + tanh)
    slope = half + 0.5 * value * (1.0 - tanh * tanh) * (c * (1.0 + 3 * 0.044715 * square))
    return value * half, slope


def mlp_kernel(tick, third, cotangent, mod, w_up, w_down, block_out, gradient, g_up, g_down, d_mod,
               normed, d_branch, hidden, d_act, act, d_hidden, branch, up, down, gu, gd, load, store):
    rows, width = third.shape
    count = w_up.shape[1] // width

    def loads(j):
        cols = pl.ds(j * width, width)
        return [pltpu.make_async_copy(w_up.at[:, cols], up.at[j % 2], load.at[0, j % 2]),
                pltpu.make_async_copy(w_down.at[cols, :], down.at[j % 2], load.at[1, j % 2])]

    def stores(j):
        cols = pl.ds(j * width, width)
        return (lambda: pltpu.make_async_copy(gu, g_up.at[:, cols], store.at[0]),
                lambda: pltpu.make_async_copy(gd, g_down.at[cols, :], store.at[1]))

    for copy in loads(0):
        copy.start()

    def norm(at, _):
        hat, _unused = normal(third[at, :])
        normed[at, :] = (hat * (1.0 + mod[7:8, :]) + mod[6:7, :]).astype(bf16)
        d_branch[at, :] = (mod[8:9, :] * cotangent[at, :].astype(f32)).astype(bf16)
        return 0

    row_blocks(rows, 16, norm, unroll=3)

    def activate(at, _):
        value, slope = gelu_both(hidden[at, :])
        act[at, :] = value.astype(bf16)
        d_hidden[at, :] = (slope * d_act[at, :]).astype(bf16)
        return 0

    d_normed = gradient
    for j in range(count):
        b = j % 2
        if j + 1 < count:
            for copy in loads(j + 1):
                copy.start()
        for copy in loads(j):
            copy.wait()
        hidden[...] = dot(normed[...], up[b])
        tick()
        d_act[...] = dot(d_branch[...], down[b], NT)
        tick()
        row_blocks(rows, 16, activate, unroll=3)
        if j > 0:
            stores(j - 1)[0]().wait()
        gu[...] = dot(normed[...], d_hidden[...], TN).astype(bf16)
        stores(j)[0]().start()
        tick()
        if j > 0:
            stores(j - 1)[1]().wait()
        gd[...] = dot(act[...], d_branch[...], TN).astype(bf16)
        stores(j)[1]().start()
        tick()
        if j == 0:
            branch[...] = dot(act[...], down[b])
            tick()
            d_normed[...] = dot(d_hidden[...], up[b], NT)
        else:
            branch[...] += dot(act[...], down[b])
            tick()
            d_normed[...] += dot(d_hidden[...], up[b], NT)
        tick()
    gate_row = mod[8:9, :]

    def last(at, total):
        value = branch[at, :]
        block_out[at, :] = (third[at, :] + gate_row * value).astype(bf16)
        return total + (cotangent[at, :].astype(f32) * value).reshape(2, 8, width).sum(0)

    d_mod[2:3, :] = jnp.sum(row_blocks(rows, 16, last, jnp.zeros((8, width), f32)), 0, keepdims=True)
    tick()

    def add_to(at, value):
        gradient[at, :] = cotangent[at, :].astype(f32) + value

    d_mod[0:1, :], d_mod[1:2, :] = back_norm(tick, rows, lambda at: third[at, :], 1.0 + mod[7:8, :], d_normed, add_to)
    for copy in stores(count - 1):
        copy().wait()


class Place:
    def __init__(self, wide):
        self.wide = wide
        self.chips = wide // 2
        self.plane = lax.axis_index("narrow")
        self.index = lax.axis_index("wide")
        self.core = lax.rem(self.index, 2)
        chip = lax.div(self.index, 2)
        odd = lax.rem(chip, 2)
        half = lax.div(chip, 2)
        self.pos = (1 - odd) * half + odd * (self.chips - 1 - half)
        self._chips = {}
        for step in range(self.chips) if self.chips <= 16 else ():
            self._chips[step] = self.chip(step)
        self._near = ((self.plane, self.member(1)), (self.plane, self.member(-1)),
                      (1 - self.plane, self.index), (self.plane, self.index + 1 - 2 * self.core))

    def chip(self, step):
        n = self.chips
        if step % n in self._chips:
            return self._chips[step % n]
        q = lax.rem(self.pos + (step % n), n)
        high = lax.div(q, n // 2)
        return (1 - high) * (2 * q) + high * (2 * (n - q) - 1)

    def member(self, step, core=None):
        return 2 * self.chip(step) + (self.core if core is None else core)

    def near(self):
        return self._near

    def beside(self):
        n = self.wide
        return ((self.plane, lax.rem(self.index + 1, n)), (self.plane, lax.rem(self.index + n - 1, n)))

def greet(devices):
    barrier = pltpu.get_barrier_semaphore()
    for device in devices:
        pl.semaphore_signal(barrier, inc=1, device_id=device, device_id_type=MESH)
    pl.semaphore_wait(barrier, len(devices))

def remote(src, dst, send, recv, device):
    return pltpu.make_async_remote_copy(src_ref=src, dst_ref=dst, send_sem=send, recv_sem=recv,
                                        device_id=device, device_id_type=MESH)

def lanes(start, size):
    return pl.ds(pl.multiple_of(start, 128), size)

def gather_scratch(wide, count):
    chips = wide // 2; reach = chips // 2
    return [DMA((count, 2, reach, 2)), DMA((count, 2, reach, 2)), DMA((count, chips - 1)), DMA((count, chips - 1)),
            DMA((count, chips)), DMA((count, chips)), DMA((count,))]

class Sends:
    def __init__(self):
        self.made = []

    def go(self, make, *args):
        make(*args).start()
        self.made.append((make, args))

    def close(self):
        for make, args in self.made:
            make(*args).wait_send()


def pieces_of(arrays):
    found = []
    for n, a in enumerate(arrays):
        rows, width = a.shape[-2:]
        row_step = 96 if rows % 96 == 0 else rows
        col_step = 1152 if width % 1152 == 0 else width
        found += [(n, r, row_step, c, col_step) for r in range(0, rows, row_step) for c in range(0, width, col_step)]
    return found


def gather_steps(place, own, full, sems, pieces):
    ring_s, ring_r, side_s, side_r, twin_s, twin_r, loc = sems
    count = len(pieces)
    chips = place.chips
    reach = chips // 2
    right, left, across, twin = range(4)
    y = place.plane
    sends = Sends()

    def here(i, part=None):
        n, r, rows, c, width = pieces[i]
        a = width // 3
        if part is None:
            return own[n].at[pl.ds(r, rows), pl.ds(c, width)]
        start, size = ((y * (width - a), a), (a, width - 2 * a), ((1 - y) * (width - a), a))[part]
        return own[n].at[pl.ds(r, rows), lanes(c + start, size)]

    def there(i, j, part=None):
        n, r, rows, c, width = pieces[i]
        a = width // 3
        if part is None:
            return full[n].at[j, pl.ds(r, rows), pl.ds(c, width)]
        start, size = ((y * (width - a), a), (a, width - 2 * a), ((1 - y) * (width - a), a))[part]
        return full[n].at[j, pl.ds(r, rows), lanes(c + start, size)]

    def ring(i, d, s, part, step):
        ref = there(i, place.member(step), part)
        return remote(
            here(i, part) if step == 0 else ref, ref, ring_s.at[i, d, s - 1, part], ring_r.at[i, d, s - 1, part],
            place.near()[d],
        )

    def side(i, slot, step, part):
        ref = there(i, place.member(step), part)
        return remote(ref, ref, side_s.at[i, slot], side_r.at[i, slot], place.near()[across])

    def core_copy(i, slot, step, core=None):
        ref = there(i, place.member(step, core))
        return remote(here(i) if step == 0 and core is None else ref, ref, twin_s.at[i, slot], twin_r.at[i, slot],
                      place.near()[twin])

    def local(i):
        return pltpu.make_async_copy(here(i), there(i, place.index), loc.at[i])

    for part in (0, 1):
        for i in range(count):
            for d in (0, 1):
                sends.go(ring, i, d, 1, part, 0)
    for i in range(count):
        local(i).start()
        sends.go(core_copy, i, chips - 1, 0)
    yield

    def shards(s):
        if s == reach:
            return [(2 * s - 2, s)]
        return [(2 * s - 2, -s), (2 * s - 1, s)]

    def finish(s, i):
        for slot, step in shards(s):
            side(i, slot, step, 2).wait_recv()
            sends.go(core_copy, i, slot, step)

    for s in range(1, reach + 1):
        for i in range(count):
            for part in (0, 1):
                for d in (0, 1):
                    if s == reach and part != d:
                        continue
                    step = -s if d == 0 else s
                    ring(i, d, s, part, step).wait_recv()
                    if s + 1 < reach or (s + 1 == reach and part == d):
                        sends.go(ring, i, d, s + 1, part, step)
                    if part == 0:
                        sends.go(side, i, 2 * s - 2 + (0 if s == reach else d), step, 0)
            if s > 1:
                finish(s - 1, i)
            yield
    for i in range(count):
        finish(reach, i)
        yield
    for i in range(count):
        for s in range(1, reach + 1):
            for slot, step in shards(s):
                core_copy(i, slot, step, 1 - place.core).wait_recv()
        core_copy(i, chips - 1, 0, 1 - place.core).wait_recv()
        local(i).wait()
    sends.close()


def scatter_scratch(wide, shapes):
    chips = wide // 2; reach = chips // 2; count = len(shapes)
    bufs = []
    for rows, width in shapes:
        bufs += [pltpu.VMEM((chips, rows, width), bf16),
                 pltpu.VMEM((chips, rows, width), bf16),
                 pltpu.VMEM((chips, rows, 2 * (width // 9)), bf16),
                 pltpu.VMEM((2, reach, rows, width - 2 * (width // 9)), bf16),
                 pltpu.VMEM((rows, width), bf16)]
    sems = [DMA((count, chips)), DMA((count, chips)), DMA((count, chips)), DMA((count, chips)), DMA((count, chips)),
            DMA((count, 2, reach)), DMA((count, 2, reach)), DMA((count,)), DMA((count,))]
    return bufs + sems

def scatter_steps(place, parts, outs, bufs, sems, pieces):
    load, twin_s, twin_r, side_s, side_r, ring_s, ring_r, last_s, last_r = sems
    count = len(pieces)
    chips = place.chips
    reach = chips // 2
    right, left, across, twin = range(4)
    y = place.plane
    other = 1 - place.core
    sends = Sends()
    go = sends.go
    own = [bufs[5*i] for i in range(count)]; tw = [bufs[5*i+1] for i in range(count)]
    sd = [bufs[5*i+2] for i in range(count)]; rg = [bufs[5*i+3] for i in range(count)]; lt = [bufs[5*i+4] for i in range(count)]
    steps = [reach] + [x for s in range(reach - 1, 0, -1) for x in (s, -s)] + [0]
    slot_of = {s: k for k, s in enumerate(steps)}
    slot_of[-reach] = slot_of[reach]
    w = [o.shape[-1] // 9 for o in own]
    def ringcols(i, d, s):
        base = y * 2 * w[i]
        if s > 1: return base, 7 * w[i]
        k = 4 if (d + i) % 2 == 0 else 3
        return (base, 4 * w[i]) if k == 4 else (base + 4 * w[i], 3 * w[i])
    def taken(i, j):
        n, r, rows, col, width = pieces[i]
        return parts[n].at[j, pl.ds(r, rows), pl.ds(col, width)]
    def twin_copy(i, k):
        return remote(taken(i, place.member(steps[k], other)), tw[i].at[k], twin_s.at[i, k], twin_r.at[i, k], place.near()[twin])
    def load_copy(i, k):
        return pltpu.make_async_copy(taken(i, place.member(steps[k])), own[i].at[k], load.at[i, k])
    def side(i, k):
        return remote(own[i].at[k, :, lanes((1 - y) * 7 * w[i], 2 * w[i])], sd[i].at[k], side_s.at[i, k], side_r.at[i, k], place.near()[across])
    def ring(i, d, s):
        start, size = ringcols(i, d, s)
        k = slot_of[(reach + 1 - s) if d == 0 else -(reach + 1 - s)]
        return remote(own[i].at[k, :, lanes(start, size)], rg[i].at[d, s-1, :, lanes(start - y * 2 * w[i], size)],
                      ring_s.at[i, d, s-1], ring_r.at[i, d, s-1], place.near()[d])
    def last(i):
        sl = lanes(y * 2 * w[i], 7 * w[i])
        return remote(own[i].at[slot_of[0], :, sl], lt[i].at[:, sl], last_s.at[i], last_r.at[i], place.near()[across])
    def add(i, dst_k, start, src, src_start, pieces):
        to, size = lanes(start, pieces * w[i]), pieces * w[i]
        own[i][dst_k, :, to] += src[:, lanes(src_start, size)]
    for k in range(chips):
        for i in range(count):
            go(twin_copy, i, k); load_copy(i, k).start()
    yield
    def pair(k):
        for i in range(count):
            load_copy(i, k).wait(); twin_copy(i, k).wait_recv()
            add(i, k, 0, tw[i].at[k], 0, 9)
            go(side, i, k)
    def planes(k):
        for i in range(count):
            side(i, k).wait_recv()
            add(i, k, y * 7 * w[i], sd[i].at[k], 0, 2)
    def ring_in(i, d, s):
        ring(i, d, s).wait_recv()
        start, size = ringcols(i, d, s)
        t = reach - s
        add(i, slot_of[t if d == 0 else -t], start, rg[i].at[d, s-1], start - y * 2 * w[i], size // w[i])
    def need(s):
        far = reach + 1 - s
        return [slot_of[far]] if s == 1 or far == 0 else [slot_of[far], slot_of[-far]]
    done = 0
    for s in range(1, reach + 1):
        ready = need(s)
        while done < min(chips, max(ready) + 3):
            pair(done); done += 1
        for k in ready: planes(k)
        yield
        for i in range(count):
            for d in (0, 1):
                if s > 1: ring_in(i, d, s - 1)
                go(ring, i, d, s)
            yield
    while done < chips:
        pair(done); done += 1
    planes(slot_of[0])
    yield
    for i in range(count):
        for d in (0, 1): ring_in(i, d, reach)
        go(last, i)
        yield
    for i in range(count):
        last(i).wait_recv()
        k = slot_of[0]
        mine, theirs = y * 7 * w[i], (1 - y) * 7 * w[i]
        for t in range(2):
            a, b = t * w[i] + mine, t * w[i] + theirs
            outs[i][:, lanes(a, w[i])] = own[i][k, :, lanes(a, w[i])]
            outs[i][:, lanes(b, w[i])] = lt[i][:, lanes(b, w[i])]
        for t in range(2, 7):
            at = pl.ds(t * w[i], w[i])
            outs[i][:, at] = own[i][k, :, at] + lt[i][:, at]
        yield
    sends.close()


def peers(place):
    n = place.wide
    return [(t, lax.rem(place.index + t, n)) for t in range(1, n)]


class Exchange:
    def __init__(self, place, parts, inbox, every, sems):
        self.place, self.parts, self.inbox, self.every = place, parts, inbox, every
        self.sems = sems
        self.sends = Sends()

    @staticmethod
    def scratch(wide, block, dtype):
        return [pltpu.VMEM((wide,) + block, dtype)] + [DMA((wide,))] * 4

    def device(self, t):
        return lax.rem(self.place.index + t, self.place.wide)

    def out(self, t):
        j = self.device(t)
        return remote(self.parts.at[j], self.inbox.at[t], self.sems[0].at[t], self.sems[1].at[t], (self.place.plane, j))

    def back(self, t, own):
        block = self.place.index if own else self.device(self.place.wide - t)
        ref = self.every.at[block]
        return remote(ref, ref, self.sems[2].at[t], self.sems[3].at[t], (self.place.plane, self.device(t)))

    def send(self):
        for t in range(1, self.place.wide):
            self.sends.go(self.out, t)

    def total(self):
        value = self.parts[self.place.index].astype(f32)
        for t in range(1, self.place.wide):
            self.out(t).wait_recv()
            value += self.inbox[t].astype(f32)
        return value

    def spread(self, value):
        self.every[self.place.index] = value.astype(self.every.dtype)
        for t in range(1, self.place.wide):
            self.sends.go(self.back, t, True)

    def arrive(self):
        for t in range(1, self.place.wide):
            self.back(t, False).wait_recv()

    def close(self):
        self.sends.close()


class Ring:
    def __init__(self, place, parts, every, scratch):
        self.place, self.parts, self.every = place, parts, every
        self.twin, self.inbox, self.outbox = scratch[:3]
        self.sems = scratch[3:]
        self.sends = Sends()

    @staticmethod
    def scratch(wide, block):
        chips = wide // 2
        reach = chips // 2
        return [pltpu.VMEM((chips,) + block, bf16), pltpu.VMEM((2, reach) + block, bf16),
                pltpu.VMEM((2, reach) + block, bf16), DMA((2,)), DMA((2, reach)), DMA((2, reach)),
                DMA((2,)), DMA((2, reach)), DMA((2, reach))]

    def go(self, make, *args):
        self.sends.go(make, *args)

    def reaches(self):
        half = self.place.chips // 2
        return (half, half - 1)

    def value(self, step):
        chip = self.place.chip(step)
        return self.parts[chip, self.place.core].astype(f32) + self.twin[chip].astype(f32)

    def pair(self):
        twin = self.place.near()[3]
        return remote(self.parts.at[:, 1 - self.place.core], self.twin, self.sems[0].at[0], self.sems[0].at[1], twin)

    def hop(self, d, s):
        return remote(self.outbox.at[d, s - 1], self.inbox.at[d, s - 1], self.sems[1].at[d, s - 1],
                      self.sems[2].at[d, s - 1], self.place.near()[d])

    def sum_steps(self):
        self.go(self.pair)
        yield
        self.pair().wait_recv()
        reaches = self.reaches()
        for s in range(1, max(reaches) + 1):
            for d in (0, 1):
                if s > reaches[d]:
                    continue
                step = reaches[d] + 1 - s
                total = self.value(step if d == 0 else -step)
                if s > 1:
                    self.hop(d, s - 1).wait_recv()
                    total += self.inbox[d, s - 2].astype(f32)
                self.outbox[d, s - 1] = total.astype(bf16)
                self.go(self.hop, d, s)
            yield
        self.total = self.value(0)
        for d in (0, 1):
            self.hop(d, reaches[d]).wait_recv()
            self.total += self.inbox[d, reaches[d] - 1].astype(f32)

    def spread(self, d, s, step):
        ref = self.every.at[self.place.chip(step), self.place.core]
        return remote(ref, ref, self.sems[4].at[d, s - 1], self.sems[5].at[d, s - 1], self.place.near()[d])

    def halves(self, own):
        ref = self.every.at[:, self.place.core if own else 1 - self.place.core]
        return remote(ref, ref, self.sems[3].at[0], self.sems[3].at[1], self.place.near()[3])

    def spread_steps(self, value):
        reaches = self.reaches()
        core = self.place.core
        self.every[self.place.chip(0), core] = value.astype(bf16)
        for d in (0, 1):
            self.go(self.spread, d, 1, 0)
        yield
        for s in range(1, max(reaches) + 1):
            for d in (0, 1):
                if s > reaches[d]:
                    continue
                step = -s if d == 0 else s
                self.spread(d, s, step).wait_recv()
                if s < reaches[d]:
                    self.go(self.spread, d, s + 1, step)
            yield
        self.go(self.halves, True)
        yield
        self.halves(False).wait_recv()

    def close(self):
        self.sends.close()


def by_chip(value):
    return value.reshape((value.shape[0] // 2, 2) + value.shape[1:])


def front_steps(modulation, text, prompt):
    modulation.send()
    yield from text.sum_steps()
    prompt[...] = text.total.astype(bf16)
    modulation.spread(modulation.total())
    yield
    modulation.arrive()
    modulation.close()
    text.close()


def text_steps(keys, prompt, kv_cols):
    def block(j, _):
        for core in (0, 1):
            keys.parts[j, core] = dot(kv_cols[j, core], prompt[...]).astype(bf16)
        return 0

    lax.fori_loop(0, keys.place.chips, block, 0)
    yield from keys.sum_steps()
    yield from keys.spread_steps(keys.total)
    keys.close()


def text_back_steps(keys, prompts, kv_rows, sems):
    place = keys.place

    def over(ref, k, own):
        half = ref.at[place.plane if own else 1 - place.plane]
        return remote(half, half, sems.at[k, 0], sems.at[k, 1], place.near()[2])

    yield from keys.sum_steps()
    yield from keys.spread_steps(keys.total)
    over(keys.both, 0, True).start()
    every = keys.every[...]
    yield from prompts.spread_steps(dot(kv_rows[...], every.reshape(-1, every.shape[-1])))
    over(prompts.both, 1, True).start()
    yield
    for k, part in ((0, keys), (1, prompts)):
        over(part.both, k, False).wait_recv()
        over(part.both, k, True).wait_send()
        part.close()


def vector_steps(vectors, sems):
    place = vectors.place
    vectors.send()
    yield
    vectors.spread(vectors.total())
    yield
    vectors.arrive()

    def over(own):
        half = vectors.both.at[place.plane if own else 1 - place.plane]
        return remote(half, half, sems.at[0], sems.at[1], place.near()[2])

    over(True).start()
    yield
    over(False).wait_recv()
    over(True).wait_send()
    vectors.close()


MOST_CHIPS = 8


class Gather:
    direct = False

    def __init__(self, wide, arrays, turns=1):
        self.turns = turns
        self.inputs = [(a, ANY) for a in arrays]
        self.outputs = [(((wide,) + a.shape, a.dtype), ANY) for a in arrays]
        self.arrays = arrays
        self.pieces = pieces_of(arrays)
        self.scratch = gather_scratch(wide, len(self.pieces))

    def steps(self, place, ins, outs, scratch):
        return gather_steps(place, ins, outs, scratch, self.pieces)

    def plain(self, _outputs):
        return [lax.all_gather(a, "wide") for a in self.arrays]


class Scatter:
    direct = False
    turns = 1

    def __init__(self, wide, pieces, turns=1):
        self.turns = turns
        arrays = []
        for piece in pieces:
            if not any(piece[0] is a for a in arrays):
                arrays.append(piece[0])
        self.given = pieces
        self.pieces = [([piece[0] is a for a in arrays].index(True),) + piece[1:] for piece in pieces]
        self.inputs = [(a, ANY) for a in arrays]
        self.outputs = [(((p[2], p[4]), bf16), VM) for p in pieces]
        self.scratch = scatter_scratch(wide, [(p[2], p[4]) for p in pieces])

    def steps(self, place, ins, outs, scratch):
        buffers = 5 * len(self.pieces)
        return scatter_steps(place, ins, outs, scratch[:buffers], scratch[buffers:], self.pieces)

    def plain(self, _outputs):
        return [plain_scatter(*piece) for piece in self.given]


def plain_scatter(array, row, rows, col, cols):
    part = array[:, row : row + rows, col : col + cols].astype(f32)
    return lax.psum(lax.psum_scatter(part, "wide"), "narrow").astype(bf16)


def pieces_in(array):
    return [(array,) + p[1:] for p in pieces_of([array])]


class Front:
    turns = 1
    direct = True

    def __init__(self, wide, mod_parts, text_parts):
        self.inputs = [(mod_parts, VM), (by_chip(text_parts), VM)]
        self.outputs = [((mod_parts.shape, f32), VM), ((text_parts.shape[1:], bf16), VM)]
        self.scratch = Exchange.scratch(wide, mod_parts.shape[1:], f32) + Ring.scratch(wide, text_parts.shape[1:])

    def steps(self, place, ins, outs, scratch):
        modulation = Exchange(place, ins[0], scratch[0], outs[0], scratch[1:5])
        return front_steps(modulation, Ring(place, ins[1], None, scratch[5:]), outs[1])

    def plain(self, _outputs):
        mod_parts, text_parts = (value for value, _ in self.inputs)
        rows = text_parts.reshape((-1,) + text_parts.shape[2:]).astype(f32)
        return [lax.psum(mod_parts, "wide"), lax.psum_scatter(rows, "wide").astype(bf16)]


class Text:
    turns = 1
    direct = False

    def __init__(self, wide, prompt, kv_cols):
        block = (kv_cols.shape[1], prompt.shape[1])
        self.inputs = [(prompt, VM), (by_chip(kv_cols), VM)]
        self.outputs = [(((wide // 2, 2) + block, bf16), VM)]
        self.scratch = [pltpu.VMEM((wide // 2, 2) + block, bf16)] + Ring.scratch(wide, block)

    def steps(self, place, ins, outs, scratch):
        return text_steps(Ring(place, scratch[0], outs[0], scratch[1:]), ins[0], ins[1])

    def plain(self, _outputs):
        prompt, kv_cols = (value for value, _ in self.inputs)
        product = lax.dot_general(kv_cols, prompt, (((3,), (0,)), ((), ())), preferred_element_type=f32)
        return [lax.psum(product, "wide").astype(bf16)]


class TextBack:
    turns = 1
    direct = False

    def __init__(self, wide, kv_parts, kv_rows):
        chips = (wide // 2, 2)
        kv_block, block = kv_parts.shape[1:], (kv_rows.shape[0], kv_parts.shape[2])
        self.inputs = [(by_chip(kv_parts), VM), (kv_rows, VM)]
        self.outputs = [(((2,) + chips + kv_block, bf16), VM), (((2,) + chips + block, bf16), VM)]
        self.scratch = Ring.scratch(wide, kv_block) + Ring.scratch(wide, block) + [DMA((2, 2))]

    def steps(self, place, ins, outs, scratch):
        keys = Ring(place, ins[0], outs[0].at[place.plane], scratch[:9])
        keys.both = outs[0]
        prompts = Ring(place, None, outs[1].at[place.plane], scratch[9:18])
        prompts.both = outs[1]
        return text_back_steps(keys, prompts, ins[1], scratch[18])

    def plain(self, _outputs):
        kv_parts, kv_rows = (value for value, _ in self.inputs)
        every = lax.psum(kv_parts.astype(f32), "wide").astype(bf16)
        rows = dot(kv_rows, every.reshape(-1, every.shape[-1])).astype(bf16)
        return [lax.all_gather(every, "narrow"), lax.all_gather(by_chip(lax.all_gather(rows, "wide")), "narrow")]


class Vectors:
    turns = 1
    direct = True

    def __init__(self, wide, parts):
        self.inputs = [(parts, VM)]
        self.outputs = [(((2,) + parts.shape, f32), VM)]
        self.scratch = Exchange.scratch(wide, parts.shape[1:], f32) + [DMA((2,))]

    def steps(self, place, ins, outs, scratch):
        vectors = Exchange(place, ins[0], scratch[0], outs[0].at[place.plane], scratch[1:5])
        vectors.both = outs[0]
        return vector_steps(vectors, scratch[5])

    def plain(self, _outputs):
        return [lax.all_gather(lax.psum(self.inputs[0][0], "wide"), "narrow")]


class Pump:
    def __init__(self, pace=1, every=1):
        self.running, self.pace, self.every = [], pace, every
        self.calls = 0

    def due(self):
        self.calls += 1
        return self.calls % self.every == 0

    def __call__(self):
        if self.due():
            self.move()

    def move(self):
        for _ in range(self.pace):
            for steps, turns in list(self.running):
                for _ in range(turns):
                    if next(steps, self) is self:
                        self.running.remove((steps, turns))
                        break

    def inside(self, index, low, high):
        for n in range(low, high):
            if self.due() and self.running:
                pl.when(index == n)(lambda: self.move())

    def along(self, index, count, calls):
        if count < 2 * calls:
            return
        for n in range(calls):
            if self.due() and self.running:
                pl.when(index == (n + 1) * count // (calls + 1))(lambda: self.move())

    def finish(self):
        while self.running:
            self.move()


def take(refs, *counts):
    found, at = [], 0
    for count in counts:
        found.append(refs[at : at + count])
        at += count
    return found


def fused_kernel(wide, talks, compute, counts, parts, pace, burst, every, *refs):
    sizes = list(counts) + [n for p in parts for n in (len(p.inputs), len(p.outputs), len(p.scratch))]
    order = [0] + [3 + 3 * i for i in range(len(parts))]
    order += [1] + [4 + 3 * i for i in range(len(parts))]
    order += [2] + [5 + 3 * i for i in range(len(parts))]
    found = dict(zip(order, take(refs, *[sizes[i] for i in order])))
    pump = Pump(pace, every)
    if talks:
        place = Place(wide)
        greet(all_near(place) if any(p.direct for p in parts) else place.near() + place.beside())
        for i, p in enumerate(parts):
            steps = p.steps(place, found[3 + 3 * i], found[4 + 3 * i], found[5 + 3 * i])
            pump.running.append((steps, p.turns))
        for _ in range(burst):
            pump.move()
    if compute is not None:
        compute(pump, *found[0], *found[1], *found[2])
    pump.finish()


def fused(name, wide, compute, inputs, outputs, scratch, parts=(), pace=1, collective_id=None, burst=1, every=1):
    if wide > 2 * MOST_CHIPS and parts:
        done = [[]] if compute is None else fused(
            name, wide, compute, inputs, outputs, scratch, collective_id=collective_id)
        return done + [part.plain(done[0]) for part in parts]
    ins = inputs + [x for p in parts for x in p.inputs]
    outs = outputs + [x for p in parts for x in p.outputs]
    talks = collective_id is not None
    options = dict(collective_id=collective_id, has_side_effects=True) if talks else {}
    found = pl.pallas_call(
        functools.partial(fused_kernel, wide, talks, compute, (len(inputs), len(outputs), len(scratch)), parts, pace, burst, every),
        out_shape=[jax.ShapeDtypeStruct(shape, dtype) for (shape, dtype), _ in outs],
        in_specs=[spec for _, spec in ins],
        out_specs=[spec for _, spec in outs],
        scratch_shapes=scratch + [x for p in parts for x in p.scratch],
        compiler_params=pltpu.CompilerParams(vmem_limit_bytes=LIMIT, **options),
        name=name,
    )(*[value for value, _ in ins])
    return take(found, len(outputs), *[len(p.outputs) for p in parts])


def on_chip(*values):
    return [(value, VM) for value in values]


def all_near(place):
    return [place.near()[2]] + [(place.plane, j) for t, j in peers(place)]


def spatial(wide, frames, patches, x, mod, heads, w_qkv, w_out, **rest):
    rows, width = x.shape
    return fused(
        "spatial", wide, functools.partial(spatial_kernel, frames, patches),
        on_chip(x, mod, heads) + [(w_qkv, ANY)] + on_chip(w_out),
        on_chip(*[((rows, n * width), d) for n, d in ((1, bf16), (3, bf16), (1, bf16), (1, bf16), (1, f32))]),
        [pltpu.VMEM(w_qkv.shape, bf16), DMA((3,))], **rest,
    )


def spatial_back(wide, frames, patches, gradient, x, mod, heads, w_qkv, w_out, normed, qkv, attn, branch, **rest):
    rows, width = x.shape
    V = pltpu.VMEM
    return fused(
        "spatial_back", wide, functools.partial(spatial_back_kernel, frames, patches),
        on_chip(gradient, x, mod, heads) + [(w_qkv, ANY)] + on_chip(w_out, normed, qkv, attn, branch),
        on_chip(((rows, width), bf16), ((width, 3 * width), bf16), ((width, width), bf16), ((3, width), f32)),
        [V((rows, width), bf16), V((rows, width), bf16), V((rows, 3 * width), bf16),
         V((rows, width), f32), V((2, width, width), bf16), DMA((2,))], **rest,
    )


def cross(wide, frames, patches, first, gain, mod, heads, valid, text_kv, w_q, w_out, w_tqkv, **rest):
    rows, width = first.shape
    return fused(
        "cross", wide, functools.partial(cross_kernel, wide, frames, patches),
        on_chip(first, gain, mod, heads, valid, text_kv, w_q, w_out) + [(w_tqkv, ANY)],
        on_chip(*[((rows, n * width), d) for n, d in ((1, bf16), (1, bf16), (1, bf16), (1, f32), (1, bf16), (3, bf16))])
        + on_chip(((frames + 4, patches, 2 * width), bf16)),
        [pltpu.VMEM((4 * patches, width), bf16), DMA((2, 2)), pltpu.VMEM(w_tqkv.shape, bf16), DMA((3,))], **rest,
    )


def cross_back(wide, frames, patches, gradient, first, gain, heads, valid, text_kv, w_q, w_out, normed, query, attn, **rest):
    rows, width = first.shape
    V = pltpu.VMEM
    return fused(
        "cross_back", wide, functools.partial(cross_back_kernel, frames, patches),
        on_chip(gradient, first, gain, heads, valid, text_kv, w_q, w_out, normed, query, attn),
        on_chip(((rows, width), f32), ((width, width), bf16), ((width, width), bf16), ((1, width), f32), (text_kv.shape, f32)),
        [V((rows, width), bf16)] * 3 + [V((rows, width), f32)], **rest,
    )


def temporal(wide, frames, patches, qkv, near, allowed, spread, heads, second, mod, w_out, **rest):
    rows, width = second.shape
    return fused(
        "temporal", wide, functools.partial(temporal_kernel, frames, patches),
        on_chip(qkv, near, allowed, spread, heads, second, mod, w_out),
        on_chip(((rows, width), bf16), ((rows, width), bf16), ((rows, width), f32)), [], **rest,
    )


def temporal_back(wide, frames, patches, gradient, qkv, near, allowed, spread, heads, mod, w_out, attn, branch, **rest):
    rows, width = gradient.shape
    V = pltpu.VMEM
    edges = (4 * patches, 2 * width)
    return fused(
        "temporal_back", wide, functools.partial(temporal_back_kernel, wide, frames, patches),
        on_chip(gradient, qkv, near, allowed, spread, heads, mod, w_out, attn, branch),
        on_chip(((width, width), bf16), ((rows, 3 * width), bf16), ((1, width), f32)),
        [V((rows, width), bf16)] * 2 + [V(edges, bf16)] * 2 + [DMA((2, 2, 2, patches // SLAB))], **rest,
    )


def temporal_rows(wide, gradient, second, mod, d_qkv, normed, w_qkv, **rest):
    rows, width = gradient.shape
    return fused(
        "temporal_rows", wide, temporal_rows_kernel,
        on_chip(gradient, second, mod, d_qkv, normed) + [(w_qkv, ANY)],
        on_chip(((rows, width), f32), ((width, 3 * width), bf16), ((2, width), f32)),
        [pltpu.VMEM((rows, width), f32), pltpu.VMEM((2, width, width), bf16), DMA((2,))], **rest,
    )


def mlp(wide, third, cotangent, mod, w_up, w_down, **rest):
    rows, width = third.shape
    V = pltpu.VMEM
    return fused(
        "mlp", wide, mlp_kernel,
        on_chip(third, cotangent, mod) + [(w_up, ANY), (w_down, ANY)],
        on_chip(((rows, width), bf16), ((rows, width), f32)) + [((w_up.shape, bf16), ANY), ((w_down.shape, bf16), ANY)]
        + on_chip(((3, width), f32)),
        [V((rows, width), bf16)] * 2 + [V((rows, width), f32)] * 2 + [V((rows, width), bf16)] * 2
        + [V((rows, width), f32)] + [V((2, width, width), bf16)] * 2 + [V((width, width), bf16)] * 2
        + [DMA((2, 2)), DMA((2,))], **rest,
    )


def time_embed(steps, model_width):
    half_width = model_width // 2
    freqs = jnp.exp(-math.log(10000.0) * jnp.arange(half_width, dtype=jnp.float32) / half_width)
    angles = steps.astype(jnp.float32)[:, None] * freqs[None, :]
    return jnp.concatenate([jnp.cos(angles), jnp.sin(angles)], -1)


def body(
    hidden,
    cotangent,
    text,
    timesteps,
    seg_ids,
    text_len,
    ada_weight,
    text_weight,
    kv_weight,
    qkv_weight,
    out_weight,
    cross_q_weight,
    cross_out_weight,
    temp_qkv_weight,
    temp_out_weight,
    up_weight,
    down_weight,
    cross_gain,
):
    frames, patches, width = hidden.shape[1:]
    rows = frames * patches
    text_count = text.shape[1]
    plane = lax.axis_index("narrow")
    position = lax.axis_index("wide")
    wide = lax.axis_size("wide")
    rows_model, rows_text = ada_weight.shape[0], text_weight.shape[0]
    head_of = jnp.arange(width) // (width // HEADS)
    heads = (head_of[None, :] == jnp.arange(HEADS)[:, None]).astype(bf16)
    spread = (head_of[:, None] == jnp.arange(HEADS)[None, :]).astype(bf16)

    def swap(value):
        return lax.ppermute(value, "narrow", [(0, 1), (1, 0)])

    def by_plane(own, other):
        return jnp.where(plane == 0, jnp.stack([own, other]), jnp.stack([other, own]))

    def whole(value):
        return value.reshape(-1, value.shape[-1])

    def joined(parts, axis):
        return jnp.concatenate([part.astype(f32) for part in parts], axis)

    def blocks(value):
        return value.reshape(wide, -1, value.shape[-1])

    signal = jax.nn.silu(time_embed(timesteps, width)[0]).astype(bf16)
    signal_rows = lax.dynamic_slice_in_dim(signal, position * rows_model, rows_model)
    mod_part = dot(signal_rows[None, :], ada_weight)
    prompt_rows = lax.dynamic_slice_in_dim(text[0], position * rows_text, rows_text, 1)
    text_part = dot(text_weight, prompt_rows, (((0,), (1,)), ((), ())))
    kv_cols = blocks(kv_weight.T)
    front = Front(wide, mod_part.reshape(wide, 1, -1), blocks(text_part.astype(bf16)))
    _none, (modulation, prompt), (full_qkv, full_out) = fused(
        "start", wide, None, [], [], [], parts=[front, Gather(wide, [qkv_weight, out_weight], turns=3)], collective_id=0
    )
    full_qkv, full_out = whole(full_qkv), whole(full_out)
    mod = modulation.reshape(9, width)

    tokens = hidden[0].reshape(rows, width)
    (normed_a, qkv_a, attn_a, branch_a, first), (kv_all,), gathered = spatial(
        wide, frames, patches, tokens, mod, heads, full_qkv, full_out, collective_id=1,
        parts=[
            Text(wide, prompt, kv_cols),
            Gather(wide, [cross_q_weight, cross_out_weight, temp_qkv_weight, temp_out_weight], turns=3),
        ],
    )
    full_cross_q, full_cross_out, full_temp_qkv, full_temp_out = map(whole, gathered)
    text_kv = whole(kv_all).T
    valid = (jnp.arange(text_count) < text_len[0]).astype(f32)[:, None]
    gain = cross_gain[None, :]
    (normed_c, query_c, attn_c, second, normed_t, qkv_t, near), (full_down,) = cross(
        wide, frames, patches, first, gain, mod, heads, valid, text_kv, full_cross_q, full_cross_out, full_temp_qkv,
        parts=[Gather(wide, [down_weight])], collective_id=2, every=2,
    )
    clip_pad = jnp.pad(seg_ids[0], 2, constant_values=-1)
    clip_local = lax.dynamic_slice_in_dim(clip_pad, position * frames, frames + 4)
    allowed = jnp.stack(
        [clip_local[offset : offset + frames] == clip_local[2 : frames + 2] for offset in range(5)]
    )
    allowed = jnp.broadcast_to(allowed[:, :, None, None], (5, frames, SLAB, HEADS)).reshape(-1, HEADS).astype(f32)
    (attn_t, branch_t, third), (full_up,) = temporal(
        wide, frames, patches, qkv_t, near, allowed, spread, heads, second, mod, full_temp_out,
        parts=[Gather(wide, [up_weight])], collective_id=3,
    )

    upstream = cotangent[0].reshape(rows, width)
    ((block_out, gradient, grad_up, grad_down, d_mod_m),) = mlp(
        wide, third, upstream, mod, whole(full_up), whole(full_down)
    )
    grad_up = grad_up.reshape(wide, rows_model, -1)

    (grad_temp_out, d_qkv_t, d_gate_t), up_parts = temporal_back(
        wide, frames, patches, gradient, qkv_t, near, allowed, spread, heads, mod, full_temp_out, attn_t, branch_t,
        parts=[Scatter(wide, pieces_in(grad_up))], collective_id=4, burst=4,
    )
    (gradient, grad_temp_qkv, d_mod_t), down_parts = temporal_rows(
        wide, gradient, second, mod, d_qkv_t, normed_t, full_temp_qkv,
        parts=[Scatter(wide, pieces_in(blocks(grad_down)))], collective_id=5, pace=2, burst=4,
    )
    (gradient, grad_cross_q, grad_cross_out, d_gain, d_text_kv), (*temp_qkv_parts, grad_temp_out) = cross_back(
        wide, frames, patches, gradient, first, gain, heads, valid, text_kv,
        full_cross_q, full_cross_out, normed_c, query_c, attn_c,
        parts=[Scatter(wide, pieces_in(blocks(grad_temp_qkv)) + pieces_in(blocks(grad_temp_out)))], collective_id=6, burst=4,
    )
    found = spatial_back(
        wide, frames, patches, gradient, tokens, mod, heads, full_qkv, full_out, normed_a, qkv_a, attn_a, branch_a,
        parts=[
            TextBack(wide, blocks(d_text_kv.T.astype(bf16)), kv_weight),
            Scatter(wide, [p for g in (grad_cross_q, grad_cross_out) for p in pieces_in(blocks(g))]),
        ],
        collective_id=7,
    )
    (grad_hidden, grad_qkv, grad_out, d_mod_a), (d_kv_both, d_prompt_both), (grad_cross_q, grad_cross_out) = found
    vectors = jnp.concatenate([d_mod_a, d_mod_t, d_gate_t, d_mod_m, d_gain], 0)
    _none, (vec_both,), (*qkv_parts, grad_out) = fused(
        "end", wide, None, [], [], [], collective_id=8,
        parts=[
            Vectors(wide, vectors.reshape(wide, 1, -1)),
            Scatter(wide, pieces_in(blocks(grad_qkv)) + pieces_in(blocks(grad_out)), turns=2),
        ],
    )
    vec_both = vec_both.reshape(2, 10, width)

    d_modulation = vec_both[:, :9].reshape(2, 9 * width)
    grad_gain = vec_both[0, 9] + vec_both[1, 9]
    both_signal = by_plane(signal_rows, swap(signal_rows)).astype(f32)
    grad_ada = (
        both_signal[0][:, None] * d_modulation[0][None, :] + both_signal[1][:, None] * d_modulation[1][None, :]
    )
    both_prompt = by_plane(prompt, swap(prompt))
    both_rows = by_plane(prompt_rows, swap(prompt_rows)).reshape(2 * text_count, -1)
    pairs = (((0, 2), (0, 2)), ((), ()))
    grad_kv = lax.dot_general(
        both_prompt, d_kv_both.reshape(2, 2 * width, text_count), pairs, preferred_element_type=f32
    )
    d_prompt = d_prompt_both.reshape(2, width, text_count).transpose(0, 2, 1).reshape(2 * text_count, width)
    grad_text = dot(both_rows, d_prompt, TN)
    shape = (1, frames, patches, width)
    return (
        block_out.reshape(shape),
        grad_hidden.reshape(shape),
        grad_ada,
        grad_text,
        grad_kv,
        joined(qkv_parts, 1),
        grad_out.astype(f32),
        grad_cross_q.astype(f32),
        grad_cross_out.astype(f32),
        joined(temp_qkv_parts, 1),
        grad_temp_out.astype(f32),
        joined(up_parts, 1),
        joined(down_parts, 0),
        grad_gain,
    )


def solution(mesh):
    return jax.shard_map(
        body,
        mesh=mesh,
        in_specs=(
            P("narrow", "wide", None, None),
            P("narrow", "wide", None, None),
            P("narrow", None, None),
            P("narrow"),
            P("narrow", None),
            P("narrow"),
            P("wide", None),
            P("wide", None),
            P("wide", None),
            P("wide", None),
            P("wide", None),
            P("wide", None),
            P("wide", None),
            P("wide", None),
            P("wide", None),
            P("wide", None),
            P("wide", None),
            P(),
        ),
        out_specs=(
            P("narrow", "wide", None, None),
            P("narrow", "wide", None, None),
            P("wide", None),
            P("wide", None),
            P("wide", None),
            P("wide", None),
            P("wide", None),
            P("wide", None),
            P("wide", None),
            P("wide", None),
            P("wide", None),
            P("wide", None),
            P("wide", None),
            P(),
        ),
        check_vma=False,
    )
```
